128 devices in a mesh: row: 16 (over z, y), col: 8 (over x, core).
Axes of the slice: x: 4, y: 4, z: 4, core: 2. Of those that a mesh axis runs over, the one named last changes fastest.
Arguments:
- readouts: bfloat16 [128, 128, 256], P('row', 'col'), may hold values from -6 to 6
- w_embed: bfloat16 [8, 64], replicated, may hold values from -2 to 2
- w_up: bfloat16 [3, 9, 64, 64], replicated, may hold values from -0.25 to 0.25
- merge_in: bfloat16 [256, 256], replicated, may hold values from -0.375 to 0.375
- merge_out: bfloat16 [256, 64], replicated, may hold values from -0.5 to 0.5
- down_in: bfloat16 [128, 256], replicated, may hold values from -0.5 to 0.5
- down_out: bfloat16 [256, 64], replicated, may hold values from -0.375 to 0.375
- w_down: bfloat16 [3, 9, 64, 64], replicated, may hold values from -0.25 to 0.25
- w_head: bfloat16 [64, 4], replicated, may hold values from -0.75 to 0.75
- qubit_slot: int32 [128, 8, 64], P('row', 'col'), may hold values from 0 to 63, each once within a row
Outputs:
- logits: float32 [32, 128, 512], P(None, 'row', 'col')
The draws below stay inside these ranges and needn't reach their ends.
Inputs may be any that keep to these rules, and one draw needn't show every extreme that they name: For each lattice row and each column tile, qubit_slot lists every number of 0 to 63 exactly once.
All inputs are finite; a program needn't handle non-finite values.
Results may differ from the reference program's by a relative error of at most 0.04.
Values may be sent and summed in bfloat16 or wider, within the bound.
No kernel may reach another device: no remote copies, remote signals or barrier semaphores. Data moves between devices by JAX's collectives and lax.ppermute only.
A program may use at most 128 MiB of HBM per device.

```python
import jax
import jax.numpy as jnp
from jax import lax

C = 64
H = 256
F = 4
NUP = 3
NDOWN = 3
S = 32
TC = 16
L = 128
LLEV = 3
DLEV = 4
N_COL = 8


def steps_of(stream_key, dims, split, least, top_value):
    loudness = 1.0
    for dim, shards_of in split:
        steps = jax.random.uniform(jax.random.fold_in(jax.random.fold_in(stream_key, 6), dim), (shards_of,), jnp.float32, least / len(split), top_value / len(split))
        loudness = loudness * jnp.repeat(jnp.exp(steps), dims[dim] // shards_of).reshape((-1,) + (1,) * (len(dims) - 1 - dim))
    return loudness


def centred(rng, extent, width, most, shards=(), kind=jnp.bfloat16):
    values = jax.random.normal(rng, extent, jnp.float32) * width
    if len(shards) > 0:
        values = steps_of(rng, extent, shards, -0.22, 0.18) * values
    return jnp.clip(values, min=-most, max=most).astype(kind)


def setup_inputs(seed: int = 0) -> dict:
    keys = jax.random.split(jax.random.key(seed), 11)
    return {
        "readouts": centred(keys[0], (L, L, S * 2 * F), 1.0, 6.0, ((0, 16), (1, 8))),
        "w_embed": centred(keys[1], (2 * F, C), (2 * F) ** -0.5, 2.0),
        "w_up": centred(keys[2], (NUP, 9, C, C), (9 * C) ** -0.5, 0.25),
        "merge_in": centred(keys[3], (4 * C, H), (4 * C) ** -0.5, 0.375),
        "merge_out": centred(keys[4], (H, C), (H // 2) ** -0.5, 0.5),
        "down_in": centred(keys[5], (2 * C, H), (2 * C) ** -0.5, 0.5),
        "down_out": centred(keys[6], (H, C), H ** -0.5, 0.375),
        "w_down": centred(keys[7], (NDOWN, 9, C, C), (9 * C) ** -0.5, 0.25),
        "w_head": centred(keys[8], (C, 4), C ** -0.5, 0.75),
        "qubit_slot": jax.vmap(lambda own: jax.random.permutation(own, 4 * TC))(jax.random.split(keys[9], L * N_COL)).reshape((L, N_COL, 4 * TC)).astype(jnp.int32),
    }


def conv_periodic(fields, weights):
    channels = fields.shape[-1]
    summed = jnp.zeros((fields.shape[0], fields.shape[1], weights.shape[-1]), jnp.float32)
    for tap_row in range(3):
        for tap_col in range(3):
            shifted = jnp.roll(fields, (1 - tap_row, 1 - tap_col), (0, 1))
            product_term = jnp.dot(shifted.reshape(-1, channels), weights[3 * tap_row + tap_col], preferred_element_type=jnp.float32)
            summed = summed + product_term.reshape(summed.shape)
    return summed

def residual_stack(fields, weights):
    for layer_index in range(weights.shape[0]):
        update = conv_periodic(fields, weights[layer_index])
        fields = (fields.astype(jnp.float32) + jax.nn.relu(update)).astype(jnp.bfloat16)
    return fields

def merge_level(fields, merge_in, merge_out):
    channels = fields.shape[-1]
    half_rows = fields.shape[0] // 2
    half_cols = fields.shape[1] // 2
    quarters = fields.reshape(half_rows, 2, half_cols, 2, channels)
    stacked = jnp.concatenate([quarters[:, 0, :, 0], quarters[:, 0, :, 1], quarters[:, 1, :, 0], quarters[:, 1, :, 1]], axis=-1)
    stacked = stacked.reshape(-1, 4 * channels)
    hidden = jax.nn.relu(jnp.dot(stacked, merge_in, preferred_element_type=jnp.float32)).astype(jnp.bfloat16)
    merged = jnp.dot(hidden, merge_out, preferred_element_type=jnp.float32).astype(jnp.bfloat16)
    return merged.reshape(half_rows, half_cols, channels)

def refine_level(parent, child_cells, down_in, down_out):
    channels = child_cells.shape[-1]
    widened = jnp.repeat(jnp.repeat(parent, 2, axis=0), 2, axis=1)
    joined = jnp.concatenate([widened, child_cells], axis=-1).reshape(-1, 2 * channels)
    inner_act = jax.nn.relu(jnp.dot(joined, down_in, preferred_element_type=jnp.float32)).astype(jnp.bfloat16)
    outcome = jnp.dot(inner_act, down_out, preferred_element_type=jnp.float32).reshape(child_cells.shape)
    return child_cells.astype(jnp.float32) + widened.astype(jnp.float32) + outcome

def decode_sample(cells_in, w_embed, w_up, merge_in, merge_out, down_in, down_out, w_down, w_head, qubit_slot):
    channels = w_embed.shape[1]
    embedded = jnp.dot(cells_in.reshape(-1, cells_in.shape[-1]), w_embed, preferred_element_type=jnp.float32)
    embedded = embedded.astype(jnp.bfloat16).reshape(L, L, channels)
    features = residual_stack(embedded, w_up)
    levels = [features]
    for level_index in range(LLEV + DLEV):
        levels.append(merge_level(levels[-1], merge_in, merge_out))
    context = levels[-1]
    for level_index in reversed(range(LLEV + DLEV)):
        wide_context = refine_level(context, levels[level_index], down_in, down_out)
        context = wide_context.astype(jnp.bfloat16) if level_index > 0 else wide_context
    scale_inv = 1.0 / jnp.sqrt(lax.optimization_barrier(jnp.mean(context * context, axis=-1, keepdims=True)) + 1e-05)
    normed = (context * scale_inv).astype(jnp.bfloat16)
    refined = residual_stack(normed, w_down)
    cell_logits = jnp.dot(refined.reshape(-1, channels), w_head, preferred_element_type=jnp.float32)
    cell_logits = cell_logits.reshape(L, N_COL, 4 * TC)
    return jnp.take_along_axis(cell_logits, qubit_slot, axis=2).reshape(L, 4 * L)

def reference(readouts, w_embed, w_up, merge_in, merge_out, down_in, down_out, w_down, w_head, qubit_slot):
    per_sample = readouts.reshape(L, L, S, 2 * F).transpose(2, 0, 1, 3)

    def one_sample(cells_in):
        return decode_sample(cells_in, w_embed, w_up, merge_in, merge_out, down_in, down_out, w_down, w_head, qubit_slot)
    return lax.map(one_sample, per_sample)
```

```python
import functools

import jax
import jax.numpy as jnp
from jax import lax
from jax.experimental import pallas as pl
from jax.experimental.pallas import tpu as pltpu
from jax.sharding import PartitionSpec as P

norm_eps = 1e-05
bf16 = jnp.bfloat16
f32 = jnp.float32
n_row = 16
n_col = 8
samples = 32
vmem_bytes = 48 * 1024 * 1024


def dot(left, right):
    return jnp.dot(left, right, preferred_element_type=f32)


def low_half(shape):
    return lax.broadcasted_iota(jnp.int32, shape, len(shape) - 1) < 64


def whole_call(body, out_shapes, scratch, args, smem=()):
    specs = [
        pl.BlockSpec(memory_space=pltpu.SMEM) if i in smem else pl.BlockSpec(memory_space=pltpu.VMEM)
        for i in range(len(args))
    ]
    return pl.pallas_call(
        body,
        out_shape=out_shapes,
        in_specs=specs,
        out_specs=jax.tree.map(lambda _: pl.BlockSpec(memory_space=pltpu.VMEM), out_shapes),
        scratch_shapes=scratch,
        compiler_params=pltpu.CompilerParams(vmem_limit_bytes=vmem_bytes),
    )(*args)


def arr(shape, dtype=bf16):
    return jax.ShapeDtypeStruct(shape, dtype)


def fill_quad_weights(src, out, layer, from_odd):
    zero = jnp.zeros((64, 64), bf16)

    def tap_of(step, parity_in, parity_out):
        place_in = 1 - parity_in if from_odd else parity_in
        place_out = parity_out if from_odd else 1 - parity_out
        tap = 2 * step + place_in - place_out
        return tap if 0 <= tap <= 2 else None

    for di in range(2):
        for dj in range(2):
            for a in range(2):
                for b in range(2):
                    base = ((di * 2 + dj) * 4 + a * 2 + b) * 64
                    for oa in range(2):
                        tap_row = tap_of(di, a, oa)
                        blocks = []
                        for ob in range(2):
                            tap_col = tap_of(dj, b, ob)
                            if tap_row is None or tap_col is None:
                                blocks.append(zero)
                            else:
                                blocks.append(src[layer, 3 * tap_row + tap_col])
                        out[layer, base : base + 64, oa * 128 : oa * 128 + 128] = jnp.concatenate(
                            blocks, axis=1
                        )


def prep_up_body(w_up, w_embed, merge_out, wq, we, mo):
    for layer in range(3):
        fill_quad_weights(w_up, wq, layer, layer % 2 == 0)
    tiled = jnp.concatenate([w_embed[...].astype(f32)] * 16, axis=0)
    none = jnp.zeros((128, 64), f32)
    for a in range(2):
        for b in range(2):
            q = 2 * a + b
            pair = [tiled, none] if b == 0 else [none, tiled]
            we[q * 128 : q * 128 + 128, a * 128 : a * 128 + 128] = jnp.concatenate(
                pair, axis=1
            ).astype(bf16)
            we[q * 128 : q * 128 + 128, (1 - a) * 128 : (1 - a) * 128 + 128] = jnp.zeros(
                (128, 128), bf16
            )
    mo[...] = jnp.concatenate([merge_out[...], merge_out[...]], axis=1)


def prep_down_body(w_down, down_in, down_out, head_tiled, wq, di0, do0, do, wh):
    for layer in range(3):
        fill_quad_weights(w_down, wq, layer, layer % 2 == 1)
    zero = jnp.zeros((64, 256), bf16)
    parent = down_in[0:64, :]
    child = down_in[64:128, :]
    di0[0:64, 0:256] = child
    di0[0:64, 256:512] = zero
    di0[64:128, 0:256] = zero
    di0[64:128, 256:512] = child
    di0[128:192, 0:256] = parent
    di0[128:192, 256:512] = parent
    di0[192:256, 0:256] = zero
    di0[192:256, 256:512] = zero
    back = down_out[...]
    none = jnp.zeros((256, 64), bf16)
    do0[0:256, :] = jnp.concatenate([back, none], axis=1)
    do0[256:512, :] = jnp.concatenate([none, back], axis=1)
    do[...] = jnp.concatenate([back, back], axis=1)
    lane = lax.broadcasted_iota(jnp.int32, (64, 128), 1)
    head = head_tiled[...].astype(f32)
    for quad in range(9):
        for a in range(2):
            for b in range(2):
                base = quad * 256 + (a * 2 + b) * 64
                column = 2 * quad - b
                if 0 <= column < 16:
                    first = a * 64 + 4 * column
                    kept = jnp.where((lane >= first) & (lane < first + 4), head, 0.0)
                else:
                    kept = jnp.zeros((64, 128), f32)
                wh[base : base + 64, :] = kept.astype(bf16)


def conv_layer(src, dst, weights, rows, cols, to_odd):
    low = low_half((cols, samples, 128))

    def step(i, carry):
        here = src[i, 0:cols]
        right = src[i, 1 : cols + 1]
        below = src[i + 1, 0:cols]
        corner = src[i + 1, 1 : cols + 1]
        stacked = jnp.concatenate([here, right, below, corner], axis=-1)
        update = dot(stacked.reshape(cols * samples, 1024), weights[...])
        update = jnp.maximum(update, 0.0).reshape(cols, samples, 256)
        if to_odd:
            old0 = jnp.where(low, corner[..., 0:128], below[..., 0:128])
            old1 = jnp.where(low, right[..., 128:256], here[..., 128:256])
        else:
            old0 = jnp.where(low, here[..., 0:128], right[..., 0:128])
            old1 = jnp.where(low, below[..., 128:256], corner[..., 128:256])
        dst[i, :, :, 0:128] = (old0.astype(f32) + update[..., 0:128]).astype(bf16)
        dst[i, :, :, 128:256] = (old1.astype(f32) + update[..., 128:256]).astype(bf16)
        return carry

    lax.fori_loop(0, rows, step, 0)


def spread_tiles(place, own, row_a, row_b, col_a, col_b, ext):
    row_even = place[0] % 2 == 0
    col_even = place[1] % 2 == 0
    after_row = jnp.where(row_even, 16, 0)
    before_row = jnp.where(row_even, 0, 16)
    after_col = jnp.where(col_even, 3, 0)
    before_col = jnp.where(col_even, 0, 3)
    for tile, ref, start in ((0, own, 8), (1, row_a, after_row), (2, row_b, before_row)):
        cells = ref[...].astype(f32)
        ext[pl.ds(start, 8), 1] = cells[:, 0:8]
        ext[pl.ds(start, 8), 2] = cells[:, 8:16]
        ext[pl.ds(start, 8), after_col] = col_a[tile].astype(f32)
        ext[pl.ds(start, 8), before_col] = col_b[tile].astype(f32)


def embed_quads(ext, we, lhs, dst, halo):
    rows = 4 + halo
    cols = 8 + halo
    first = 8 - halo
    sub = lax.broadcasted_iota(jnp.int32, (16, 128), 0)
    lane = lax.broadcasted_iota(jnp.int32, (16, 128), 1)
    own_lanes = (lane // 8 == sub).astype(f32)

    def step(i, carry):
        for quad in range(cols):
            for a in range(2):
                row = first + 2 * i + (1 - a)
                for b in range(2):
                    col = first + 2 * quad + (1 - b)
                    cell = ext[row, col // 8, col % 8 : col % 8 + 1, :]
                    for half in range(2):
                        part = cell[:, half * 128 : half * 128 + 128]
                        spread = jnp.broadcast_to(part, (16, 128)) * own_lanes
                        start = quad * 32 + half * 16
                        q = 2 * a + b
                        lhs[start : start + 16, q * 128 : q * 128 + 128] = spread.astype(bf16)
        embedded = dot(lhs[...], we[...]).astype(bf16)
        dst[i] = embedded.reshape(cols, samples, 256)
        return carry

    lax.fori_loop(0, rows, step, 0)


def merge_pair(top, bottom, merge_in, mo):
    count = top.shape[0]
    stacked = jnp.concatenate([top, bottom], axis=-1).reshape(count * samples, 256)
    hidden = jnp.maximum(dot(stacked, merge_in), 0.0).astype(bf16)
    return dot(hidden, mo).astype(bf16).reshape(count, samples, 128)


def merge_quads(src, dst, merge_in, mo, rows, cols):
    def step(i, carry):
        stacked = src[i].reshape(cols * samples, 256)
        hidden = jnp.maximum(dot(stacked, merge_in[...]), 0.0).astype(bf16)
        dst[i] = dot(hidden, mo[...]).astype(bf16).reshape(cols, samples, 128)
        return carry

    lax.fori_loop(0, rows, step, 0)


def paired_columns(cells):
    count = cells.shape[0] // 2
    split = cells.reshape(count, 2, samples, 128)
    low = low_half((count, samples, 128))
    return jnp.where(low, split[:, 0], split[:, 1])


def up_own_body(
    place, own, row_a, row_b, col_a, col_b, wq, we, merge_in, mo, out, ext, lhs, f0, f1, f2, f3, l1
):
    spread_tiles(place, own, row_a, row_b, col_a, col_b, ext)
    embed_quads(ext, we, lhs, f0, 3)
    conv_layer(f0, f1, wq.at[0], 6, 10, False)
    conv_layer(f1, f2, wq.at[1], 5, 9, True)
    conv_layer(f2, f3, wq.at[2], 4, 8, False)
    merge_quads(f3, l1, merge_in, mo, 4, 8)
    top = jnp.concatenate([paired_columns(l1[0]), paired_columns(l1[2])], axis=0)
    bottom = jnp.concatenate([paired_columns(l1[1]), paired_columns(l1[3])], axis=0)
    l2 = merge_pair(top, bottom, merge_in[...], mo[...])
    l3 = merge_pair(paired_columns(l2[0:4]), paired_columns(l2[4:8]), merge_in[...], mo[...])
    out[...] = paired_columns(l3)[0]


def up_wide_first_body(place, own, row_a, row_b, col_a, col_b, wq, we, f1, ext, lhs, f0):
    spread_tiles(place, own, row_a, row_b, col_a, col_b, ext)
    embed_quads(ext, we, lhs, f0, 7)
    conv_layer(f0, f1, wq.at[0], 10, 14, False)


def up_wide_second_body(f1, wq, f3, f2):
    conv_layer(f1, f2, wq.at[1], 9, 13, True)
    conv_layer(f2, f3, wq.at[2], 8, 12, False)


def up_wide_merge_body(f3, merge_in, mo, l1, l2):
    merge_quads(f3, l1, merge_in, mo, 8, 12)
    for i in range(4):
        l2[i] = merge_pair(
            paired_columns(l1[2 * i]), paired_columns(l1[2 * i + 1]), merge_in[...], mo[...]
        )


def mid_body(place, z0, z1, z2, z3, merge_in, mo, a3, a4, p5, send1, send3, strip, l4s):
    row = place[0]
    col = place[1]
    deep = row // 4
    high = row % 4
    wide = col // 2
    core = col % 2
    for m, ref in enumerate((z0, z1, z2, z3)):
        for n in range(4):
            for k in range(2):
                strip[deep ^ m, high ^ n, core ^ k] = ref[n, k]
    cells = strip[...].reshape(8, 2, 2, samples, 128)
    l4 = merge_pair(
        cells[:, 0].reshape(16, samples, 128),
        cells[:, 1].reshape(16, samples, 128),
        merge_in[...],
        mo[...],
    )
    l4s[...] = l4.reshape(8, 2, samples, 128)
    pairs = paired_columns(l4).reshape(4, 2, samples, 128)
    l5 = merge_pair(pairs[:, 0], pairs[:, 1], merge_in[...], mo[...])
    packed = paired_columns(l5)
    p5[...] = packed
    low = low_half((samples, 128))
    wide_even = wide % 2 == 0
    for d in range(3):
        line = (row + d + (n_row - 1)) % n_row
        left = strip[line // 4, line % 4, 0]
        right = strip[line // 4, line % 4, 1]
        a3[d, 0] = left
        a3[d, 1] = right
        left4 = l4s[line // 2, 0]
        right4 = l4s[line // 2, 1]
        a4[d, 0] = left4
        a4[d, 1] = right4
        to_right = jnp.where(low, right4, right)
        to_left = jnp.where(low, left, left4)
        send1[d] = jnp.where(wide_even, to_right, to_left)
        send3[d] = jnp.where(wide_even, to_left, to_right)
    send1[3:5] = packed
    send3[3:5] = packed


def both_lanes(cells):
    wide = cells.astype(f32)
    turned = pltpu.roll(wide, 64, wide.ndim - 1)
    low = low_half(wide.shape)
    return jnp.where(low, wide, turned).astype(bf16), jnp.where(low, turned, wide).astype(bf16)


def refine(parent, child, down_in, do):
    count = parent.shape[0]
    low = low_half(parent.shape)
    joined = jnp.where(low, parent, child).reshape(count * samples, 128)
    inner = jnp.maximum(dot(joined, down_in), 0.0).astype(bf16)
    outcome = dot(inner, do).reshape(count, samples, 128)
    return (outcome + child.astype(f32) + parent.astype(f32)).astype(bf16)


def descent_body(
    place,
    slots,
    a3,
    a4,
    p5,
    q1,
    q2,
    q3,
    f3,
    l1,
    l2,
    merge_in,
    mo,
    down_in,
    do,
    di0,
    do0,
    wq,
    wh,
    out,
    l5s,
    c6s,
    c3s,
    p3s,
    c2s,
    n0,
    r1,
    r2,
    r3,
):
    row = place[0]
    col = place[1]
    wide = col // 2
    core = col % 2
    wide_even = wide % 2 == 0
    merge_weights = merge_in[...]
    back_weights = mo[...]
    in_weights = down_in[...]
    out_weights = do[...]

    for m, ref, start in ((0, p5, 0), (1, q1, 3), (2, q2, 0), (3, q3, 3)):
        for pair in range(2):
            first, second = both_lanes(ref[start + pair])
            l5s[wide ^ m, 2 * pair] = first
            l5s[wide ^ m, 2 * pair + 1] = second
    grid = l5s[...].reshape(2, 2, 2, 2, samples, 128)
    low4 = low_half((4, samples, 128))
    top = jnp.where(
        low4,
        grid[:, 0, :, 0].reshape(4, samples, 128),
        grid[:, 1, :, 0].reshape(4, samples, 128),
    )
    bottom = jnp.where(
        low4,
        grid[:, 0, :, 1].reshape(4, samples, 128),
        grid[:, 1, :, 1].reshape(4, samples, 128),
    )
    l6 = merge_pair(top, bottom, merge_weights, back_weights)
    low1 = low_half((1, samples, 128))
    l7 = merge_pair(
        jnp.where(low1, l6[0:1], l6[2:3]),
        jnp.where(low1, l6[1:2], l6[3:4]),
        merge_weights,
        back_weights,
    )
    c6s[...] = refine(
        jnp.broadcast_to(l7, (4, samples, 128)), l6, in_weights, out_weights
    ).reshape(2, 2, samples, 128)

    side = jnp.where(core == 0, (wide + 3) % 4, (wide + 1) % 4)
    lines = [(row + d + (n_row - 1)) % n_row for d in range(3)]
    parents5 = []
    children5 = []
    for place_x in (wide, side):
        for line in lines:
            deep = line // 4
            parents5.append(c6s[place_x // 2, deep // 2])
            children5.append(l5s[place_x, deep])
    c5 = refine(jnp.stack(parents5), jnp.stack(children5), in_weights, out_weights)

    from_first = jnp.logical_xor(wide_even, core == 0)
    side_cells = jnp.where(from_first, q1[0:3], q3[0:3])
    side_low, side_high = both_lanes(side_cells)
    side4 = jnp.where(core == 0, side_low, side_high)
    side3 = jnp.where(core == 0, side_high, side_low)
    own4 = a4[...]
    children4 = jnp.concatenate([own4[:, 0], own4[:, 1], side4], axis=0)
    parents4 = jnp.concatenate([c5[0:3], c5[0:3], c5[3:6]], axis=0)
    c4 = refine(parents4, children4, in_weights, out_weights)
    own3_0, own3_1 = both_lanes(a3[:, 0])
    own3_2, own3_3 = both_lanes(a3[:, 1])
    for k, cells in enumerate((side3, own3_0, own3_1, own3_2, own3_3, side3)):
        c3s[k] = cells
    for k, start in enumerate((6, 0, 0, 3, 3, 6)):
        p3s[k] = c4[start : start + 3]
    window = pl.ds(2 * core, 4)
    c3 = refine(
        p3s[window].reshape(12, samples, 128),
        c3s[window].reshape(12, samples, 128),
        in_weights,
        out_weights,
    ).reshape(4, 3, samples, 128)
    parents2 = jnp.stack([c3[j, i] for i in (0, 1, 1, 2) for j in (0, 1, 1, 2, 2, 3)])
    c2s[...] = refine(
        parents2, l2[...].reshape(24, samples, 128), in_weights, out_weights
    ).reshape(4, 6, samples, 128)

    sub = lax.broadcasted_iota(jnp.int32, (128, 128), 0)
    lane = lax.broadcasted_iota(jnp.int32, (128, 128), 1)
    averager = jnp.where((sub < 64) == (lane < 64), 1.0 / 64, 0.0).astype(bf16)

    def fine_row(i, carry):
        parent = c2s[i // 2]
        parent = jnp.broadcast_to(parent[:, None], (6, 2, samples, 128)).reshape(12, samples, 128)
        c1 = refine(parent, l1[i], in_weights, out_weights)
        c1_wide = c1.astype(f32).reshape(12 * samples, 128)
        for a in range(2):
            child = f3[i, :, :, a * 128 : a * 128 + 128]
            joined = jnp.concatenate([child, c1], axis=-1).reshape(12 * samples, 256)
            inner = jnp.maximum(dot(joined, di0[...]), 0.0).astype(bf16)
            fine = dot(inner, do0[...])
            fine = fine + child.astype(f32).reshape(12 * samples, 128) + c1_wide
            mean = dot((fine * fine).astype(bf16), averager)
            normed = fine * lax.rsqrt(mean + norm_eps)
            n0[i, :, :, a * 128 : a * 128 + 128] = normed.astype(bf16).reshape(12, samples, 128)
        return carry

    lax.fori_loop(0, 8, fine_row, 0)
    conv_layer(n0, r1, wq.at[0], 7, 11, True)
    conv_layer(r1, r2, wq.at[1], 6, 10, False)
    conv_layer(r2, r3, wq.at[2], 5, 9, True)
    stacked = jnp.concatenate(
        [r3[:, quad].reshape(5 * samples, 256) for quad in range(9)], axis=-1
    )
    cell_logits = dot(stacked, wh[...]).reshape(5, samples, 128)
    coarse = cell_logits.astype(bf16)
    rest = (cell_logits - coarse.astype(f32)).astype(bf16)
    places = lax.broadcasted_iota(jnp.int32, (128, 64), 0)
    for i in range(8):
        quad_row = (i + 1) // 2
        chosen = (places == slots[i : i + 1, :] + 64 * (i % 2)).astype(bf16)
        out[:, i, :] = dot(coarse[quad_row], chosen) + dot(rest[quad_row], chosen)


def swap(value, partner):
    pairs = []
    for r in range(n_row):
        for c in range(n_col):
            pr, pc = partner(r, c)
            pairs.append((r * n_col + c, pr * n_col + pc))
    return lax.ppermute(value, ("row", "col"), pairs)


def pair_after(i, count):
    return i ^ 1


def pair_before(i, count):
    return (((i - 1) % count ^ 1) + 1) % count


def on_device(
    readouts, w_embed, w_up, merge_in, merge_out, down_in, down_out, w_down, w_head, qubit_slot
):
    row = lax.axis_index("row")
    col = lax.axis_index("col")
    place = jnp.stack([row, col]).astype(jnp.int32)
    col_even = col % 2 == 0

    row_a = swap(readouts, lambda r, c: (pair_after(r, n_row), c))
    row_b = swap(readouts, lambda r, c: (pair_before(r, n_row), c))
    tiles = jnp.stack([readouts, row_a, row_b])
    left = tiles[:, :, 0:8]
    right = tiles[:, :, 8:16]
    col_a = swap(jnp.where(col_even, right, left), lambda r, c: (r, pair_after(c, n_col)))
    col_b = swap(jnp.where(col_even, left, right), lambda r, c: (r, pair_before(c, n_col)))

    wq_up, we, mo = whole_call(
        prep_up_body,
        (arr((3, 1024, 256)), arr((512, 256)), arr((256, 128))),
        [],
        (w_up, w_embed, merge_out),
    )
    wq_down, di0, do0, do, wh = whole_call(
        prep_down_body,
        (
            arr((3, 1024, 256)),
            arr((256, 512)),
            arr((512, 128)),
            arr((256, 128)),
            arr((2304, 128)),
        ),
        [],
        (w_down, down_in, down_out, jnp.tile(w_head, (1, 32))),
    )

    tile_args = (place, readouts, row_a, row_b, col_a, col_b)
    quads = lambda rows, cols: pltpu.VMEM((rows, cols, samples, 256), bf16)
    ext = pltpu.VMEM((24, 4, 8, 256), f32)
    l3 = whole_call(
        up_own_body,
        arr((samples, 128)),
        [
            ext,
            pltpu.VMEM((11 * samples, 512), bf16),
            quads(7, 11),
            quads(6, 10),
            quads(5, 9),
            quads(4, 8),
            pltpu.VMEM((4, 8, samples, 128), bf16),
        ],
        (*tile_args, wq_up, we, merge_in, mo),
        smem=(0,),
    )

    pair = jnp.stack([l3, swap(l3, lambda r, c: (r, c ^ 1))])
    four = jnp.stack([pair] + [swap(pair, lambda r, c, m=m: (r ^ m, c)) for m in (1, 2, 3)])
    f1 = whole_call(
        up_wide_first_body,
        arr((10, 14, samples, 256)),
        [ext, pltpu.VMEM((15 * samples, 512), bf16), quads(11, 15)],
        (*tile_args, wq_up, we),
        smem=(0,),
    )
    strips = [four] + [swap(four, lambda r, c, m=m: (r ^ (4 * m), c)) for m in (1, 2, 3)]
    f3 = whole_call(
        up_wide_second_body, arr((8, 12, samples, 256)), [quads(9, 13)], (f1, wq_up)
    )
    a3, a4, p5, send1, send3 = whole_call(
        mid_body,
        (
            arr((3, 2, samples, 128)),
            arr((3, 2, samples, 128)),
            arr((2, samples, 128)),
            arr((5, samples, 128)),
            arr((5, samples, 128)),
        ),
        [pltpu.VMEM((4, 4, 2, samples, 128), bf16), pltpu.VMEM((8, 2, samples, 128), bf16)],
        (place, *strips, merge_in, mo),
        smem=(0,),
    )
    q1 = swap(send1, lambda r, c: (r, c ^ 2))
    q2 = swap(p5, lambda r, c: (r, c ^ 4))
    q3 = swap(send3, lambda r, c: (r, c ^ 6))
    l1, l2 = whole_call(
        up_wide_merge_body,
        (arr((8, 12, samples, 128)), arr((4, 6, samples, 128))),
        [],
        (f3, merge_in, mo),
    )
    slots = qubit_slot.reshape(qubit_slot.shape[0], qubit_slot.shape[2])
    return whole_call(
        descent_body,
        arr((samples, 8, 64), f32),
        [
            pltpu.VMEM((4, 4, samples, 128), bf16),
            pltpu.VMEM((2, 2, samples, 128), bf16),
            pltpu.VMEM((6, 3, samples, 128), bf16),
            pltpu.VMEM((6, 3, samples, 128), bf16),
            pltpu.VMEM((4, 6, samples, 128), bf16),
            quads(8, 12),
            quads(7, 11),
            quads(6, 10),
            quads(5, 9),
        ],
        (
            place,
            slots,
            a3,
            a4,
            p5,
            q1,
            q2,
            q3,
            f3,
            l1,
            l2,
            merge_in,
            mo,
            down_in,
            do,
            di0,
            do0,
            wq_down,
            wh,
        ),
        smem=(0,),
    )


def solution(mesh):
    placed = (P("row", "col", None), P(), P(), P(), P(), P(), P(), P(), P(), P("row", "col", None))
    return jax.shard_map(
        on_device, mesh=mesh, in_specs=placed, out_specs=P(None, "row", "col"), check_vma=False
    )
```

```python
import functools

import jax
import jax.numpy as jnp
from jax import lax
from jax.experimental import pallas as pl
from jax.experimental.pallas import tpu as pltpu
from jax.sharding import PartitionSpec as P

norm_eps = 1e-05
bf16 = jnp.bfloat16
f32 = jnp.float32
n_row = 16
n_col = 8
samples = 32
vmem_bytes = 48 * 1024 * 1024


def dot(left, right):
    return jnp.dot(left, right, preferred_element_type=f32)


def low_half(shape):
    return lax.broadcasted_iota(jnp.int32, shape, len(shape) - 1) < 64


def whole_call(body, out_shapes, scratch, args, smem=(), outside=()):
    specs = [
        pl.BlockSpec(
            memory_space=pltpu.SMEM if i in smem else pltpu.HBM if i in outside else pltpu.VMEM
        )
        for i in range(len(args))
    ]
    return pl.pallas_call(
        body,
        out_shape=out_shapes,
        in_specs=specs,
        out_specs=jax.tree.map(lambda _: pl.BlockSpec(memory_space=pltpu.VMEM), out_shapes),
        scratch_shapes=scratch,
        compiler_params=pltpu.CompilerParams(vmem_limit_bytes=vmem_bytes),
    )(*args)


def arr(shape, dtype=bf16):
    return jax.ShapeDtypeStruct(shape, dtype)


def fill_quad_weights(src, out, layer, from_odd):
    zero = jnp.zeros((64, 64), bf16)

    def tap_of(step, parity_in, parity_out):
        place_in = 1 - parity_in if from_odd else parity_in
        place_out = parity_out if from_odd else 1 - parity_out
        tap = 2 * step + place_in - place_out
        return tap if 0 <= tap <= 2 else None

    for di in range(2):
        for dj in range(2):
            for a in range(2):
                for b in range(2):
                    base = ((di * 2 + dj) * 4 + a * 2 + b) * 64
                    for oa in range(2):
                        tap_row = tap_of(di, a, oa)
                        blocks = []
                        for ob in range(2):
                            tap_col = tap_of(dj, b, ob)
                            if tap_row is None or tap_col is None:
                                blocks.append(zero)
                            else:
                                blocks.append(src[layer, 3 * tap_row + tap_col])
                        out[layer, base : base + 64, oa * 128 : oa * 128 + 128] = jnp.concatenate(
                            blocks, axis=1
                        )


def dot_rows(left, right):
    return lax.dot_general(left, right, (((0,), (0,)), ((), ())), preferred_element_type=f32)


def lane_copies(first, second):
    row = lax.broadcasted_iota(jnp.int32, (64, 128), 0)
    lane = lax.broadcasted_iota(jnp.int32, (64, 128), 1)
    kept = jnp.where(lane < 64, first, second) > 0
    return jnp.where(kept & (row == lane % 64), 1.0, 0.0).astype(bf16)


def copies_in(sems, *pairs):
    copies = [pltpu.make_async_copy(src, dst, sems.at[i]) for i, (src, dst) in enumerate(pairs)]
    for copy in copies:
        copy.start()
    return copies


def prep_up_body(
    own, w_up, w_embed, merge_in, merge_out_t, own_out, wq, we, mi, mo, w_up_s, w_embed_s, mo_s, sems
):
    copies = copies_in(
        sems,
        (w_up, w_up_s),
        (w_embed, w_embed_s),
        (merge_out_t, mo_s),
        (own, own_out),
        (merge_in, mi),
    )
    copies[0].wait()
    for layer in range(3):
        fill_quad_weights(w_up_s, wq, layer, layer % 2 == 0)
    copies[1].wait()
    tiled = jnp.concatenate([w_embed_s[...].astype(f32)] * 16, axis=0)
    none = jnp.zeros((128, 64), f32)
    for a in range(2):
        for b in range(2):
            q = 2 * a + b
            pair = [tiled, none] if b == 0 else [none, tiled]
            we[q * 128 : q * 128 + 128, a * 128 : a * 128 + 128] = jnp.concatenate(
                pair, axis=1
            ).astype(bf16)
            we[q * 128 : q * 128 + 128, (1 - a) * 128 : (1 - a) * 128 + 128] = jnp.zeros(
                (128, 128), bf16
            )
    copies[2].wait()
    mo[...] = dot_rows(mo_s[...], lane_copies(1, 1)).astype(bf16)
    copies[3].wait()
    copies[4].wait()


def prep_down_body(
    w_down,
    down_in,
    down_out_t,
    w_head_t,
    wq,
    di,
    di0,
    do0,
    do,
    wh,
    w_down_s,
    do_s,
    head_s,
    sems,
):
    copies = copies_in(
        sems, (w_down, w_down_s), (down_in, di), (down_out_t, do_s), (w_head_t, head_s)
    )
    copies[0].wait()
    for layer in range(3):
        fill_quad_weights(w_down_s, wq, layer, layer % 2 == 0)
    copies[1].wait()
    zero = jnp.zeros((64, 256), bf16)
    parent = di[0:64, :]
    child = di[64:128, :]
    di0[0:64, 0:256] = child
    di0[0:64, 256:512] = zero
    di0[64:128, 0:256] = zero
    di0[64:128, 256:512] = child
    di0[128:192, 0:256] = parent
    di0[128:192, 256:512] = parent
    di0[192:256, 0:256] = zero
    di0[192:256, 256:512] = zero
    copies[2].wait()
    back = do_s[...]
    do0[0:256, :] = dot_rows(back, lane_copies(1, 0)).astype(bf16)
    do0[256:512, :] = dot_rows(back, lane_copies(0, 1)).astype(bf16)
    do[...] = dot_rows(back, lane_copies(1, 1)).astype(bf16)
    copies[3].wait()
    output = lax.broadcasted_iota(jnp.int32, (4, 128), 0)
    lane = lax.broadcasted_iota(jnp.int32, (4, 128), 1)
    head = dot_rows(head_s[...], jnp.where(lane % 4 == output, 1.0, 0.0).astype(bf16))
    lane = lax.broadcasted_iota(jnp.int32, (64, 128), 1)
    for quad in range(8):
        for a in range(2):
            for b in range(2):
                base = quad * 256 + (a * 2 + b) * 64
                first = a * 64 + 4 * (2 * quad + b)
                kept = jnp.where((lane >= first) & (lane < first + 4), head, 0.0)
                wh[base : base + 64, :] = kept.astype(bf16)


def conv_layer(src, dst, weights, rows, cols, to_odd):
    low = low_half((cols, samples, 128))
    for i in range(rows):
        here = src[i, 0:cols]
        right = src[i, 1 : cols + 1]
        below = src[i + 1, 0:cols]
        corner = src[i + 1, 1 : cols + 1]
        stacked = jnp.concatenate([here, right, below, corner], axis=-1)
        update = dot(stacked.reshape(cols * samples, 1024), weights[...])
        update = jnp.maximum(update, 0.0).reshape(cols, samples, 256)
        if to_odd:
            old0 = jnp.where(low, corner[..., 0:128], below[..., 0:128])
            old1 = jnp.where(low, right[..., 128:256], here[..., 128:256])
        else:
            old0 = jnp.where(low, here[..., 0:128], right[..., 0:128])
            old1 = jnp.where(low, below[..., 128:256], corner[..., 128:256])
        dst[i, :, :, 0:128] = (old0.astype(f32) + update[..., 0:128]).astype(bf16)
        dst[i, :, :, 128:256] = (old1.astype(f32) + update[..., 128:256]).astype(bf16)


def spread_tiles(place, tiles, col_a, col_b, ext):
    row_even = place[0] % 2 == 0
    col_even = place[1] % 2 == 0
    after_row = jnp.where(row_even, 16, 0)
    before_row = jnp.where(row_even, 0, 16)
    after_col = jnp.where(col_even, 3, 0)
    before_col = jnp.where(col_even, 0, 3)
    for tile, start in ((0, 8), (1, after_row), (2, before_row)):
        cells = tiles[tile].astype(f32)
        ext[pl.ds(start, 8), 1] = cells[:, 0:8]
        ext[pl.ds(start, 8), 2] = cells[:, 8:16]
        ext[pl.ds(start, 8), after_col] = col_a[tile].astype(f32)
        ext[pl.ds(start, 8), before_col] = col_b[tile].astype(f32)


def embed_quads(ext, we, dst, halo):
    rows = 4 + halo
    cols = 8 + halo
    first = 8 - halo
    sub = lax.broadcasted_iota(jnp.int32, (16, 128), 0)
    lane = lax.broadcasted_iota(jnp.int32, (16, 128), 1)
    own_lanes = (lane // 8 == sub).astype(f32)
    for i in range(rows):
        quads = []
        for quad in range(cols):
            parts = []
            for a in range(2):
                row = first + 2 * i + (1 - a)
                for b in range(2):
                    col = first + 2 * quad + (1 - b)
                    cell = ext[row, col // 8, col % 8 : col % 8 + 1, :]
                    halves = [
                        jnp.broadcast_to(cell[:, k : k + 128], (16, 128)) * own_lanes
                        for k in (0, 128)
                    ]
                    parts.append(jnp.concatenate(halves, axis=0).astype(bf16))
            quads.append(jnp.concatenate(parts, axis=-1))
        embedded = dot(jnp.concatenate(quads, axis=0), we[...]).astype(bf16)
        dst[i] = embedded.reshape(cols, samples, 256)


def merge_pair(top, bottom, merge_in, mo):
    count = top.shape[0]
    stacked = jnp.concatenate([top, bottom], axis=-1).reshape(count * samples, 256)
    hidden = jnp.maximum(dot(stacked, merge_in), 0.0).astype(bf16)
    return dot(hidden, mo).astype(bf16).reshape(count, samples, 128)


def merge_quads(src, dst, merge_in, mo, rows, cols):
    for i in range(rows):
        stacked = src[i].reshape(cols * samples, 256)
        hidden = jnp.maximum(dot(stacked, merge_in[...]), 0.0).astype(bf16)
        dst[i] = dot(hidden, mo[...]).astype(bf16).reshape(cols, samples, 128)


def paired_columns(cells):
    count = cells.shape[0] // 2
    split = cells.reshape(count, 2, samples, 128)
    low = low_half((count, samples, 128))
    return jnp.where(low, split[:, 0], split[:, 1])


def up_own_body(place, tiles, col_a, col_b, wq, we, merge_in, mo, out, ext, f0, f1, f2, f3, l1):
    spread_tiles(place, tiles, col_a, col_b, ext)
    embed_quads(ext, we, f0, 3)
    conv_layer(f0, f1, wq.at[0], 6, 10, False)
    conv_layer(f1, f2, wq.at[1], 5, 9, True)
    conv_layer(f2, f3, wq.at[2], 4, 8, False)
    merge_quads(f3, l1, merge_in, mo, 4, 8)
    top = jnp.concatenate([paired_columns(l1[0]), paired_columns(l1[2])], axis=0)
    bottom = jnp.concatenate([paired_columns(l1[1]), paired_columns(l1[3])], axis=0)
    l2 = merge_pair(top, bottom, merge_in[...], mo[...])
    l3 = merge_pair(paired_columns(l2[0:4]), paired_columns(l2[4:8]), merge_in[...], mo[...])
    out[...] = paired_columns(l3)[0]


def up_wide_first_body(place, tiles, col_a, col_b, wq, we, f1, ext, f0):
    spread_tiles(place, tiles, col_a, col_b, ext)
    embed_quads(ext, we, f0, 7)
    conv_layer(f0, f1, wq.at[0], 10, 14, False)


def up_wide_second_body(f1, wq, f3, f2):
    conv_layer(f1, f2, wq.at[1], 9, 13, True)
    conv_layer(f2, f3, wq.at[2], 8, 12, False)


def up_wide_merge_body(f3, merge_in, mo, l1, l2):
    merge_quads(f3, l1, merge_in, mo, 8, 12)
    for i in range(4):
        l2[i] = merge_pair(
            paired_columns(l1[2 * i]), paired_columns(l1[2 * i + 1]), merge_in[...], mo[...]
        )


def mid_body(place, z0, z1, z2, z3, merge_in, mo, a3, a4, p5, send1, send3, strip, l4s):
    row = place[0]
    col = place[1]
    deep = row // 4
    high = row % 4
    wide = col // 2
    core = col % 2
    for m, ref in enumerate((z0, z1, z2, z3)):
        for n in range(4):
            for k in range(2):
                strip[deep ^ m, high ^ n, core ^ k] = ref[n, k]
    cells = strip[...].reshape(8, 2, 2, samples, 128)
    l4 = merge_pair(
        cells[:, 0].reshape(16, samples, 128),
        cells[:, 1].reshape(16, samples, 128),
        merge_in[...],
        mo[...],
    )
    l4s[...] = l4.reshape(8, 2, samples, 128)
    pairs = paired_columns(l4).reshape(4, 2, samples, 128)
    l5 = merge_pair(pairs[:, 0], pairs[:, 1], merge_in[...], mo[...])
    packed = paired_columns(l5)
    p5[...] = packed
    low = low_half((samples, 128))
    wide_even = wide % 2 == 0
    for d in range(3):
        line = (row + d + (n_row - 1)) % n_row
        left = strip[line // 4, line % 4, 0]
        right = strip[line // 4, line % 4, 1]
        a3[d, 0] = left
        a3[d, 1] = right
        left4 = l4s[line // 2, 0]
        right4 = l4s[line // 2, 1]
        a4[d, 0] = left4
        a4[d, 1] = right4
        to_right = jnp.where(low, right4, right)
        to_left = jnp.where(low, left, left4)
        send1[d] = jnp.where(wide_even, to_right, to_left)
        send3[d] = jnp.where(wide_even, to_left, to_right)
    send1[3:5] = packed
    send3[3:5] = packed


def both_lanes(cells):
    wide = cells.astype(f32)
    turned = pltpu.roll(wide, 64, wide.ndim - 1)
    low = low_half(wide.shape)
    return jnp.where(low, wide, turned).astype(bf16), jnp.where(low, turned, wide).astype(bf16)


def refine(parent, child, down_in, do):
    count = parent.shape[0]
    low = low_half(parent.shape)
    joined = jnp.where(low, parent, child).reshape(count * samples, 128)
    inner = jnp.maximum(dot(joined, down_in), 0.0).astype(bf16)
    outcome = dot(inner, do).reshape(count, samples, 128)
    return (outcome + child.astype(f32) + parent.astype(f32)).astype(bf16)


def descent_body(
    place,
    slots,
    a3,
    a4,
    p5,
    q1,
    q2,
    q3,
    f3,
    l1,
    l2,
    merge_in,
    mo,
    down_in,
    do,
    di0,
    do0,
    wq,
    wh,
    out,
    l5s,
    c6s,
    c3s,
    p3s,
    c2s,
    n0,
    r1,
    r2,
    r3,
):
    row = place[0]
    col = place[1]
    wide = col // 2
    core = col % 2
    wide_even = wide % 2 == 0
    merge_weights = merge_in[...]
    back_weights = mo[...]
    in_weights = down_in[...]
    out_weights = do[...]

    for m, ref, start in ((0, p5, 0), (1, q1, 3), (2, q2, 0), (3, q3, 3)):
        for pair in range(2):
            first, second = both_lanes(ref[start + pair])
            l5s[wide ^ m, 2 * pair] = first
            l5s[wide ^ m, 2 * pair + 1] = second
    grid = l5s[...].reshape(2, 2, 2, 2, samples, 128)
    low4 = low_half((4, samples, 128))
    top = jnp.where(
        low4,
        grid[:, 0, :, 0].reshape(4, samples, 128),
        grid[:, 1, :, 0].reshape(4, samples, 128),
    )
    bottom = jnp.where(
        low4,
        grid[:, 0, :, 1].reshape(4, samples, 128),
        grid[:, 1, :, 1].reshape(4, samples, 128),
    )
    l6 = merge_pair(top, bottom, merge_weights, back_weights)
    low1 = low_half((1, samples, 128))
    l7 = merge_pair(
        jnp.where(low1, l6[0:1], l6[2:3]),
        jnp.where(low1, l6[1:2], l6[3:4]),
        merge_weights,
        back_weights,
    )
    c6s[...] = refine(
        jnp.broadcast_to(l7, (4, samples, 128)), l6, in_weights, out_weights
    ).reshape(2, 2, samples, 128)

    side = jnp.where(core == 0, (wide + 3) % 4, (wide + 1) % 4)
    lines = [(row + d + (n_row - 1)) % n_row for d in range(3)]
    parents5 = []
    children5 = []
    for place_x in (wide, side):
        for line in lines:
            deep = line // 4
            parents5.append(c6s[place_x // 2, deep // 2])
            children5.append(l5s[place_x, deep])
    c5 = refine(jnp.stack(parents5), jnp.stack(children5), in_weights, out_weights)

    from_first = jnp.logical_xor(wide_even, core == 0)
    side_cells = jnp.where(from_first, q1[0:3], q3[0:3])
    side_low, side_high = both_lanes(side_cells)
    side4 = jnp.where(core == 0, side_low, side_high)
    side3 = jnp.where(core == 0, side_high, side_low)
    own4 = a4[...]
    children4 = jnp.concatenate([own4[:, 0], own4[:, 1], side4], axis=0)
    parents4 = jnp.concatenate([c5[0:3], c5[0:3], c5[3:6]], axis=0)
    c4 = refine(parents4, children4, in_weights, out_weights)
    own3_0, own3_1 = both_lanes(a3[:, 0])
    own3_2, own3_3 = both_lanes(a3[:, 1])
    for k, cells in enumerate((side3, own3_0, own3_1, own3_2, own3_3, side3)):
        c3s[k] = cells
    for k, start in enumerate((6, 0, 0, 3, 3, 6)):
        p3s[k] = c4[start : start + 3]
    window = pl.ds(2 * core, 4)
    c3 = refine(
        p3s[window].reshape(12, samples, 128),
        c3s[window].reshape(12, samples, 128),
        in_weights,
        out_weights,
    ).reshape(4, 3, samples, 128)
    parents2 = jnp.stack([c3[j, i] for i in (0, 1, 1, 2) for j in (0, 1, 1, 2, 2, 3)])
    c2s[...] = refine(
        parents2, l2[...].reshape(24, samples, 128), in_weights, out_weights
    ).reshape(4, 6, samples, 128)

    sub = lax.broadcasted_iota(jnp.int32, (128, 128), 0)
    lane = lax.broadcasted_iota(jnp.int32, (128, 128), 1)
    averager = jnp.where((sub < 64) == (lane < 64), 1.0 / 64, 0.0).astype(bf16)

    low11 = low_half((11, samples, 128))
    for i in range(8):
        parent = c2s[i // 2]
        parent = jnp.broadcast_to(parent[:, None], (6, 2, samples, 128)).reshape(12, samples, 128)
        c1 = refine(parent, l1[i], in_weights, out_weights)
        c1_wide = c1.astype(f32).reshape(12 * samples, 128)
        for a in range(2):
            row_to = i - (1 - a)
            if not 0 <= row_to < 7:
                continue
            child = f3[i, :, :, a * 128 : a * 128 + 128]
            joined = jnp.concatenate([child, c1], axis=-1).reshape(12 * samples, 256)
            inner = jnp.maximum(dot(joined, di0[...]), 0.0).astype(bf16)
            fine = dot(inner, do0[...])
            fine = fine + child.astype(f32).reshape(12 * samples, 128) + c1_wide
            mean = dot((fine * fine).astype(bf16), averager)
            normed = (fine * lax.rsqrt(mean + norm_eps)).astype(bf16).reshape(12, samples, 128)
            n0[row_to, :, :, a * 128 : a * 128 + 128] = jnp.where(low11, normed[1:12], normed[0:11])
    conv_layer(n0, r1, wq.at[0], 6, 10, False)
    conv_layer(r1, r2, wq.at[1], 5, 9, True)
    conv_layer(r2, r3, wq.at[2], 4, 8, False)
    stacked = jnp.concatenate(
        [r3[:, quad].reshape(4 * samples, 256) for quad in range(8)], axis=-1
    )
    cell_logits = dot(stacked, wh[...]).reshape(4, samples, 128)
    coarse = cell_logits.astype(bf16)
    rest = (cell_logits - coarse.astype(f32)).astype(bf16)
    places = lax.broadcasted_iota(jnp.int32, (128, 64), 0)
    for i in range(8):
        chosen = (places == slots[i : i + 1, :] + 64 * (i % 2)).astype(bf16)
        out[:, i, :] = dot(coarse[i // 2], chosen) + dot(rest[i // 2], chosen)


def swap(value, partner):
    pairs = []
    for r in range(n_row):
        for c in range(n_col):
            pr, pc = partner(r, c)
            pairs.append((r * n_col + c, pr * n_col + pc))
    return lax.ppermute(value, ("row", "col"), pairs)


def pair_after(i, count):
    return i ^ 1


def pair_before(i, count):
    return (((i - 1) % count ^ 1) + 1) % count


def on_device(
    readouts, w_embed, w_up, merge_in, merge_out, down_in, down_out, w_down, w_head, qubit_slot
):
    row = lax.axis_index("row")
    col = lax.axis_index("col")
    place = jnp.stack([row, col]).astype(jnp.int32)
    col_even = col % 2 == 0

    row_a = swap(readouts, lambda r, c: (pair_after(r, n_row), c))
    row_b = swap(readouts, lambda r, c: (pair_before(r, n_row), c))
    own, wq_up, we, mi, mo = whole_call(
        prep_up_body,
        (
            arr((8, 16, 256)),
            arr((3, 1024, 256)),
            arr((512, 256)),
            arr((256, 256)),
            arr((256, 128)),
        ),
        [
            pltpu.VMEM((3, 9, 64, 64), bf16),
            pltpu.VMEM((8, 64), bf16),
            pltpu.VMEM((64, 256), bf16),
            pltpu.SemaphoreType.DMA((5,)),
        ],
        (readouts, w_up, w_embed, merge_in, merge_out.T),
        outside=(0, 1, 2, 3, 4),
    )
    tiles = jnp.stack([own, row_a, row_b])
    left = tiles[:, :, 0:8]
    right = tiles[:, :, 8:16]
    col_a = swap(jnp.where(col_even, right, left), lambda r, c: (r, pair_after(c, n_col)))
    col_b = swap(jnp.where(col_even, left, right), lambda r, c: (r, pair_before(c, n_col)))
    w_down, tiles = lax.optimization_barrier((w_down, tiles))
    wq_down, di, di0, do0, do, wh = whole_call(
        prep_down_body,
        (
            arr((3, 1024, 256)),
            arr((128, 256)),
            arr((256, 512)),
            arr((512, 128)),
            arr((256, 128)),
            arr((2048, 128)),
        ),
        [
            pltpu.VMEM((3, 9, 64, 64), bf16),
            pltpu.VMEM((64, 256), bf16),
            pltpu.VMEM((4, 64), bf16),
            pltpu.SemaphoreType.DMA((4,)),
        ],
        (w_down, down_in, down_out.T, w_head.T),
        outside=(0, 1, 2, 3),
    )

    quads = lambda rows, cols: pltpu.VMEM((rows, cols, samples, 256), bf16)
    ext = pltpu.VMEM((24, 4, 8, 256), f32)
    l3 = whole_call(
        up_own_body,
        arr((samples, 128)),
        [
            ext,
            quads(7, 11),
            quads(6, 10),
            quads(5, 9),
            quads(4, 8),
            pltpu.VMEM((4, 8, samples, 128), bf16),
        ],
        (place, tiles, col_a, col_b, wq_up, we, mi, mo),
        smem=(0,),
    )

    pair = jnp.stack([l3, swap(l3, lambda r, c: (r, c ^ 1))])
    four = jnp.stack([pair] + [swap(pair, lambda r, c, m=m: (r ^ m, c)) for m in (1, 2, 3)])
    col_a, pair = lax.optimization_barrier((col_a, pair))
    f1 = whole_call(
        up_wide_first_body,
        arr((10, 14, samples, 256)),
        [ext, quads(11, 15)],
        (place, tiles, col_a, col_b, wq_up, we),
        smem=(0,),
    )
    four, f1 = lax.optimization_barrier((four, f1))
    strips = [four] + [swap(four, lambda r, c, m=m: (r ^ (4 * m), c)) for m in (1, 2, 3)]
    f3 = whole_call(
        up_wide_second_body, arr((8, 12, samples, 256)), [quads(9, 13)], (f1, wq_up)
    )
    strips[3], f3 = lax.optimization_barrier((strips[3], f3))
    a3, a4, p5, send1, send3 = whole_call(
        mid_body,
        (
            arr((3, 2, samples, 128)),
            arr((3, 2, samples, 128)),
            arr((2, samples, 128)),
            arr((5, samples, 128)),
            arr((5, samples, 128)),
        ),
        [pltpu.VMEM((4, 4, 2, samples, 128), bf16), pltpu.VMEM((8, 2, samples, 128), bf16)],
        (place, *strips, mi, mo),
        smem=(0,),
    )
    q1 = swap(send1, lambda r, c: (r, c ^ 2))
    q2 = swap(p5, lambda r, c: (r, c ^ 4))
    q3 = swap(send3, lambda r, c: (r, c ^ 6))
    l1, l2 = whole_call(
        up_wide_merge_body,
        (arr((8, 12, samples, 128)), arr((4, 6, samples, 128))),
        [],
        (f3, mi, mo),
    )
    slots = qubit_slot.reshape(qubit_slot.shape[0], qubit_slot.shape[2])
    return whole_call(
        descent_body,
        arr((samples, 8, 64), f32),
        [
            pltpu.VMEM((4, 4, samples, 128), bf16),
            pltpu.VMEM((2, 2, samples, 128), bf16),
            pltpu.VMEM((6, 3, samples, 128), bf16),
            pltpu.VMEM((6, 3, samples, 128), bf16),
            pltpu.VMEM((4, 6, samples, 128), bf16),
            quads(7, 11),
            quads(6, 10),
            quads(5, 9),
            quads(4, 8),
        ],
        (
            place,
            slots,
            a3,
            a4,
            p5,
            q1,
            q2,
            q3,
            f3,
            l1,
            l2,
            mi,
            mo,
            di,
            do,
            di0,
            do0,
            wq_down,
            wh,
        ),
        smem=(0,),
    )


def solution(mesh):
    placed = (P("row", "col", None), P(), P(), P(), P(), P(), P(), P(), P(), P("row", "col", None))
    return jax.shard_map(
        on_device, mesh=mesh, in_specs=placed, out_specs=P(None, "row", "col"), check_vma=False
    )
```

```python
import functools

import jax
import jax.numpy as jnp
from jax import lax
from jax.experimental import pallas as pl
from jax.experimental.pallas import tpu as pltpu
from jax.sharding import PartitionSpec as P

norm_eps = 1e-05
bf16 = jnp.bfloat16
f32 = jnp.float32
n_row = 16
n_col = 8
samples = 32
vmem_bytes = 20 * 1024 * 1024


def dot(left, right):
    return jnp.dot(left, right, preferred_element_type=f32)


def low_half(shape):
    return lax.broadcasted_iota(jnp.int32, shape, len(shape) - 1) < 64


def whole_call(body, out_shapes, scratch, args, smem=(), outside=()):
    args = [
        pltpu.with_memory_space_constraint(x, pltpu.HBM) if i in outside else x
        for i, x in enumerate(args)
    ]
    specs = [
        pl.BlockSpec(
            memory_space=pltpu.SMEM if i in smem else pltpu.HBM if i in outside else pltpu.VMEM
        )
        for i in range(len(args))
    ]
    return pl.pallas_call(
        body,
        out_shape=out_shapes,
        in_specs=specs,
        out_specs=jax.tree.map(lambda _: pl.BlockSpec(memory_space=pltpu.VMEM), out_shapes),
        scratch_shapes=scratch,
        compiler_params=pltpu.CompilerParams(vmem_limit_bytes=vmem_bytes),
    )(*args)


def arr(shape, dtype=bf16):
    return jax.ShapeDtypeStruct(shape, dtype)


def fill_quad_weights(src, out, layer, from_odd):
    zero = jnp.zeros((64, 64), bf16)

    def tap_of(step, parity_in, parity_out):
        place_in = 1 - parity_in if from_odd else parity_in
        place_out = parity_out if from_odd else 1 - parity_out
        tap = 2 * step + place_in - place_out
        return tap if 0 <= tap <= 2 else None

    for di in range(2):
        for dj in range(2):
            for a in range(2):
                for b in range(2):
                    base = ((di * 2 + dj) * 4 + a * 2 + b) * 64
                    for oa in range(2):
                        tap_row = tap_of(di, a, oa)
                        blocks = []
                        for ob in range(2):
                            tap_col = tap_of(dj, b, ob)
                            if tap_row is None or tap_col is None:
                                blocks.append(zero)
                            else:
                                blocks.append(src[layer, 3 * tap_row + tap_col])
                        out[layer, base : base + 64, oa * 128 : oa * 128 + 128] = jnp.concatenate(
                            blocks, axis=1
                        )


def dot_rows(left, right):
    return lax.dot_general(left, right, (((0,), (0,)), ((), ())), preferred_element_type=f32)


def lane_copies(first, second):
    row = lax.broadcasted_iota(jnp.int32, (64, 128), 0)
    lane = lax.broadcasted_iota(jnp.int32, (64, 128), 1)
    kept = jnp.where(lane < 64, first, second) > 0
    return jnp.where(kept & (row == lane % 64), 1.0, 0.0).astype(bf16)


def copies_in(sems, *pairs):
    copies = [pltpu.make_async_copy(src, dst, sems.at[i]) for i, (src, dst) in enumerate(pairs)]
    for copy in copies:
        copy.start()
    return copies


def prep_up_body(
    own, w_up, w_embed, merge_in, merge_out_t, own_out, wq, we, mi, mo, w_up_s, w_embed_s, mo_s, sems
):
    copies = copies_in(
        sems,
        (w_up, w_up_s),
        (w_embed, w_embed_s),
        (merge_out_t, mo_s),
        (own, own_out),
        (merge_in, mi),
    )
    copies[0].wait()
    for layer in range(3):
        fill_quad_weights(w_up_s, wq, layer, layer % 2 == 0)
    copies[1].wait()
    tiled = jnp.concatenate([w_embed_s[...].astype(f32)] * 16, axis=0)
    none = jnp.zeros((128, 64), f32)
    for a in range(2):
        for b in range(2):
            q = 2 * a + b
            pair = [tiled, none] if b == 0 else [none, tiled]
            we[q * 128 : q * 128 + 128, a * 128 : a * 128 + 128] = jnp.concatenate(
                pair, axis=1
            ).astype(bf16)
            we[q * 128 : q * 128 + 128, (1 - a) * 128 : (1 - a) * 128 + 128] = jnp.zeros(
                (128, 128), bf16
            )
    copies[2].wait()
    mo[...] = dot_rows(mo_s[...], lane_copies(1, 1)).astype(bf16)
    copies[3].wait()
    copies[4].wait()


def prep_down_body(
    w_down,
    down_in,
    down_out_t,
    w_head_t,
    wq,
    di,
    di0,
    do0,
    do,
    wh,
    w_down_s,
    do_s,
    head_s,
    sems,
):
    copies = copies_in(
        sems, (w_down, w_down_s), (down_in, di), (down_out_t, do_s), (w_head_t, head_s)
    )
    copies[0].wait()
    for layer in range(3):
        fill_quad_weights(w_down_s, wq, layer, layer % 2 == 0)
    copies[1].wait()
    zero = jnp.zeros((64, 256), bf16)
    parent = di[0:64, :]
    child = di[64:128, :]
    di0[0:64, 0:256] = child
    di0[0:64, 256:512] = zero
    di0[64:128, 0:256] = zero
    di0[64:128, 256:512] = child
    di0[128:192, 0:256] = parent
    di0[128:192, 256:512] = parent
    di0[192:256, 0:256] = zero
    di0[192:256, 256:512] = zero
    copies[2].wait()
    back = do_s[...]
    do0[0:256, :] = dot_rows(back, lane_copies(1, 0)).astype(bf16)
    do0[256:512, :] = dot_rows(back, lane_copies(0, 1)).astype(bf16)
    do[...] = dot_rows(back, lane_copies(1, 1)).astype(bf16)
    copies[3].wait()
    output = lax.broadcasted_iota(jnp.int32, (4, 128), 0)
    lane = lax.broadcasted_iota(jnp.int32, (4, 128), 1)
    head = dot_rows(head_s[...], jnp.where(lane % 4 == output, 1.0, 0.0).astype(bf16))
    lane = lax.broadcasted_iota(jnp.int32, (64, 128), 1)
    for quad in range(8):
        for a in range(2):
            for b in range(2):
                base = quad * 256 + (a * 2 + b) * 64
                first = a * 64 + 4 * (2 * quad + b)
                kept = jnp.where((lane >= first) & (lane < first + 4), head, 0.0)
                wh[base : base + 64, :] = kept.astype(bf16)


def row_chunks(first, last, cols):
    step = max(1, 14 // cols)
    return [(i, min(i + step, last)) for i in range(first, last, step)]


def conv_block(src, dst, weights, row_range, col_range, to_odd, src_at=(0, 0), dst_at=(0, 0)):
    c0, c1 = col_range
    cols = c1 - c0
    for r0, r1 in row_chunks(*row_range, cols):
        rows = r1 - r0
        i, j = r0 - src_at[0], c0 - src_at[1]
        here = src[i : i + rows, j : j + cols]
        right = src[i : i + rows, j + 1 : j + 1 + cols]
        below = src[i + 1 : i + 1 + rows, j : j + cols]
        corner = src[i + 1 : i + 1 + rows, j + 1 : j + 1 + cols]
        stacked = jnp.concatenate([here, right, below, corner], axis=-1)
        update = dot(stacked.reshape(rows * cols * samples, 1024), weights[...])
        update = jnp.maximum(update, 0.0).reshape(rows, cols, samples, 256)
        low = low_half((rows, cols, samples, 128))
        if to_odd:
            old0 = jnp.where(low, corner[..., 0:128], below[..., 0:128])
            old1 = jnp.where(low, right[..., 128:256], here[..., 128:256])
        else:
            old0 = jnp.where(low, here[..., 0:128], right[..., 0:128])
            old1 = jnp.where(low, below[..., 128:256], corner[..., 128:256])
        new0 = (old0.astype(f32) + update[..., 0:128]).astype(bf16)
        new1 = (old1.astype(f32) + update[..., 128:256]).astype(bf16)
        i, j = r0 - dst_at[0], c0 - dst_at[1]
        dst[i : i + rows, j : j + cols, :, 0:128] = new0
        dst[i : i + rows, j : j + cols, :, 128:256] = new1


def spread_tiles(place, tiles, ext):
    row_even = place[0] % 2 == 0
    after_row = jnp.where(row_even, 16, 0)
    before_row = jnp.where(row_even, 0, 16)
    for tile, start in ((0, 8), (1, after_row), (2, before_row)):
        cells = tiles[tile].astype(f32)
        ext[pl.ds(start, 8), 1] = cells[:, 0:8]
        ext[pl.ds(start, 8), 2] = cells[:, 8:16]


def spread_sides(place, col_a, col_b, ext):
    row_even = place[0] % 2 == 0
    col_even = place[1] % 2 == 0
    after_row = jnp.where(row_even, 16, 0)
    before_row = jnp.where(row_even, 0, 16)
    after_col = jnp.where(col_even, 3, 0)
    before_col = jnp.where(col_even, 0, 3)
    for tile, start in ((0, 8), (1, after_row), (2, before_row)):
        ext[pl.ds(start, 8), after_col] = col_a[tile].astype(f32)
        ext[pl.ds(start, 8), before_col] = col_b[tile].astype(f32)


def embed_block(ext, we, dst, row_range, col_range, dst_at=(0, 0)):
    c0, c1 = col_range
    cols = c1 - c0
    sub = lax.broadcasted_iota(jnp.int32, (16, 128), 0)
    lane = lax.broadcasted_iota(jnp.int32, (16, 128), 1)
    own_lanes = (lane // 8 == sub).astype(f32)
    for r0, r1 in row_chunks(*row_range, cols):
        quads = []
        for i in range(r0, r1):
            for quad in range(c0, c1):
                parts = []
                for a in range(2):
                    row = 1 + 2 * i + (1 - a)
                    for b in range(2):
                        col = 1 + 2 * quad + (1 - b)
                        cell = ext[row, col // 8, col % 8 : col % 8 + 1, :]
                        halves = [
                            jnp.broadcast_to(cell[:, k : k + 128], (16, 128)) * own_lanes
                            for k in (0, 128)
                        ]
                        parts.append(jnp.concatenate(halves, axis=0).astype(bf16))
                quads.append(jnp.concatenate(parts, axis=-1))
        embedded = dot(jnp.concatenate(quads, axis=0), we[...]).astype(bf16)
        i, j = r0 - dst_at[0], c0 - dst_at[1]
        dst[i : i + r1 - r0, j : j + cols] = embedded.reshape(r1 - r0, cols, samples, 256)


def merge_block(src, dst, merge_in, mo, row_range, col_range):
    c0, c1 = col_range
    cols = c1 - c0
    for r0, r1 in row_chunks(*row_range, cols):
        stacked = src[r0:r1, c0:c1].reshape((r1 - r0) * cols * samples, 256)
        hidden = jnp.maximum(dot(stacked, merge_in[...]), 0.0).astype(bf16)
        merged = dot(hidden, mo[...]).astype(bf16)
        dst[r0:r1, c0:c1] = merged.reshape(r1 - r0, cols, samples, 128)


def blocks_ring(rows, cols):
    return [
        ((0, 2), (0, cols)),
        ((2, rows - 2), (0, 2)),
        ((2, rows - 2), (cols - 2, cols)),
        ((rows - 2, rows), (0, cols)),
    ]


def copy_rim(dst, inner, sides, rows, cols):
    for place, row in ((2, 0), (rows - 3, rows - 5)):
        dst[place, 2:4] = sides[0, row, 0:2]
        dst[place, 4 : cols - 4] = inner[row]
        dst[place, cols - 4 : cols - 2] = sides[1, row, 1:3]
    dst[3 : rows - 3, 2] = sides[0, 1 : rows - 5, 0]
    dst[3 : rows - 3, cols - 3] = sides[1, 1 : rows - 5, 2]


def merge_pair(top, bottom, merge_in, mo):
    count = top.shape[0]
    stacked = jnp.concatenate([top, bottom], axis=-1).reshape(count * samples, 256)
    hidden = jnp.maximum(dot(stacked, merge_in), 0.0).astype(bf16)
    return dot(hidden, mo).astype(bf16).reshape(count, samples, 128)


def paired_columns(cells):
    count = cells.shape[0] // 2
    split = cells.reshape(count, 2, samples, 128)
    low = low_half((count, samples, 128))
    return jnp.where(low, split[:, 0], split[:, 1])


def up_inner_body(place, tiles, wq, we, merge_in, mo, f0, f1, f2, f3, l1, ext):
    at = (2, 4)
    spread_tiles(place, tiles, ext)
    embed_block(ext, we, f0, (2, 9), (4, 11), at)
    conv_block(f0, f1, wq.at[0], (2, 8), (4, 10), False, at, at)
    conv_block(f1, f2, wq.at[1], (2, 7), (4, 9), True, at, at)
    conv_block(f2, f3, wq.at[2], (2, 6), (4, 8), False, at, at)
    merge_block(f3, l1, merge_in, mo, (0, 4), (0, 4))


def up_own_body(
    place,
    tiles,
    col_a,
    col_b,
    wq,
    we,
    merge_in,
    mo,
    i0,
    i1,
    i2,
    il1,
    s0,
    s1,
    s2,
    s3,
    l1,
    out,
    ext,
):
    spread_tiles(place, tiles, ext)
    spread_sides(place, col_a, col_b, ext)
    for ref, inner, rows, cols in ((s0, i0, 7, 7), (s1, i1, 6, 6), (s2, i2, 5, 5)):
        ref[0, :, 2] = inner[:, 0]
        ref[1, :, 0] = inner[:, cols - 1]
    left = (2, 4)
    for k, cols in ((0, left), (1, (11, 13))):
        embed_block(ext, we, s0.at[k], (2, 9), cols, (2, 2 if k == 0 else 10))
    for k, cols in ((0, left), (1, (10, 12))):
        src_at = (2, 2 if k == 0 else 10)
        dst_at = (2, 2 if k == 0 else 9)
        conv_block(s0.at[k], s1.at[k], wq.at[0], (2, 8), cols, False, src_at, dst_at)
    for k, cols in ((0, left), (1, (9, 11))):
        src_at = (2, 2 if k == 0 else 9)
        dst_at = (2, 2 if k == 0 else 8)
        conv_block(s1.at[k], s2.at[k], wq.at[1], (2, 7), cols, True, src_at, dst_at)
    for k, cols in ((0, left), (1, (8, 10))):
        src_at = (2, 2 if k == 0 else 8)
        conv_block(s2.at[k], s3.at[k], wq.at[2], (2, 6), cols, False, src_at, (2, cols[0]))
    merged = merge_pair(
        s3[..., 0:128].reshape(16, samples, 128),
        s3[..., 128:256].reshape(16, samples, 128),
        merge_in[...],
        mo[...],
    ).reshape(2, 4, 2, samples, 128)
    cells = jnp.concatenate([merged[0], il1[...], merged[1]], axis=1)
    l1[...] = cells
    top = jnp.concatenate([paired_columns(cells[0]), paired_columns(cells[2])], axis=0)
    bottom = jnp.concatenate([paired_columns(cells[1]), paired_columns(cells[3])], axis=0)
    l2 = merge_pair(top, bottom, merge_in[...], mo[...])
    l3 = merge_pair(paired_columns(l2[0:4]), paired_columns(l2[4:8]), merge_in[...], mo[...])
    out[...] = paired_columns(l3)[0]


def up_ring_first_body(place, tiles, col_a, col_b, wq, we, i0, s0, i1, s1, f1, ext, f0):
    spread_tiles(place, tiles, ext)
    spread_sides(place, col_a, col_b, ext)
    copy_rim(f0, i0, s0, 11, 15)
    for block in blocks_ring(11, 15):
        embed_block(ext, we, f0, *block)
    for block in blocks_ring(10, 14):
        conv_block(f0, f1, wq.at[0], *block, False)
    copy_rim(f1, i1, s1, 10, 14)


def up_ring_second_body(f1, wq, i2, s2, i3, s3, f3, f2):
    copy_rim(f2, i2, s2, 9, 13)
    for block in blocks_ring(9, 13):
        conv_block(f1, f2, wq.at[1], *block, True)
    for block in blocks_ring(8, 12):
        conv_block(f2, f3, wq.at[2], *block, False)
    f3[2:6, 4:8] = i3[...]
    f3[2:6, 2:4] = s3[0]
    f3[2:6, 8:10] = s3[1]


def up_ring_merge_body(f3, merge_in, mo, own1, l1, l2):
    for block in blocks_ring(8, 12):
        merge_block(f3, l1, merge_in, mo, *block)
    l1[2:6, 2:10] = own1[...]
    for i in (0, 2):
        top = jnp.concatenate([paired_columns(l1[2 * i]), paired_columns(l1[2 * i + 2])], axis=0)
        bottom = jnp.concatenate(
            [paired_columns(l1[2 * i + 1]), paired_columns(l1[2 * i + 3])], axis=0
        )
        l2[i : i + 2] = merge_pair(top, bottom, merge_in[...], mo[...]).reshape(2, 6, samples, 128)


def mid_body(place, z0, z1, z2, z3, merge_in, mo, a3, a4, p5, send1, send3, strip, l4s):
    row = place[0]
    col = place[1]
    deep = row // 4
    high = row % 4
    wide = col // 2
    core = col % 2
    for m, ref in enumerate((z0, z1, z2, z3)):
        for n in range(4):
            for k in range(2):
                strip[deep ^ m, high ^ n, core ^ k] = ref[n, k]
    cells = strip[...].reshape(8, 2, 2, samples, 128)
    l4 = merge_pair(
        cells[:, 0].reshape(16, samples, 128),
        cells[:, 1].reshape(16, samples, 128),
        merge_in[...],
        mo[...],
    )
    l4s[...] = l4.reshape(8, 2, samples, 128)
    pairs = paired_columns(l4).reshape(4, 2, samples, 128)
    l5 = merge_pair(pairs[:, 0], pairs[:, 1], merge_in[...], mo[...])
    packed = paired_columns(l5)
    p5[...] = packed
    low = low_half((samples, 128))
    wide_even = wide % 2 == 0
    for d in range(3):
        line = (row + d + (n_row - 1)) % n_row
        left = strip[line // 4, line % 4, 0]
        right = strip[line // 4, line % 4, 1]
        a3[d, 0] = left
        a3[d, 1] = right
        left4 = l4s[line // 2, 0]
        right4 = l4s[line // 2, 1]
        a4[d, 0] = left4
        a4[d, 1] = right4
        to_right = jnp.where(low, right4, right)
        to_left = jnp.where(low, left, left4)
        send1[d] = jnp.where(wide_even, to_right, to_left)
        send3[d] = jnp.where(wide_even, to_left, to_right)
    send1[3:5] = packed
    send3[3:5] = packed


def both_lanes(cells):
    wide = cells.astype(f32)
    turned = pltpu.roll(wide, 64, wide.ndim - 1)
    low = low_half(wide.shape)
    return jnp.where(low, wide, turned).astype(bf16), jnp.where(low, turned, wide).astype(bf16)


def refine(parent, child, down_in, do):
    count = parent.shape[0]
    low = low_half(parent.shape)
    joined = jnp.where(low, parent, child).reshape(count * samples, 128)
    inner = jnp.maximum(dot(joined, down_in), 0.0).astype(bf16)
    outcome = dot(inner, do).reshape(count, samples, 128)
    return (outcome + child.astype(f32) + parent.astype(f32)).astype(bf16)


def descent_body(
    place,
    slots,
    a3,
    a4,
    p5,
    q1,
    q2,
    q3,
    f3,
    l1,
    l2,
    merge_in,
    mo,
    down_in,
    do,
    di0,
    do0,
    wq,
    wh,
    out,
    l5s,
    c6s,
    c3s,
    p3s,
    c2s,
    n0,
    r1,
    r2,
    r3,
):
    row = place[0]
    col = place[1]
    wide = col // 2
    core = col % 2
    wide_even = wide % 2 == 0
    merge_weights = merge_in[...]
    back_weights = mo[...]
    in_weights = down_in[...]
    out_weights = do[...]

    for m, ref, start in ((0, p5, 0), (1, q1, 3), (2, q2, 0), (3, q3, 3)):
        for pair in range(2):
            first, second = both_lanes(ref[start + pair])
            l5s[wide ^ m, 2 * pair] = first
            l5s[wide ^ m, 2 * pair + 1] = second
    grid = l5s[...].reshape(2, 2, 2, 2, samples, 128)
    low4 = low_half((4, samples, 128))
    top = jnp.where(
        low4,
        grid[:, 0, :, 0].reshape(4, samples, 128),
        grid[:, 1, :, 0].reshape(4, samples, 128),
    )
    bottom = jnp.where(
        low4,
        grid[:, 0, :, 1].reshape(4, samples, 128),
        grid[:, 1, :, 1].reshape(4, samples, 128),
    )
    l6 = merge_pair(top, bottom, merge_weights, back_weights)
    low1 = low_half((1, samples, 128))
    l7 = merge_pair(
        jnp.where(low1, l6[0:1], l6[2:3]),
        jnp.where(low1, l6[1:2], l6[3:4]),
        merge_weights,
        back_weights,
    )
    c6s[...] = refine(
        jnp.broadcast_to(l7, (4, samples, 128)), l6, in_weights, out_weights
    ).reshape(2, 2, samples, 128)

    side = jnp.where(core == 0, (wide + 3) % 4, (wide + 1) % 4)
    lines = [(row + d + (n_row - 1)) % n_row for d in range(3)]
    parents5 = []
    children5 = []
    for place_x in (wide, side):
        for line in lines:
            deep = line // 4
            parents5.append(c6s[place_x // 2, deep // 2])
            children5.append(l5s[place_x, deep])
    c5 = refine(jnp.stack(parents5), jnp.stack(children5), in_weights, out_weights)

    from_first = jnp.logical_xor(wide_even, core == 0)
    side_cells = jnp.where(from_first, q1[0:3], q3[0:3])
    side_low, side_high = both_lanes(side_cells)
    side4 = jnp.where(core == 0, side_low, side_high)
    side3 = jnp.where(core == 0, side_high, side_low)
    own4 = a4[...]
    children4 = jnp.concatenate([own4[:, 0], own4[:, 1], side4], axis=0)
    parents4 = jnp.concatenate([c5[0:3], c5[0:3], c5[3:6]], axis=0)
    c4 = refine(parents4, children4, in_weights, out_weights)
    own3_0, own3_1 = both_lanes(a3[:, 0])
    own3_2, own3_3 = both_lanes(a3[:, 1])
    for k, cells in enumerate((side3, own3_0, own3_1, own3_2, own3_3, side3)):
        c3s[k] = cells
    for k, start in enumerate((6, 0, 0, 3, 3, 6)):
        p3s[k] = c4[start : start + 3]
    window = pl.ds(2 * core, 4)
    c3 = refine(
        p3s[window].reshape(12, samples, 128),
        c3s[window].reshape(12, samples, 128),
        in_weights,
        out_weights,
    ).reshape(4, 3, samples, 128)
    parents2 = jnp.stack([c3[j, i] for i in (0, 1, 1, 2) for j in (0, 1, 1, 2, 2, 3)])
    c2s[...] = refine(
        parents2, l2[...].reshape(24, samples, 128), in_weights, out_weights
    ).reshape(4, 6, samples, 128)

    sub = lax.broadcasted_iota(jnp.int32, (128, 128), 0)
    lane = lax.broadcasted_iota(jnp.int32, (128, 128), 1)
    averager = jnp.where((sub < 64) == (lane < 64), 1.0 / 64, 0.0).astype(bf16)

    low11 = low_half((11, samples, 128))
    for i in range(8):
        parent = c2s[i // 2]
        parent = jnp.broadcast_to(parent[:, None], (6, 2, samples, 128)).reshape(12, samples, 128)
        c1 = refine(parent, l1[i], in_weights, out_weights)
        c1_wide = c1.astype(f32).reshape(12 * samples, 128)
        for a in range(2):
            row_to = i - (1 - a)
            if not 0 <= row_to < 7:
                continue
            child = f3[i, :, :, a * 128 : a * 128 + 128]
            joined = jnp.concatenate([child, c1], axis=-1).reshape(12 * samples, 256)
            inner = jnp.maximum(dot(joined, di0[...]), 0.0).astype(bf16)
            fine = dot(inner, do0[...])
            fine = fine + child.astype(f32).reshape(12 * samples, 128) + c1_wide
            mean = dot((fine * fine).astype(bf16), averager)
            normed = (fine * lax.rsqrt(mean + norm_eps)).astype(bf16).reshape(12, samples, 128)
            n0[row_to, :, :, a * 128 : a * 128 + 128] = jnp.where(low11, normed[1:12], normed[0:11])
    conv_block(n0, r1, wq.at[0], (0, 6), (0, 10), False)
    conv_block(r1, r2, wq.at[1], (0, 5), (0, 9), True)
    conv_block(r2, r3, wq.at[2], (0, 4), (0, 8), False)
    stacked = jnp.concatenate(
        [r3[:, quad].reshape(4 * samples, 256) for quad in range(8)], axis=-1
    )
    cell_logits = dot(stacked, wh[...]).reshape(4, samples, 128)
    coarse = cell_logits.astype(bf16)
    rest = (cell_logits - coarse.astype(f32)).astype(bf16)
    places = lax.broadcasted_iota(jnp.int32, (128, 64), 0)
    for i in range(8):
        chosen = (places == slots[i : i + 1, :] + 64 * (i % 2)).astype(bf16)
        out[:, i, :] = dot(coarse[i // 2], chosen) + dot(rest[i // 2], chosen)


def swap(value, partner):
    pairs = []
    for r in range(n_row):
        for c in range(n_col):
            pr, pc = partner(r, c)
            pairs.append((r * n_col + c, pr * n_col + pc))
    return lax.ppermute(value, ("row", "col"), pairs)


def pair_after(i, count):
    return i ^ 1


def pair_before(i, count):
    return (((i - 1) % count ^ 1) + 1) % count


def on_device(
    readouts, w_embed, w_up, merge_in, merge_out, down_in, down_out, w_down, w_head, qubit_slot
):
    row = lax.axis_index("row")
    col = lax.axis_index("col")
    place = jnp.stack([row, col]).astype(jnp.int32)
    col_even = col % 2 == 0

    row_a = swap(readouts, lambda r, c: (pair_after(r, n_row), c))
    row_b = swap(readouts, lambda r, c: (pair_before(r, n_row), c))
    own, wq_up, we, mi, mo = whole_call(
        prep_up_body,
        (
            arr((8, 16, 256)),
            arr((3, 1024, 256)),
            arr((512, 256)),
            arr((256, 256)),
            arr((256, 128)),
        ),
        [
            pltpu.VMEM((3, 9, 64, 64), bf16),
            pltpu.VMEM((8, 64), bf16),
            pltpu.VMEM((64, 256), bf16),
            pltpu.SemaphoreType.DMA((5,)),
        ],
        (readouts, w_up, w_embed, merge_in, merge_out.T),
        outside=(0, 1, 2, 3, 4),
    )
    tiles = jnp.stack([own, row_a, row_b])
    left = tiles[:, :, 0:8]
    right = tiles[:, :, 8:16]
    col_a = swap(jnp.where(col_even, right, left), lambda r, c: (r, pair_after(c, n_col)))
    col_b = swap(jnp.where(col_even, left, right), lambda r, c: (r, pair_before(c, n_col)))
    wq_down, di, di0, do0, do, wh = whole_call(
        prep_down_body,
        (
            arr((3, 1024, 256)),
            arr((128, 256)),
            arr((256, 512)),
            arr((512, 128)),
            arr((256, 128)),
            arr((2048, 128)),
        ),
        [
            pltpu.VMEM((3, 9, 64, 64), bf16),
            pltpu.VMEM((64, 256), bf16),
            pltpu.VMEM((4, 64), bf16),
            pltpu.SemaphoreType.DMA((4,)),
        ],
        (w_down, down_in, down_out.T, w_head.T),
        outside=(0, 1, 2, 3),
    )

    quads = lambda rows, cols: pltpu.VMEM((rows, cols, samples, 256), bf16)
    ext = pltpu.VMEM((24, 4, 8, 256), f32)
    i0, i1, i2, i3, il1 = whole_call(
        up_inner_body,
        (
            arr((7, 7, samples, 256)),
            arr((6, 6, samples, 256)),
            arr((5, 5, samples, 256)),
            arr((4, 4, samples, 256)),
            arr((4, 4, samples, 128)),
        ),
        [ext],
        (place, tiles, wq_up, we, mi, mo),
        smem=(0,),
    )
    i0, col_a, col_b = lax.optimization_barrier((i0, col_a, col_b))
    s0, s1, s2, s3, own1, l3 = whole_call(
        up_own_body,
        (
            arr((2, 7, 3, samples, 256)),
            arr((2, 6, 3, samples, 256)),
            arr((2, 5, 3, samples, 256)),
            arr((2, 4, 2, samples, 256)),
            arr((4, 8, samples, 128)),
            arr((samples, 128)),
        ),
        [ext],
        (place, tiles, col_a, col_b, wq_up, we, mi, mo, i0, i1, i2, il1),
        smem=(0,),
    )

    pair = jnp.stack([l3, swap(l3, lambda r, c: (r, c ^ 1))])
    four = jnp.stack([pair] + [swap(pair, lambda r, c, m=m: (r ^ m, c)) for m in (1, 2, 3)])
    s0, pair = lax.optimization_barrier((s0, pair))
    f1 = whole_call(
        up_ring_first_body,
        arr((10, 14, samples, 256)),
        [ext, quads(11, 15)],
        (place, tiles, col_a, col_b, wq_up, we, i0, s0, i1, s1),
        smem=(0,),
    )
    four, f1 = lax.optimization_barrier((four, f1))
    strips = [four] + [swap(four, lambda r, c, m=m: (r ^ (4 * m), c)) for m in (1, 2, 3)]
    f3 = whole_call(
        up_ring_second_body,
        arr((8, 12, samples, 256)),
        [quads(9, 13)],
        (f1, wq_up, i2, s2, i3, s3),
    )
    strips[3], f3 = lax.optimization_barrier((strips[3], f3))
    a3, a4, p5, send1, send3 = whole_call(
        mid_body,
        (
            arr((3, 2, samples, 128)),
            arr((3, 2, samples, 128)),
            arr((2, samples, 128)),
            arr((5, samples, 128)),
            arr((5, samples, 128)),
        ),
        [pltpu.VMEM((4, 4, 2, samples, 128), bf16), pltpu.VMEM((8, 2, samples, 128), bf16)],
        (place, *strips, mi, mo),
        smem=(0,),
    )
    q1 = swap(send1, lambda r, c: (r, c ^ 2))
    q2 = swap(p5, lambda r, c: (r, c ^ 4))
    q3 = swap(send3, lambda r, c: (r, c ^ 6))
    l1, l2 = whole_call(
        up_ring_merge_body,
        (arr((8, 12, samples, 128)), arr((4, 6, samples, 128))),
        [],
        (f3, mi, mo, own1),
    )
    slots = qubit_slot.reshape(qubit_slot.shape[0], qubit_slot.shape[2])
    return whole_call(
        descent_body,
        arr((samples, 8, 64), f32),
        [
            pltpu.VMEM((4, 4, samples, 128), bf16),
            pltpu.VMEM((2, 2, samples, 128), bf16),
            pltpu.VMEM((6, 3, samples, 128), bf16),
            pltpu.VMEM((6, 3, samples, 128), bf16),
            pltpu.VMEM((4, 6, samples, 128), bf16),
            quads(7, 11),
            quads(6, 10),
            quads(5, 9),
            quads(4, 8),
        ],
        (
            place,
            slots,
            a3,
            a4,
            p5,
            q1,
            q2,
            q3,
            f3,
            l1,
            l2,
            mi,
            mo,
            di,
            do,
            di0,
            do0,
            wq_down,
            wh,
        ),
        smem=(0,),
    )


def solution(mesh):
    placed = (P("row", "col", None), P(), P(), P(), P(), P(), P(), P(), P(), P("row", "col", None))
    return jax.shard_map(
        on_device, mesh=mesh, in_specs=placed, out_specs=P(None, "row", "col"), check_vma=False
    )
```

```python
import functools

import jax
import jax.numpy as jnp
from jax import lax
from jax.experimental import pallas as pl
from jax.experimental.pallas import tpu as pltpu
from jax.sharding import PartitionSpec as P

norm_eps = 1e-05
bf16 = jnp.bfloat16
f32 = jnp.float32
n_row = 16
n_col = 8
samples = 32
vmem_bytes = 20 * 1024 * 1024
high_masks = (0, 3, 1, 2)
deep_masks = (0, 3, 1, 2)


def dot(left, right):
    return jnp.dot(left, right, preferred_element_type=f32)


def relu16(wide):
    return jnp.maximum(wide.astype(bf16), 0)


def low_half(shape):
    return lax.broadcasted_iota(jnp.int32, shape, len(shape) - 1) < 64


def whole_call(body, out_shapes, scratch, args, smem=(), outside=()):
    args = [
        pltpu.with_memory_space_constraint(x, pltpu.HBM) if i in outside else x
        for i, x in enumerate(args)
    ]
    specs = [
        pl.BlockSpec(
            memory_space=pltpu.SMEM if i in smem else pltpu.HBM if i in outside else pltpu.VMEM
        )
        for i in range(len(args))
    ]
    return pl.pallas_call(
        body,
        out_shape=out_shapes,
        in_specs=specs,
        out_specs=jax.tree.map(lambda _: pl.BlockSpec(memory_space=pltpu.VMEM), out_shapes),
        scratch_shapes=scratch,
        compiler_params=pltpu.CompilerParams(vmem_limit_bytes=vmem_bytes),
    )(*args)


def arr(shape, dtype=bf16):
    return jax.ShapeDtypeStruct(shape, dtype)


def fill_quad_weights(src, out, layer, from_odd):
    zero = jnp.zeros((64, 64), bf16)

    def tap_of(step, parity_in, parity_out):
        place_in = 1 - parity_in if from_odd else parity_in
        place_out = parity_out if from_odd else 1 - parity_out
        tap = 2 * step + place_in - place_out
        return tap if 0 <= tap <= 2 else None

    for di in range(2):
        for dj in range(2):
            for a in range(2):
                for b in range(2):
                    base = ((di * 2 + dj) * 4 + a * 2 + b) * 64
                    for oa in range(2):
                        tap_row = tap_of(di, a, oa)
                        blocks = []
                        for ob in range(2):
                            tap_col = tap_of(dj, b, ob)
                            if tap_row is None or tap_col is None:
                                blocks.append(zero)
                            else:
                                blocks.append(src[layer, 3 * tap_row + tap_col])
                        out[layer, base : base + 64, oa * 128 : oa * 128 + 128] = jnp.concatenate(
                            blocks, axis=1
                        )


def dot_rows(left, right):
    return lax.dot_general(left, right, (((0,), (0,)), ((), ())), preferred_element_type=f32)


def lane_copies(first, second):
    row = lax.broadcasted_iota(jnp.int32, (64, 128), 0)
    lane = lax.broadcasted_iota(jnp.int32, (64, 128), 1)
    kept = jnp.where(lane < 64, first, second) > 0
    return jnp.where(kept & (row == lane % 64), 1.0, 0.0).astype(bf16)


def copies_in(sems, *pairs):
    copies = [pltpu.make_async_copy(src, dst, sems.at[i]) for i, (src, dst) in enumerate(pairs)]
    for copy in copies:
        copy.start()
    return copies


def prep_body(
    own,
    w_up,
    w_embed,
    merge_in,
    merge_out_t,
    w_down,
    down_in,
    down_out_t,
    w_head_t,
    own_out,
    wq,
    we,
    mi,
    mo,
    wq_down,
    di,
    dc,
    dp,
    do0,
    do,
    wh,
    w_up_s,
    w_embed_s,
    mo_s,
    w_down_s,
    do_s,
    head_s,
    sems,
):
    copies = copies_in(
        sems,
        (w_up, w_up_s),
        (w_embed, w_embed_s),
        (merge_out_t, mo_s),
        (own, own_out),
        (merge_in, mi),
        (w_down, w_down_s),
        (down_in, di),
        (down_out_t, do_s),
        (w_head_t, head_s),
    )
    copies[0].wait()
    for layer in range(3):
        fill_quad_weights(w_up_s, wq, layer, layer % 2 == 0)
    copies[1].wait()
    tiled = jnp.concatenate([w_embed_s[...].astype(f32)] * 16, axis=0)
    none = jnp.zeros((128, 64), f32)
    for a in range(2):
        for b in range(2):
            q = 2 * a + b
            pair = [tiled, none] if b == 0 else [none, tiled]
            we[q * 128 : q * 128 + 128, a * 128 : a * 128 + 128] = jnp.concatenate(
                pair, axis=1
            ).astype(bf16)
            we[q * 128 : q * 128 + 128, (1 - a) * 128 : (1 - a) * 128 + 128] = jnp.zeros(
                (128, 128), bf16
            )
    copies[2].wait()
    mo[...] = dot_rows(mo_s[...], lane_copies(1, 1)).astype(bf16)
    copies[3].wait()
    copies[4].wait()
    copies[5].wait()
    for layer in range(3):
        fill_quad_weights(w_down_s, wq_down, layer, layer % 2 == 0)
    copies[6].wait()
    zero = jnp.zeros((64, 256), bf16)
    child = di[64:128, :]
    dc[0:64, 0:256] = child
    dc[0:64, 256:512] = zero
    dc[64:128, 0:256] = zero
    dc[64:128, 256:512] = child
    dp[0:64, :] = di[0:64, :]
    dp[64:128, :] = zero
    copies[7].wait()
    back = do_s[...]
    do0[0:256, :] = dot_rows(back, lane_copies(1, 0)).astype(bf16)
    do0[256:512, :] = dot_rows(back, lane_copies(0, 1)).astype(bf16)
    do[...] = dot_rows(back, lane_copies(1, 1)).astype(bf16)
    copies[8].wait()
    output = lax.broadcasted_iota(jnp.int32, (4, 128), 0)
    lane = lax.broadcasted_iota(jnp.int32, (4, 128), 1)
    head = dot_rows(head_s[...], jnp.where(lane % 4 == output, 1.0, 0.0).astype(bf16))
    lane = lax.broadcasted_iota(jnp.int32, (64, 128), 1)
    for quad in range(8):
        for a in range(2):
            for b in range(2):
                base = quad * 256 + (a * 2 + b) * 64
                first = a * 64 + 4 * (2 * quad + b)
                kept = jnp.where((lane >= first) & (lane < first + 4), head, 0.0)
                wh[base : base + 64, :] = kept.astype(bf16)


def row_chunks(first, last, cols):
    step = max(1, 14 // cols)
    return [(i, min(i + step, last)) for i in range(first, last, step)]


def conv_block(src, dst, weights, row_range, col_range, to_odd, src_at=(0, 0), dst_at=(0, 0)):
    c0, c1 = col_range
    cols = c1 - c0
    for r0, r1 in row_chunks(*row_range, cols):
        rows = r1 - r0
        i, j = r0 - src_at[0], c0 - src_at[1]
        here = src[i : i + rows, j : j + cols]
        right = src[i : i + rows, j + 1 : j + 1 + cols]
        below = src[i + 1 : i + 1 + rows, j : j + cols]
        corner = src[i + 1 : i + 1 + rows, j + 1 : j + 1 + cols]
        stacked = jnp.concatenate([here, right, below, corner], axis=-1)
        update = dot(stacked.reshape(rows * cols * samples, 1024), weights[...])
        update = jnp.maximum(update, 0.0).reshape(rows, cols, samples, 256)
        low = low_half((rows, cols, samples, 128))
        if to_odd:
            old0 = jnp.where(low, corner[..., 0:128], below[..., 0:128])
            old1 = jnp.where(low, right[..., 128:256], here[..., 128:256])
        else:
            old0 = jnp.where(low, here[..., 0:128], right[..., 0:128])
            old1 = jnp.where(low, below[..., 128:256], corner[..., 128:256])
        new0 = (old0.astype(f32) + update[..., 0:128]).astype(bf16)
        new1 = (old1.astype(f32) + update[..., 128:256]).astype(bf16)
        i, j = r0 - dst_at[0], c0 - dst_at[1]
        dst[i : i + rows, j : j + cols, :, 0:128] = new0
        dst[i : i + rows, j : j + cols, :, 128:256] = new1


def spread_tiles(place, tiles, ext):
    row_even = place[0] % 2 == 0
    after_row = jnp.where(row_even, 16, 0)
    before_row = jnp.where(row_even, 0, 16)
    for tile, start in ((0, 8), (1, before_row), (2, after_row)):
        cells = tiles[tile].astype(f32)
        ext[pl.ds(start, 8), 1] = cells[:, 0:8]
        ext[pl.ds(start, 8), 2] = cells[:, 8:16]


def spread_sides(place, col_a, col_b, ext):
    row_even = place[0] % 2 == 0
    col_even = place[1] % 2 == 0
    after_row = jnp.where(row_even, 16, 0)
    before_row = jnp.where(row_even, 0, 16)
    after_col = jnp.where(col_even, 3, 0)
    before_col = jnp.where(col_even, 0, 3)
    for tile, start in ((0, 8), (1, before_row), (2, after_row)):
        ext[pl.ds(start, 8), after_col] = col_a[tile].astype(f32)
        ext[pl.ds(start, 8), before_col] = col_b[tile].astype(f32)


def embed_block(ext, we, dst, row_range, col_range, dst_at=(0, 0)):
    c0, c1 = col_range
    cols = c1 - c0
    sub = lax.broadcasted_iota(jnp.int32, (16, 128), 0)
    lane = lax.broadcasted_iota(jnp.int32, (16, 128), 1)
    own_lanes = (lane // 8 == sub).astype(f32)
    for r0, r1 in row_chunks(*row_range, cols):
        quads = []
        for i in range(r0, r1):
            for quad in range(c0, c1):
                parts = []
                for a in range(2):
                    row = 1 + 2 * i + (1 - a)
                    for b in range(2):
                        col = 1 + 2 * quad + (1 - b)
                        cell = ext[row, col // 8, col % 8 : col % 8 + 1, :]
                        halves = [
                            jnp.broadcast_to(cell[:, k : k + 128], (16, 128)) * own_lanes
                            for k in (0, 128)
                        ]
                        parts.append(jnp.concatenate(halves, axis=0).astype(bf16))
                quads.append(jnp.concatenate(parts, axis=-1))
        embedded = dot(jnp.concatenate(quads, axis=0), we[...]).astype(bf16)
        i, j = r0 - dst_at[0], c0 - dst_at[1]
        dst[i : i + r1 - r0, j : j + cols] = embedded.reshape(r1 - r0, cols, samples, 256)


def merge_block(src, dst, merge_in, mo, row_range, col_range):
    c0, c1 = col_range
    cols = c1 - c0
    for r0, r1 in row_chunks(*row_range, cols):
        stacked = src[r0:r1, c0:c1].reshape((r1 - r0) * cols * samples, 256)
        hidden = relu16(dot(stacked, merge_in[...]))
        merged = dot(hidden, mo[...]).astype(bf16)
        dst[r0:r1, c0:c1] = merged.reshape(r1 - r0, cols, samples, 128)


def blocks_ring(rows, cols):
    return [
        ((0, 2), (0, cols)),
        ((2, rows - 2), (0, 2)),
        ((2, rows - 2), (cols - 2, cols)),
        ((rows - 2, rows), (0, cols)),
    ]


def copy_rim(dst, inner, sides, rows, cols):
    for place, row in ((2, 0), (rows - 3, rows - 5)):
        dst[place, 2:4] = sides[0, row, 0:2]
        dst[place, 4 : cols - 4] = inner[row]
        dst[place, cols - 4 : cols - 2] = sides[1, row, 1:3]
    dst[3 : rows - 3, 2] = sides[0, 1 : rows - 5, 0]
    dst[3 : rows - 3, cols - 3] = sides[1, 1 : rows - 5, 2]


def merge_pair(top, bottom, merge_in, mo):
    count = top.shape[0]
    stacked = jnp.concatenate([top, bottom], axis=-1).reshape(count * samples, 256)
    hidden = relu16(dot(stacked, merge_in))
    return dot(hidden, mo).astype(bf16).reshape(count, samples, 128)


def paired_columns(cells):
    count = cells.shape[0] // 2
    split = cells.reshape(count, 2, samples, 128)
    low = low_half((count, samples, 128))
    return jnp.where(low, split[:, 0], split[:, 1])


def up_inner_body(place, tiles, wq, we, merge_in, mo, f0, f1, f2, f3, l1, ext):
    at = (2, 4)
    spread_tiles(place, tiles, ext)
    embed_block(ext, we, f0, (2, 9), (4, 11), at)
    conv_block(f0, f1, wq.at[0], (2, 8), (4, 10), False, at, at)
    conv_block(f1, f2, wq.at[1], (2, 7), (4, 9), True, at, at)
    conv_block(f2, f3, wq.at[2], (2, 6), (4, 8), False, at, at)
    merge_block(f3, l1, merge_in, mo, (0, 4), (0, 4))


def up_own_body(
    place,
    tiles,
    col_b,
    col_a,
    wq,
    we,
    merge_in,
    mo,
    i0,
    i1,
    i2,
    il1,
    s0,
    s1,
    s2,
    s3,
    l1,
    out,
    ext,
):
    spread_tiles(place, tiles, ext)
    spread_sides(place, col_a, col_b, ext)
    for ref, inner, rows, cols in ((s0, i0, 7, 7), (s1, i1, 6, 6), (s2, i2, 5, 5)):
        ref[0, :, 2] = inner[:, 0]
        ref[1, :, 0] = inner[:, cols - 1]
    left = (2, 4)
    for k, cols in ((0, left), (1, (11, 13))):
        embed_block(ext, we, s0.at[k], (2, 9), cols, (2, 2 if k == 0 else 10))
    for k, cols in ((0, left), (1, (10, 12))):
        src_at = (2, 2 if k == 0 else 10)
        dst_at = (2, 2 if k == 0 else 9)
        conv_block(s0.at[k], s1.at[k], wq.at[0], (2, 8), cols, False, src_at, dst_at)
    for k, cols in ((0, left), (1, (9, 11))):
        src_at = (2, 2 if k == 0 else 9)
        dst_at = (2, 2 if k == 0 else 8)
        conv_block(s1.at[k], s2.at[k], wq.at[1], (2, 7), cols, True, src_at, dst_at)
    for k, cols in ((0, left), (1, (8, 10))):
        src_at = (2, 2 if k == 0 else 8)
        conv_block(s2.at[k], s3.at[k], wq.at[2], (2, 6), cols, False, src_at, (2, cols[0]))
    merged = merge_pair(
        s3[..., 0:128].reshape(16, samples, 128),
        s3[..., 128:256].reshape(16, samples, 128),
        merge_in[...],
        mo[...],
    ).reshape(2, 4, 2, samples, 128)
    cells = jnp.concatenate([merged[0], il1[...], merged[1]], axis=1)
    l1[...] = cells
    top = jnp.concatenate([paired_columns(cells[0]), paired_columns(cells[2])], axis=0)
    bottom = jnp.concatenate([paired_columns(cells[1]), paired_columns(cells[3])], axis=0)
    l2 = merge_pair(top, bottom, merge_in[...], mo[...])
    l3 = merge_pair(paired_columns(l2[0:4]), paired_columns(l2[4:8]), merge_in[...], mo[...])
    out[...] = paired_columns(l3)[0]


def up_ring_first_body(place, tiles, col_b, col_a, wq, we, i0, s0, i1, s1, f1, ext, f0):
    spread_tiles(place, tiles, ext)
    spread_sides(place, col_a, col_b, ext)
    copy_rim(f0, i0, s0, 11, 15)
    for block in blocks_ring(11, 15):
        embed_block(ext, we, f0, *block)
    for block in blocks_ring(10, 14):
        conv_block(f0, f1, wq.at[0], *block, False)
    copy_rim(f1, i1, s1, 10, 14)


def up_ring_second_body(f1, wq, i2, s2, i3, s3, f3, f2):
    copy_rim(f2, i2, s2, 9, 13)
    for block in blocks_ring(9, 13):
        conv_block(f1, f2, wq.at[1], *block, True)
    for block in blocks_ring(8, 12):
        conv_block(f2, f3, wq.at[2], *block, False)
    f3[2:6, 4:8] = i3[...]
    f3[2:6, 2:4] = s3[0]
    f3[2:6, 8:10] = s3[1]


def up_ring_merge_body(f3, merge_in, mo, own1, dc, l1, l2, child0, child1):
    for block in blocks_ring(8, 12):
        merge_block(f3, l1, merge_in, mo, *block)
    l1[2:6, 2:10] = own1[...]
    for i in (0, 2):
        top = jnp.concatenate([paired_columns(l1[2 * i]), paired_columns(l1[2 * i + 2])], axis=0)
        bottom = jnp.concatenate(
            [paired_columns(l1[2 * i + 1]), paired_columns(l1[2 * i + 3])], axis=0
        )
        l2[i : i + 2] = merge_pair(top, bottom, merge_in[...], mo[...]).reshape(2, 6, samples, 128)
    for i in range(8):
        for a in range(2):
            if 0 <= i - (1 - a) < 7:
                cells = f3[i, :, :, a * 128 : a * 128 + 128].reshape(12 * samples, 128)
                child0[i - (1 - a), a] = dot(cells, dc[...]).astype(bf16)
        child1[i] = dot(l1[i].reshape(12 * samples, 128), dc[:, 0:256]).astype(bf16)


def mid_body(place, z0, z1, z2, z3, merge_in, mo, a3, a4, p5, send1, send3, strip, l4s):
    row = place[0]
    col = place[1]
    deep = row // 4
    high = row % 4
    wide = col // 2
    core = col % 2
    for m, ref in zip(deep_masks, (z0, z1, z2, z3)):
        for n, mask in enumerate(high_masks):
            for k in range(2):
                strip[deep ^ m, high ^ mask, core ^ k] = ref[n, k]
    cells = strip[...].reshape(8, 2, 2, samples, 128)
    l4 = merge_pair(
        cells[:, 0].reshape(16, samples, 128),
        cells[:, 1].reshape(16, samples, 128),
        merge_in[...],
        mo[...],
    )
    l4s[...] = l4.reshape(8, 2, samples, 128)
    pairs = paired_columns(l4).reshape(4, 2, samples, 128)
    l5 = merge_pair(pairs[:, 0], pairs[:, 1], merge_in[...], mo[...])
    packed = paired_columns(l5)
    p5[...] = packed
    low = low_half((samples, 128))
    wide_even = wide % 2 == 0
    for d in range(3):
        line = (row + d + (n_row - 1)) % n_row
        left = strip[line // 4, line % 4, 0]
        right = strip[line // 4, line % 4, 1]
        a3[d, 0] = left
        a3[d, 1] = right
        left4 = l4s[line // 2, 0]
        right4 = l4s[line // 2, 1]
        a4[d, 0] = left4
        a4[d, 1] = right4
        to_right = jnp.where(low, right4, right)
        to_left = jnp.where(low, left, left4)
        send1[d] = jnp.where(wide_even, to_right, to_left)
        send3[d] = jnp.where(wide_even, to_left, to_right)
    send1[3:5] = packed
    send3[3:5] = packed


def both_lanes(cells):
    wide = cells.astype(f32)
    turned = pltpu.roll(wide, 64, wide.ndim - 1)
    low = low_half(wide.shape)
    return jnp.where(low, wide, turned).astype(bf16), jnp.where(low, turned, wide).astype(bf16)


def refine(parent, child, down_in, do):
    count = parent.shape[0]
    low = low_half(parent.shape)
    joined = jnp.where(low, parent, child).reshape(count * samples, 128)
    inner = relu16(dot(joined, down_in))
    outcome = dot(inner, do).reshape(count, samples, 128)
    return (outcome + child.astype(f32) + parent.astype(f32)).astype(bf16)


def descent_body(
    place,
    slots,
    a3,
    a4,
    p5,
    q1,
    q2,
    q3,
    f3,
    l1,
    l2,
    merge_in,
    mo,
    down_in,
    do,
    dp,
    do0,
    child0,
    child1,
    wq,
    wh,
    out,
    l5s,
    c6s,
    c3s,
    p3s,
    c2s,
    p2s,
    c1s,
    p1s,
    n0,
    r1,
    r2,
    r3,
):
    row = place[0]
    col = place[1]
    wide = col // 2
    core = col % 2
    wide_even = wide % 2 == 0
    merge_weights = merge_in[...]
    back_weights = mo[...]
    in_weights = down_in[...]
    out_weights = do[...]

    for m, ref, start in ((0, p5, 0), (1, q1, 3), (2, q2, 0), (3, q3, 3)):
        for pair in range(2):
            first, second = both_lanes(ref[start + pair])
            l5s[wide ^ m, 2 * pair] = first
            l5s[wide ^ m, 2 * pair + 1] = second
    grid = l5s[...].reshape(2, 2, 2, 2, samples, 128)
    low4 = low_half((4, samples, 128))
    top = jnp.where(
        low4,
        grid[:, 0, :, 0].reshape(4, samples, 128),
        grid[:, 1, :, 0].reshape(4, samples, 128),
    )
    bottom = jnp.where(
        low4,
        grid[:, 0, :, 1].reshape(4, samples, 128),
        grid[:, 1, :, 1].reshape(4, samples, 128),
    )
    l6 = merge_pair(top, bottom, merge_weights, back_weights)
    low1 = low_half((1, samples, 128))
    l7 = merge_pair(
        jnp.where(low1, l6[0:1], l6[2:3]),
        jnp.where(low1, l6[1:2], l6[3:4]),
        merge_weights,
        back_weights,
    )
    c6s[...] = refine(
        jnp.broadcast_to(l7, (4, samples, 128)), l6, in_weights, out_weights
    ).reshape(2, 2, samples, 128)

    side = jnp.where(core == 0, (wide + 3) % 4, (wide + 1) % 4)
    lines = [(row + d + (n_row - 1)) % n_row for d in range(3)]
    parents5 = []
    children5 = []
    for place_x in (wide, side):
        for line in lines:
            deep = line // 4
            parents5.append(c6s[place_x // 2, deep // 2])
            children5.append(l5s[place_x, deep])
    c5 = refine(jnp.stack(parents5), jnp.stack(children5), in_weights, out_weights)

    from_first = jnp.logical_xor(wide_even, core == 0)
    side_cells = jnp.where(from_first, q1[0:3], q3[0:3])
    side_low, side_high = both_lanes(side_cells)
    side4 = jnp.where(core == 0, side_low, side_high)
    side3 = jnp.where(core == 0, side_high, side_low)
    own4 = a4[...]
    children4 = jnp.concatenate([own4[:, 0], own4[:, 1], side4], axis=0)
    parents4 = jnp.concatenate([c5[0:3], c5[0:3], c5[3:6]], axis=0)
    c4 = refine(parents4, children4, in_weights, out_weights)
    own3_0, own3_1 = both_lanes(a3[:, 0])
    own3_2, own3_3 = both_lanes(a3[:, 1])
    for k, cells in enumerate((side3, own3_0, own3_1, own3_2, own3_3, side3)):
        c3s[k] = cells
    for k, start in enumerate((6, 0, 0, 3, 3, 6)):
        p3s[k] = c4[start : start + 3]
    window = pl.ds(2 * core, 4)
    c3 = refine(
        p3s[window].reshape(12, samples, 128),
        c3s[window].reshape(12, samples, 128),
        in_weights,
        out_weights,
    ).reshape(4, 3, samples, 128)
    parents2 = jnp.stack([c3[j, i] for i in (0, 1, 1, 2) for j in (0, 1, 1, 2, 2, 3)])
    c2s[...] = refine(
        parents2, l2[...].reshape(24, samples, 128), in_weights, out_weights
    ).reshape(4, 6, samples, 128)

    rows = 12 * samples
    low11 = low_half((11, samples, 128))
    sub = lax.broadcasted_iota(jnp.int32, (256, 256), 0)
    lane = lax.broadcasted_iota(jnp.int32, (256, 256), 1)
    averager = jnp.where(sub // 64 == lane // 64, 1.0 / 64, 0.0).astype(bf16)
    for i in range(4):
        p2s[i] = dot(c2s[i].reshape(6 * samples, 128), dp[...]).reshape(6, samples, 256)
    for i in range(8):
        parent = c2s[i // 2].astype(f32)[:, None]
        parent = jnp.broadcast_to(parent, (6, 2, samples, 128)).reshape(rows, 128)
        part = jnp.broadcast_to(p2s[i // 2][:, None], (6, 2, samples, 256)).reshape(rows, 256)
        inner = relu16(child1[i].astype(f32) + part)
        c1 = dot(inner, out_weights) + l1[i].astype(f32).reshape(rows, 128) + parent
        c1s[i] = c1.astype(bf16)
    for i in range(8):
        p1s[i] = dot(c1s[i], dp[...])
    for i in range(8):
        part = p1s[i]
        part = jnp.concatenate([part, part], axis=-1)
        context = c1s[i].astype(f32)
        halves = [a for a in range(2) if 0 <= i - (1 - a) < 7]
        fine = []
        for a in halves:
            inner = relu16(child0[i - (1 - a), a].astype(f32) + part)
            child = f3[i, :, :, a * 128 : a * 128 + 128].astype(f32).reshape(rows, 128)
            fine.append(dot(inner, do0[...]) + child + context)
        fine = jnp.concatenate(fine, axis=-1)
        width = fine.shape[-1]
        mean = dot((fine * fine).astype(bf16), averager[:width, :width])
        normed = (fine * lax.rsqrt(mean + norm_eps)).astype(bf16).reshape(12, samples, width)
        for k, a in enumerate(halves):
            part16 = normed[..., k * 128 : k * 128 + 128]
            n0[i - (1 - a), :, :, a * 128 : a * 128 + 128] = jnp.where(
                low11, part16[1:12], part16[0:11]
            )
    conv_block(n0, r1, wq.at[0], (0, 6), (0, 10), False)
    conv_block(r1, r2, wq.at[1], (0, 5), (0, 9), True)
    conv_block(r2, r3, wq.at[2], (0, 4), (0, 8), False)
    stacked = jnp.concatenate(
        [r3[:, quad].reshape(4 * samples, 256) for quad in range(8)], axis=-1
    )
    cell_logits = dot(stacked, wh[...]).reshape(4, samples, 128)
    coarse = cell_logits.astype(bf16)
    rest = (cell_logits - coarse.astype(f32)).astype(bf16)
    places = lax.broadcasted_iota(jnp.int32, (128, 64), 0)
    for i in range(8):
        chosen = (places == slots[i : i + 1, :] + 64 * (i % 2)).astype(bf16)
        out[:, i, :] = dot(coarse[i // 2], chosen) + dot(rest[i // 2], chosen)


def swap(value, partner):
    pairs = []
    for r in range(n_row):
        for c in range(n_col):
            pr, pc = partner(r, c)
            pairs.append((r * n_col + c, pr * n_col + pc))
    return lax.ppermute(value, ("row", "col"), pairs)


def pair_after(i, count):
    return i ^ 1


def pair_before(i, count):
    return (((i - 1) % count ^ 1) + 1) % count


def on_device(
    readouts, w_embed, w_up, merge_in, merge_out, down_in, down_out, w_down, w_head, qubit_slot
):
    row = lax.axis_index("row")
    col = lax.axis_index("col")
    place = jnp.stack([row, col]).astype(jnp.int32)
    col_even = col % 2 == 0

    row_a = swap(readouts, lambda r, c: (pair_after(r, n_row), c))
    row_b = swap(readouts, lambda r, c: (pair_before(r, n_row), c))
    own, wq_up, we, mi, mo, wq_down, di, dc, dp, do0, do, wh = whole_call(
        prep_body,
        (
            arr((8, 16, 256)),
            arr((3, 1024, 256)),
            arr((512, 256)),
            arr((256, 256)),
            arr((256, 128)),
            arr((3, 1024, 256)),
            arr((128, 256)),
            arr((128, 512)),
            arr((128, 256)),
            arr((512, 128)),
            arr((256, 128)),
            arr((2048, 128)),
        ),
        [
            pltpu.VMEM((3, 9, 64, 64), bf16),
            pltpu.VMEM((8, 64), bf16),
            pltpu.VMEM((64, 256), bf16),
            pltpu.VMEM((3, 9, 64, 64), bf16),
            pltpu.VMEM((64, 256), bf16),
            pltpu.VMEM((4, 64), bf16),
            pltpu.SemaphoreType.DMA((9,)),
        ],
        (
            readouts,
            w_up,
            w_embed,
            merge_in,
            merge_out.T,
            w_down,
            down_in,
            down_out.T,
            w_head.T,
        ),
        outside=tuple(range(9)),
    )
    tiles = jnp.stack([own, row_b, row_a])
    left = tiles[:, :, 0:8]
    right = tiles[:, :, 8:16]
    col_a = swap(jnp.where(col_even, right, left), lambda r, c: (r, pair_after(c, n_col)))
    col_b = swap(jnp.where(col_even, left, right), lambda r, c: (r, pair_before(c, n_col)))
    quads = lambda rows, cols: pltpu.VMEM((rows, cols, samples, 256), bf16)
    ext = pltpu.VMEM((24, 4, 8, 256), f32)
    i0, i1, i2, i3, il1 = whole_call(
        up_inner_body,
        (
            arr((7, 7, samples, 256)),
            arr((6, 6, samples, 256)),
            arr((5, 5, samples, 256)),
            arr((4, 4, samples, 256)),
            arr((4, 4, samples, 128)),
        ),
        [ext],
        (place, tiles, wq_up, we, mi, mo),
        smem=(0,),
    )
    i0, col_b, col_a = lax.optimization_barrier((i0, col_b, col_a))
    s0, s1, s2, s3, own1, l3 = whole_call(
        up_own_body,
        (
            arr((2, 7, 3, samples, 256)),
            arr((2, 6, 3, samples, 256)),
            arr((2, 5, 3, samples, 256)),
            arr((2, 4, 2, samples, 256)),
            arr((4, 8, samples, 128)),
            arr((samples, 128)),
        ),
        [ext],
        (place, tiles, col_b, col_a, wq_up, we, mi, mo, i0, i1, i2, il1),
        smem=(0,),
    )

    pair = jnp.stack([l3, swap(l3, lambda r, c: (r, c ^ 1))])
    four = jnp.stack([pair] + [swap(pair, lambda r, c, m=m: (r ^ m, c)) for m in high_masks[1:]])
    s0, pair = lax.optimization_barrier((s0, pair))
    f1 = whole_call(
        up_ring_first_body,
        arr((10, 14, samples, 256)),
        [ext, quads(11, 15)],
        (place, tiles, col_b, col_a, wq_up, we, i0, s0, i1, s1),
        smem=(0,),
    )
    four, f1 = lax.optimization_barrier((four, f1))
    strips = [four] + [swap(four, lambda r, c, m=m: (r ^ (4 * m), c)) for m in deep_masks[1:]]
    f3 = whole_call(
        up_ring_second_body,
        arr((8, 12, samples, 256)),
        [quads(9, 13)],
        (f1, wq_up, i2, s2, i3, s3),
    )
    strips[3], f3 = lax.optimization_barrier((strips[3], f3))
    a3, a4, p5, send1, send3 = whole_call(
        mid_body,
        (
            arr((3, 2, samples, 128)),
            arr((3, 2, samples, 128)),
            arr((2, samples, 128)),
            arr((5, samples, 128)),
            arr((5, samples, 128)),
        ),
        [pltpu.VMEM((4, 4, 2, samples, 128), bf16), pltpu.VMEM((8, 2, samples, 128), bf16)],
        (place, *strips, mi, mo),
        smem=(0,),
    )
    q1 = swap(send1, lambda r, c: (r, c ^ 2))
    q2 = swap(p5, lambda r, c: (r, c ^ 4))
    q3 = swap(send3, lambda r, c: (r, c ^ 6))
    l1, l2, child0, child1 = whole_call(
        up_ring_merge_body,
        (
            arr((8, 12, samples, 128)),
            arr((4, 6, samples, 128)),
            arr((7, 2, 12 * samples, 512)),
            arr((8, 12 * samples, 256)),
        ),
        [],
        (f3, mi, mo, own1, dc),
    )
    slots = qubit_slot.reshape(qubit_slot.shape[0], qubit_slot.shape[2])
    return whole_call(
        descent_body,
        arr((samples, 8, 64), f32),
        [
            pltpu.VMEM((4, 4, samples, 128), bf16),
            pltpu.VMEM((2, 2, samples, 128), bf16),
            pltpu.VMEM((6, 3, samples, 128), bf16),
            pltpu.VMEM((6, 3, samples, 128), bf16),
            pltpu.VMEM((4, 6, samples, 128), bf16),
            pltpu.VMEM((4, 6, samples, 256), f32),
            pltpu.VMEM((8, 12 * samples, 128), bf16),
            pltpu.VMEM((8, 12 * samples, 256), f32),
            quads(7, 11),
            quads(6, 10),
            quads(5, 9),
            quads(4, 8),
        ],
        (
            place,
            slots,
            a3,
            a4,
            p5,
            q1,
            q2,
            q3,
            f3,
            l1,
            l2,
            mi,
            mo,
            di,
            do,
            dp,
            do0,
            child0,
            child1,
            wq_down,
            wh,
        ),
        smem=(0,),
    )


def solution(mesh):
    placed = (P("row", "col", None), P(), P(), P(), P(), P(), P(), P(), P(), P("row", "col", None))
    return jax.shard_map(
        on_device, mesh=mesh, in_specs=placed, out_specs=P(None, "row", "col"), check_vma=False
    )
```

```python
import functools

import jax
import jax.numpy as jnp
from jax import lax
from jax.experimental import pallas as pl
from jax.experimental.pallas import tpu as pltpu
from jax.sharding import PartitionSpec as P

norm_eps = 1e-05
bf16 = jnp.bfloat16
f32 = jnp.float32
n_row = 16
n_col = 8
samples = 32
vmem_bytes = 20 * 1024 * 1024
high_masks = (0, 2, 3, 1)
deep_masks = (0, 3, 1, 2)


def dot(left, right):
    return jnp.dot(left, right, preferred_element_type=f32)


def relu16(wide):
    return jnp.maximum(wide.astype(bf16), 0)


def low_half(shape):
    return lax.broadcasted_iota(jnp.int32, shape, len(shape) - 1) < 64


def whole_call(body, out_shapes, scratch, args, smem=(), outside=()):
    args = [
        pltpu.with_memory_space_constraint(x, pltpu.HBM) if i in outside else x
        for i, x in enumerate(args)
    ]
    specs = [
        pl.BlockSpec(
            memory_space=pltpu.SMEM if i in smem else pltpu.HBM if i in outside else pltpu.VMEM
        )
        for i in range(len(args))
    ]
    return pl.pallas_call(
        body,
        out_shape=out_shapes,
        in_specs=specs,
        out_specs=jax.tree.map(lambda _: pl.BlockSpec(memory_space=pltpu.VMEM), out_shapes),
        scratch_shapes=scratch,
        compiler_params=pltpu.CompilerParams(vmem_limit_bytes=vmem_bytes),
    )(*args)


def arr(shape, dtype=bf16):
    return jax.ShapeDtypeStruct(shape, dtype)


def fill_quad_weights(src, out, layer, from_odd):
    zero = jnp.zeros((64, 64), bf16)

    def tap_of(step, parity_in, parity_out):
        place_in = 1 - parity_in if from_odd else parity_in
        place_out = parity_out if from_odd else 1 - parity_out
        tap = 2 * step + place_in - place_out
        return tap if 0 <= tap <= 2 else None

    for di in range(2):
        for dj in range(2):
            for a in range(2):
                for b in range(2):
                    base = ((di * 2 + dj) * 4 + a * 2 + b) * 64
                    for oa in range(2):
                        tap_row = tap_of(di, a, oa)
                        blocks = []
                        for ob in range(2):
                            tap_col = tap_of(dj, b, ob)
                            if tap_row is None or tap_col is None:
                                blocks.append(zero)
                            else:
                                blocks.append(src[layer, 3 * tap_row + tap_col])
                        out[layer, base : base + 64, oa * 128 : oa * 128 + 128] = jnp.concatenate(
                            blocks, axis=1
                        )


def dot_rows(left, right):
    return lax.dot_general(left, right, (((0,), (0,)), ((), ())), preferred_element_type=f32)


def lane_copies(first, second):
    row = lax.broadcasted_iota(jnp.int32, (64, 128), 0)
    lane = lax.broadcasted_iota(jnp.int32, (64, 128), 1)
    kept = jnp.where(lane < 64, first, second) > 0
    return jnp.where(kept & (row == lane % 64), 1.0, 0.0).astype(bf16)


def copies_in(sems, *pairs):
    copies = [pltpu.make_async_copy(src, dst, sems.at[i]) for i, (src, dst) in enumerate(pairs)]
    for copy in copies:
        copy.start()
    return copies


def prep_body(
    own,
    w_up,
    w_embed,
    merge_in,
    merge_out_t,
    w_down,
    down_in,
    down_out_t,
    w_head_t,
    own_out,
    wq,
    we,
    mi,
    mo,
    wq_down,
    di,
    dc,
    dp,
    do0,
    do,
    wh,
    w2,
    w7,
    w_up_s,
    w_embed_s,
    mo_s,
    w_down_s,
    do_s,
    head_s,
    sems,
):
    copies = copies_in(
        sems,
        (w_up, w_up_s),
        (w_embed, w_embed_s),
        (merge_out_t, mo_s),
        (own, own_out),
        (merge_in, mi),
        (w_down, w_down_s),
        (down_in, di),
        (down_out_t, do_s),
        (w_head_t, head_s),
    )
    copies[0].wait()
    for layer in range(3):
        fill_quad_weights(w_up_s, wq, layer, layer % 2 == 0)
    copies[1].wait()
    tiled = jnp.concatenate([w_embed_s[...].astype(f32)] * 16, axis=0)
    none = jnp.zeros((128, 64), f32)
    for a in range(2):
        for b in range(2):
            q = 2 * a + b
            pair = [tiled, none] if b == 0 else [none, tiled]
            we[q * 128 : q * 128 + 128, a * 128 : a * 128 + 128] = jnp.concatenate(
                pair, axis=1
            ).astype(bf16)
            we[q * 128 : q * 128 + 128, (1 - a) * 128 : (1 - a) * 128 + 128] = jnp.zeros(
                (128, 128), bf16
            )
    copies[2].wait()
    mo[...] = dot_rows(mo_s[...], lane_copies(1, 1)).astype(bf16)
    copies[3].wait()
    copies[4].wait()
    copies[5].wait()
    for layer in range(3):
        fill_quad_weights(w_down_s, wq_down, layer, layer % 2 == 0)
    copies[6].wait()
    zero = jnp.zeros((64, 256), bf16)
    child = di[64:128, :]
    dc[0:64, 0:256] = child
    dc[0:64, 256:512] = zero
    dc[64:128, 0:256] = zero
    dc[64:128, 256:512] = child
    dp[0:64, :] = di[0:64, :]
    dp[64:128, :] = zero
    copies[7].wait()
    back = do_s[...]
    do0[0:256, :] = dot_rows(back, lane_copies(1, 0)).astype(bf16)
    do0[256:512, :] = dot_rows(back, lane_copies(0, 1)).astype(bf16)
    do[...] = dot_rows(back, lane_copies(1, 1)).astype(bf16)
    w2[0:128, :] = dp[...]
    w2[128:384, :] = dot(do[...], dp[...]).astype(bf16)
    w7[...] = dot(mo[...], dp[...]).astype(bf16)
    copies[8].wait()
    output = lax.broadcasted_iota(jnp.int32, (4, 128), 0)
    lane = lax.broadcasted_iota(jnp.int32, (4, 128), 1)
    head = dot_rows(head_s[...], jnp.where(lane % 4 == output, 1.0, 0.0).astype(bf16))
    lane = lax.broadcasted_iota(jnp.int32, (64, 128), 1)
    for quad in range(8):
        for a in range(2):
            for b in range(2):
                base = quad * 256 + (a * 2 + b) * 64
                first = a * 64 + 4 * (2 * quad + b)
                kept = jnp.where((lane >= first) & (lane < first + 4), head, 0.0)
                wh[base : base + 64, :] = kept.astype(bf16)


def row_chunks(first, last, cols):
    step = max(1, 14 // cols)
    return [(i, min(i + step, last)) for i in range(first, last, step)]


def conv_block(src, dst, weights, row_range, col_range, to_odd, src_at=(0, 0), dst_at=(0, 0)):
    c0, c1 = col_range
    cols = c1 - c0
    for r0, r1 in row_chunks(*row_range, cols):
        rows = r1 - r0
        i, j = r0 - src_at[0], c0 - src_at[1]
        here = src[i : i + rows, j : j + cols]
        right = src[i : i + rows, j + 1 : j + 1 + cols]
        below = src[i + 1 : i + 1 + rows, j : j + cols]
        corner = src[i + 1 : i + 1 + rows, j + 1 : j + 1 + cols]
        stacked = jnp.concatenate([here, right, below, corner], axis=-1)
        update = dot(stacked.reshape(rows * cols * samples, 1024), weights[...])
        update = jnp.maximum(update, 0.0).reshape(rows, cols, samples, 256)
        low = low_half((rows, cols, samples, 128))
        if to_odd:
            old0 = jnp.where(low, corner[..., 0:128], below[..., 0:128])
            old1 = jnp.where(low, right[..., 128:256], here[..., 128:256])
        else:
            old0 = jnp.where(low, here[..., 0:128], right[..., 0:128])
            old1 = jnp.where(low, below[..., 128:256], corner[..., 128:256])
        new0 = (old0.astype(f32) + update[..., 0:128]).astype(bf16)
        new1 = (old1.astype(f32) + update[..., 128:256]).astype(bf16)
        i, j = r0 - dst_at[0], c0 - dst_at[1]
        dst[i : i + rows, j : j + cols, :, 0:128] = new0
        dst[i : i + rows, j : j + cols, :, 128:256] = new1


def spread_tiles(place, tiles, ext):
    row_even = place[0] % 2 == 0
    after_row = jnp.where(row_even, 16, 0)
    before_row = jnp.where(row_even, 0, 16)
    for tile, start in ((0, 8), (1, before_row), (2, after_row)):
        cells = tiles[tile].astype(f32)
        ext[pl.ds(start, 8), 1] = cells[:, 0:8]
        ext[pl.ds(start, 8), 2] = cells[:, 8:16]


def spread_sides(place, col_a, col_b, ext):
    row_even = place[0] % 2 == 0
    col_even = place[1] % 2 == 0
    after_row = jnp.where(row_even, 16, 0)
    before_row = jnp.where(row_even, 0, 16)
    after_col = jnp.where(col_even, 3, 0)
    before_col = jnp.where(col_even, 0, 3)
    for tile, start in ((0, 8), (1, before_row), (2, after_row)):
        ext[pl.ds(start, 8), after_col] = col_a[tile].astype(f32)
        ext[pl.ds(start, 8), before_col] = col_b[tile].astype(f32)


def embed_block(ext, we, dst, row_range, col_range, dst_at=(0, 0)):
    c0, c1 = col_range
    cols = c1 - c0
    sub = lax.broadcasted_iota(jnp.int32, (16, 128), 0)
    lane = lax.broadcasted_iota(jnp.int32, (16, 128), 1)
    own_lanes = (lane // 8 == sub).astype(f32)
    for r0, r1 in row_chunks(*row_range, cols):
        quads = []
        for i in range(r0, r1):
            for quad in range(c0, c1):
                parts = []
                for a in range(2):
                    row = 1 + 2 * i + (1 - a)
                    for b in range(2):
                        col = 1 + 2 * quad + (1 - b)
                        cell = ext[row, col // 8, col % 8 : col % 8 + 1, :]
                        halves = [
                            jnp.broadcast_to(cell[:, k : k + 128], (16, 128)) * own_lanes
                            for k in (0, 128)
                        ]
                        parts.append(jnp.concatenate(halves, axis=0).astype(bf16))
                quads.append(jnp.concatenate(parts, axis=-1))
        embedded = dot(jnp.concatenate(quads, axis=0), we[...]).astype(bf16)
        i, j = r0 - dst_at[0], c0 - dst_at[1]
        dst[i : i + r1 - r0, j : j + cols] = embedded.reshape(r1 - r0, cols, samples, 256)


def merge_block(src, dst, merge_in, mo, row_range, col_range):
    c0, c1 = col_range
    cols = c1 - c0
    for r0, r1 in row_chunks(*row_range, cols):
        stacked = src[r0:r1, c0:c1].reshape((r1 - r0) * cols * samples, 256)
        hidden = relu16(dot(stacked, merge_in[...]))
        merged = dot(hidden, mo[...]).astype(bf16)
        dst[r0:r1, c0:c1] = merged.reshape(r1 - r0, cols, samples, 128)


def blocks_ring(rows, cols):
    return [
        ((0, 2), (0, cols)),
        ((2, rows - 2), (0, 2)),
        ((2, rows - 2), (cols - 2, cols)),
        ((rows - 2, rows), (0, cols)),
    ]


def copy_rim(dst, inner, sides, rows, cols):
    for place, row in ((2, 0), (rows - 3, rows - 5)):
        dst[place, 2:4] = sides[0, row, 0:2]
        dst[place, 4 : cols - 4] = inner[row]
        dst[place, cols - 4 : cols - 2] = sides[1, row, 1:3]
    dst[3 : rows - 3, 2] = sides[0, 1 : rows - 5, 0]
    dst[3 : rows - 3, cols - 3] = sides[1, 1 : rows - 5, 2]


def merge_pair(top, bottom, merge_in, mo):
    count = top.shape[0]
    stacked = jnp.concatenate([top, bottom], axis=-1).reshape(count * samples, 256)
    hidden = relu16(dot(stacked, merge_in))
    return dot(hidden, mo).astype(bf16).reshape(count, samples, 128)


def paired_columns(cells):
    count = cells.shape[0] // 2
    split = cells.reshape(count, 2, samples, 128)
    low = low_half((count, samples, 128))
    return jnp.where(low, split[:, 0], split[:, 1])


def up_inner_body(place, tiles, wq, we, merge_in, mo, f0, f1, f2, f3, l1, ext):
    at = (2, 4)
    spread_tiles(place, tiles, ext)
    embed_block(ext, we, f0, (2, 9), (4, 11), at)
    conv_block(f0, f1, wq.at[0], (2, 8), (4, 10), False, at, at)
    conv_block(f1, f2, wq.at[1], (2, 7), (4, 9), True, at, at)
    conv_block(f2, f3, wq.at[2], (2, 6), (4, 8), False, at, at)
    merge_block(f3, l1, merge_in, mo, (0, 4), (0, 4))


def up_own_body(
    place,
    tiles,
    col_b,
    col_a,
    wq,
    we,
    merge_in,
    mo,
    i0,
    i1,
    i2,
    il1,
    s0,
    s1,
    s2,
    s3,
    l1,
    out,
    ext,
):
    spread_tiles(place, tiles, ext)
    spread_sides(place, col_a, col_b, ext)
    for ref, inner, rows, cols in ((s0, i0, 7, 7), (s1, i1, 6, 6), (s2, i2, 5, 5)):
        ref[0, :, 2] = inner[:, 0]
        ref[1, :, 0] = inner[:, cols - 1]
    left = (2, 4)
    for k, cols in ((0, left), (1, (11, 13))):
        embed_block(ext, we, s0.at[k], (2, 9), cols, (2, 2 if k == 0 else 10))
    for k, cols in ((0, left), (1, (10, 12))):
        src_at = (2, 2 if k == 0 else 10)
        dst_at = (2, 2 if k == 0 else 9)
        conv_block(s0.at[k], s1.at[k], wq.at[0], (2, 8), cols, False, src_at, dst_at)
    for k, cols in ((0, left), (1, (9, 11))):
        src_at = (2, 2 if k == 0 else 9)
        dst_at = (2, 2 if k == 0 else 8)
        conv_block(s1.at[k], s2.at[k], wq.at[1], (2, 7), cols, True, src_at, dst_at)
    for k, cols in ((0, left), (1, (8, 10))):
        src_at = (2, 2 if k == 0 else 8)
        conv_block(s2.at[k], s3.at[k], wq.at[2], (2, 6), cols, False, src_at, (2, cols[0]))
    merged = merge_pair(
        s3[..., 0:128].reshape(16, samples, 128),
        s3[..., 128:256].reshape(16, samples, 128),
        merge_in[...],
        mo[...],
    ).reshape(2, 4, 2, samples, 128)
    cells = jnp.concatenate([merged[0], il1[...], merged[1]], axis=1)
    l1[...] = cells
    top = jnp.concatenate([paired_columns(cells[0]), paired_columns(cells[2])], axis=0)
    bottom = jnp.concatenate([paired_columns(cells[1]), paired_columns(cells[3])], axis=0)
    l2 = merge_pair(top, bottom, merge_in[...], mo[...])
    l3 = merge_pair(paired_columns(l2[0:4]), paired_columns(l2[4:8]), merge_in[...], mo[...])
    out[...] = paired_columns(l3)[0]


def up_ring_embed_body(ext, we, i0, s0, f0):
    copy_rim(f0, i0, s0, 11, 15)
    for block in blocks_ring(11, 15):
        embed_block(ext, we, f0, *block)


def up_ring_first_body(f0, wq, i1, s1, f1):
    for block in blocks_ring(10, 14):
        conv_block(f0, f1, wq.at[0], *block, False)
    copy_rim(f1, i1, s1, 10, 14)


def up_ring_second_body(f1, wq, i2, s2, i3, s3, f3, f2):
    copy_rim(f2, i2, s2, 9, 13)
    for block in blocks_ring(9, 13):
        conv_block(f1, f2, wq.at[1], *block, True)
    for block in blocks_ring(8, 12):
        conv_block(f2, f3, wq.at[2], *block, False)
    f3[2:6, 4:8] = i3[...]
    f3[2:6, 2:4] = s3[0]
    f3[2:6, 8:10] = s3[1]


def up_ring_merge_body(f3, merge_in, mo, own1, dc, l1, l2, child0, child1):
    for block in blocks_ring(8, 12):
        merge_block(f3, l1, merge_in, mo, *block)
    l1[2:6, 2:10] = own1[...]
    for i in (0, 2):
        top = jnp.concatenate([paired_columns(l1[2 * i]), paired_columns(l1[2 * i + 2])], axis=0)
        bottom = jnp.concatenate(
            [paired_columns(l1[2 * i + 1]), paired_columns(l1[2 * i + 3])], axis=0
        )
        l2[i : i + 2] = merge_pair(top, bottom, merge_in[...], mo[...]).reshape(2, 6, samples, 128)
    for i in range(8):
        for a in range(2):
            if 0 <= i - (1 - a) < 7:
                cells = f3[i, :, :, a * 128 : a * 128 + 128].reshape(12 * samples, 128)
                child0[i - (1 - a), a] = dot(cells, dc[...]).astype(bf16)
        child1[i] = dot(l1[i].reshape(12 * samples, 128), dc[:, 0:256]).astype(bf16)


def mid_body(place, z0, z1, z2, z3, merge_in, mo, a3, a4, p5, send1, send3, strip, l4s):
    row = place[0]
    col = place[1]
    deep = row // 4
    high = row % 4
    wide = col // 2
    core = col % 2
    for m, ref in zip(deep_masks, (z0, z1, z2, z3)):
        for n, mask in enumerate(high_masks):
            for k in range(2):
                strip[deep ^ m, high ^ mask, core ^ k] = ref[n, k]
    cells = strip[...].reshape(8, 2, 2, samples, 128)
    l4 = merge_pair(
        cells[:, 0].reshape(16, samples, 128),
        cells[:, 1].reshape(16, samples, 128),
        merge_in[...],
        mo[...],
    )
    l4s[...] = l4.reshape(8, 2, samples, 128)
    pairs = paired_columns(l4).reshape(4, 2, samples, 128)
    l5 = merge_pair(pairs[:, 0], pairs[:, 1], merge_in[...], mo[...])
    packed = paired_columns(l5)
    p5[...] = packed
    low = low_half((samples, 128))
    wide_even = wide % 2 == 0
    for d in range(3):
        line = (row + d + (n_row - 1)) % n_row
        left = strip[line // 4, line % 4, 0]
        right = strip[line // 4, line % 4, 1]
        a3[d, 0] = left
        a3[d, 1] = right
        left4 = l4s[line // 2, 0]
        right4 = l4s[line // 2, 1]
        a4[d, 0] = left4
        a4[d, 1] = right4
        to_right = jnp.where(low, right4, right)
        to_left = jnp.where(low, left, left4)
        send1[d] = jnp.where(wide_even, to_right, to_left)
        send3[d] = jnp.where(wide_even, to_left, to_right)
    send1[3:5] = packed
    send3[3:5] = packed


def both_lanes(cells):
    wide = cells.astype(f32)
    turned = pltpu.roll(wide, 64, wide.ndim - 1)
    low = low_half(wide.shape)
    return jnp.where(low, wide, turned).astype(bf16), jnp.where(low, turned, wide).astype(bf16)


def descent_body(
    place,
    slots,
    a3,
    a4,
    p5,
    q1,
    q2,
    q3,
    f3,
    l1,
    l2,
    merge_in,
    mo,
    do,
    dc,
    dp,
    w2,
    w7,
    do0,
    child0,
    child1,
    wq,
    wh,
    out,
    l5s,
    c6s,
    g6s,
    c2s,
    p2s,
    c1s,
    p1s,
    n0,
    r1,
    r2,
    r3,
):
    row = place[0]
    col = place[1]
    wide = col // 2
    core = col % 2
    wide_even = wide % 2 == 0
    merge_weights = merge_in[...]
    back_weights = mo[...]
    child_weights = dc[:, 0:256]
    parent_weights = dp[...]
    step_weights = w2[...]
    out_weights = do[...]

    for m, ref, start in ((0, p5, 0), (1, q1, 3), (2, q2, 0), (3, q3, 3)):
        for pair in range(2):
            first, second = both_lanes(ref[start + pair])
            l5s[wide ^ m, 2 * pair] = first
            l5s[wide ^ m, 2 * pair + 1] = second
    grid = l5s[...].reshape(2, 2, 2, 2, samples, 128)
    low4 = low_half((4, samples, 128))
    top = jnp.where(
        low4,
        grid[:, 0, :, 0].reshape(4, samples, 128),
        grid[:, 1, :, 0].reshape(4, samples, 128),
    )
    bottom = jnp.where(
        low4,
        grid[:, 0, :, 1].reshape(4, samples, 128),
        grid[:, 1, :, 1].reshape(4, samples, 128),
    )
    l6 = merge_pair(top, bottom, merge_weights, back_weights)
    low1 = low_half((1, samples, 128))
    stacked7 = jnp.concatenate(
        [jnp.where(low1, l6[0:1], l6[2:3]), jnp.where(low1, l6[1:2], l6[3:4])], axis=-1
    )
    hidden7 = relu16(dot(stacked7.reshape(samples, 256), merge_weights))
    part7 = dot(hidden7, w7[...]).reshape(1, samples, 256)
    c7 = dot(hidden7, back_weights).reshape(1, samples, 128)

    def descend(parent, part, child):
        count = child.shape[0]
        flat = child.reshape(count * samples, 128)
        ahead = dot(flat, child_weights).reshape(count, samples, 256)
        inner = relu16(ahead + part).reshape(count * samples, 256)
        step = dot(jnp.concatenate([flat, inner], axis=-1), step_weights)
        part = part + step.reshape(count, samples, 256)
        outcome = dot(inner, out_weights).reshape(count, samples, 128)
        return outcome + child.astype(f32) + parent, part

    c6, part6 = descend(c7, part7, l6)
    c6s[...] = c6.reshape(2, 2, samples, 128)
    g6s[...] = part6.reshape(2, 2, samples, 256)

    side = jnp.where(core == 0, (wide + 3) % 4, (wide + 1) % 4)
    lines = [(row + d + (n_row - 1)) % n_row for d in range(3)]
    parents5 = []
    parts5 = []
    children5 = []
    for place_x in (wide, side):
        for line in lines:
            deep = line // 4
            parents5.append(c6s[place_x // 2, deep // 2])
            parts5.append(g6s[place_x // 2, deep // 2])
            children5.append(l5s[place_x, deep])
    c5, part5 = descend(jnp.stack(parents5), jnp.stack(parts5), jnp.stack(children5))

    from_first = jnp.logical_xor(wide_even, core == 0)
    side_cells = jnp.where(from_first, q1[0:3], q3[0:3])
    side_low, side_high = both_lanes(side_cells)
    side4 = jnp.where(core == 0, side_low, side_high)
    side3 = jnp.where(core == 0, side_high, side_low)
    own4 = a4[...]
    children4 = jnp.concatenate([own4[:, 0], own4[:, 1], side4, side4], axis=0)
    parents4 = jnp.concatenate([c5[0:3], c5, c5[3:6]], axis=0)
    parts4 = jnp.concatenate([part5[0:3], part5, part5[3:6]], axis=0)
    c4, part4 = descend(parents4, parts4, children4)
    own3_0, own3_1 = both_lanes(a3[:, 0])
    own3_2, own3_3 = both_lanes(a3[:, 1])
    first_core = core == 0

    def window(blocks):
        left = jnp.concatenate(blocks[0:4], axis=0)
        right = jnp.concatenate(blocks[2:6], axis=0)
        return jnp.where(first_core, left, right)

    starts = (6, 0, 0, 3, 3, 6)
    c3, part3 = descend(
        window([c4[k : k + 3] for k in starts]),
        window([part4[k : k + 3] for k in starts]),
        window([side3, own3_0, own3_1, own3_2, own3_3, side3]),
    )
    above = [3 * j + i for i in (0, 1, 1, 2) for j in (0, 1, 1, 2, 2, 3)]
    c2, part2 = descend(
        jnp.stack([c3[k] for k in above]),
        jnp.stack([part3[k] for k in above]),
        l2[...].reshape(24, samples, 128),
    )
    c2s[...] = c2.reshape(4, 6, samples, 128)
    p2s[...] = part2.astype(bf16).reshape(4, 6, samples, 256)

    rows = 12 * samples
    low11 = low_half((11, samples, 128))
    sub = lax.broadcasted_iota(jnp.int32, (256, 256), 0)
    lane = lax.broadcasted_iota(jnp.int32, (256, 256), 1)
    averager = jnp.where(sub // 64 == lane // 64, 1.0 / 64, 0.0).astype(bf16)
    for i in range(8):
        parent = c2s[i // 2][:, None]
        parent = jnp.broadcast_to(parent, (6, 2, samples, 128)).reshape(rows, 128)
        part = jnp.broadcast_to(p2s[i // 2][:, None], (6, 2, samples, 256)).reshape(rows, 256)
        inner = relu16(child1[i] + part)
        c1 = dot(inner, out_weights) + l1[i].astype(f32).reshape(rows, 128) + parent
        c1s[i] = c1.astype(bf16)
    for i in range(8):
        p1s[i] = dot(c1s[i], parent_weights)
    for i in range(8):
        part = p1s[i]
        part = jnp.concatenate([part, part], axis=-1).astype(bf16)
        context = c1s[i].astype(f32)
        halves = [a for a in range(2) if 0 <= i - (1 - a) < 7]
        fine = []
        for a in halves:
            inner = relu16(child0[i - (1 - a), a] + part)
            child = f3[i, :, :, a * 128 : a * 128 + 128].astype(f32).reshape(rows, 128)
            fine.append(dot(inner, do0[...]) + child + context)
        fine = jnp.concatenate(fine, axis=-1)
        width = fine.shape[-1]
        mean = dot((fine * fine).astype(bf16), averager[:width, :width])
        normed = (fine * lax.rsqrt(mean + norm_eps)).astype(bf16).reshape(12, samples, width)
        for k, a in enumerate(halves):
            part16 = normed[..., k * 128 : k * 128 + 128]
            n0[i - (1 - a), :, :, a * 128 : a * 128 + 128] = jnp.where(
                low11, part16[1:12], part16[0:11]
            )
    conv_block(n0, r1, wq.at[0], (0, 6), (0, 10), False)
    conv_block(r1, r2, wq.at[1], (0, 5), (0, 9), True)
    conv_block(r2, r3, wq.at[2], (0, 4), (0, 8), False)
    stacked = jnp.concatenate(
        [r3[:, quad].reshape(4 * samples, 256) for quad in range(8)], axis=-1
    )
    cell_logits = dot(stacked, wh[...]).reshape(4, samples, 128)
    coarse = cell_logits.astype(bf16)
    rest = (cell_logits - coarse.astype(f32)).astype(bf16)
    places = lax.broadcasted_iota(jnp.int32, (128, 64), 0)
    for i in range(8):
        chosen = (places == slots[i : i + 1, :] + 64 * (i % 2)).astype(bf16)
        out[:, i, :] = dot(coarse[i // 2], chosen) + dot(rest[i // 2], chosen)


def swap(value, partner):
    pairs = []
    for r in range(n_row):
        for c in range(n_col):
            pr, pc = partner(r, c)
            pairs.append((r * n_col + c, pr * n_col + pc))
    return lax.ppermute(value, ("row", "col"), pairs)


def pair_after(i, count):
    return i ^ 1


def pair_before(i, count):
    return (((i - 1) % count ^ 1) + 1) % count


def on_device(
    readouts, w_embed, w_up, merge_in, merge_out, down_in, down_out, w_down, w_head, qubit_slot
):
    row = lax.axis_index("row")
    col = lax.axis_index("col")
    place = jnp.stack([row, col]).astype(jnp.int32)
    col_even = col % 2 == 0

    row_a = swap(readouts, lambda r, c: (pair_after(r, n_row), c))
    row_b = swap(readouts, lambda r, c: (pair_before(r, n_row), c))
    own, wq_up, we, mi, mo, wq_down, di, dc, dp, do0, do, wh, w2, w7 = whole_call(
        prep_body,
        (
            arr((8, 16, 256)),
            arr((3, 1024, 256)),
            arr((512, 256)),
            arr((256, 256)),
            arr((256, 128)),
            arr((3, 1024, 256)),
            arr((128, 256)),
            arr((128, 512)),
            arr((128, 256)),
            arr((512, 128)),
            arr((256, 128)),
            arr((2048, 128)),
            arr((384, 256)),
            arr((256, 256)),
        ),
        [
            pltpu.VMEM((3, 9, 64, 64), bf16),
            pltpu.VMEM((8, 64), bf16),
            pltpu.VMEM((64, 256), bf16),
            pltpu.VMEM((3, 9, 64, 64), bf16),
            pltpu.VMEM((64, 256), bf16),
            pltpu.VMEM((4, 64), bf16),
            pltpu.SemaphoreType.DMA((9,)),
        ],
        (
            readouts,
            w_up,
            w_embed,
            merge_in,
            merge_out.T,
            w_down,
            down_in,
            down_out.T,
            w_head.T,
        ),
        outside=tuple(range(9)),
    )
    tiles = jnp.stack([own, row_b, row_a])
    left = tiles[:, :, 0:8]
    right = tiles[:, :, 8:16]
    col_a = swap(jnp.where(col_even, right, left), lambda r, c: (r, pair_after(c, n_col)))
    col_b = swap(jnp.where(col_even, left, right), lambda r, c: (r, pair_before(c, n_col)))
    quads = lambda rows, cols: pltpu.VMEM((rows, cols, samples, 256), bf16)
    ext = pltpu.VMEM((24, 4, 8, 256), f32)
    i0, i1, i2, i3, il1 = whole_call(
        up_inner_body,
        (
            arr((7, 7, samples, 256)),
            arr((6, 6, samples, 256)),
            arr((5, 5, samples, 256)),
            arr((4, 4, samples, 256)),
            arr((4, 4, samples, 128)),
        ),
        [ext],
        (place, tiles, wq_up, we, mi, mo),
        smem=(0,),
    )
    i0, col_b, col_a = lax.optimization_barrier((i0, col_b, col_a))
    s0, s1, s2, s3, own1, l3, cells = whole_call(
        up_own_body,
        (
            arr((2, 7, 3, samples, 256)),
            arr((2, 6, 3, samples, 256)),
            arr((2, 5, 3, samples, 256)),
            arr((2, 4, 2, samples, 256)),
            arr((4, 8, samples, 128)),
            arr((samples, 128)),
            arr((24, 4, 8, 256), f32),
        ),
        [],
        (place, tiles, col_b, col_a, wq_up, we, mi, mo, i0, i1, i2, il1),
        smem=(0,),
    )

    pair = jnp.stack([l3, swap(l3, lambda r, c: (r, c ^ 1))])
    f0 = whole_call(
        up_ring_embed_body,
        arr((11, 15, samples, 256)),
        [],
        (cells, we, i0, s0),
    )
    pair, f0 = lax.optimization_barrier((pair, f0))
    four = jnp.stack([pair] + [swap(pair, lambda r, c, m=m: (r ^ m, c)) for m in high_masks[1:]])
    f1 = whole_call(
        up_ring_first_body, arr((10, 14, samples, 256)), [], (f0, wq_up, i1, s1)
    )
    four, f1 = lax.optimization_barrier((four, f1))
    strips = [four] + [swap(four, lambda r, c, m=m: (r ^ (4 * m), c)) for m in deep_masks[1:]]
    f3 = whole_call(
        up_ring_second_body,
        arr((8, 12, samples, 256)),
        [quads(9, 13)],
        (f1, wq_up, i2, s2, i3, s3),
    )
    strips[3], f3 = lax.optimization_barrier((strips[3], f3))
    a3, a4, p5, send1, send3 = whole_call(
        mid_body,
        (
            arr((3, 2, samples, 128)),
            arr((3, 2, samples, 128)),
            arr((2, samples, 128)),
            arr((5, samples, 128)),
            arr((5, samples, 128)),
        ),
        [pltpu.VMEM((4, 4, 2, samples, 128), bf16), pltpu.VMEM((8, 2, samples, 128), bf16)],
        (place, *strips, mi, mo),
        smem=(0,),
    )
    q1 = swap(send1, lambda r, c: (r, c ^ 2))
    q2 = swap(p5, lambda r, c: (r, c ^ 4))
    q3 = swap(send3, lambda r, c: (r, c ^ 6))
    l1, l2, child0, child1 = whole_call(
        up_ring_merge_body,
        (
            arr((8, 12, samples, 128)),
            arr((4, 6, samples, 128)),
            arr((7, 2, 12 * samples, 512)),
            arr((8, 12 * samples, 256)),
        ),
        [],
        (f3, mi, mo, own1, dc),
    )
    slots = qubit_slot.reshape(qubit_slot.shape[0], qubit_slot.shape[2])
    return whole_call(
        descent_body,
        arr((samples, 8, 64), f32),
        [
            pltpu.VMEM((4, 4, samples, 128), bf16),
            pltpu.VMEM((2, 2, samples, 128), f32),
            pltpu.VMEM((2, 2, samples, 256), f32),
            pltpu.VMEM((4, 6, samples, 128), f32),
            pltpu.VMEM((4, 6, samples, 256), bf16),
            pltpu.VMEM((8, 12 * samples, 128), bf16),
            pltpu.VMEM((8, 12 * samples, 256), f32),
            quads(7, 11),
            quads(6, 10),
            quads(5, 9),
            quads(4, 8),
        ],
        (
            place,
            slots,
            a3,
            a4,
            p5,
            q1,
            q2,
            q3,
            f3,
            l1,
            l2,
            mi,
            mo,
            do,
            dc,
            dp,
            w2,
            w7,
            do0,
            child0,
            child1,
            wq_down,
            wh,
        ),
        smem=(0,),
    )


def solution(mesh):
    placed = (P("row", "col", None), P(), P(), P(), P(), P(), P(), P(), P(), P("row", "col", None))
    return jax.shard_map(
        on_device, mesh=mesh, in_specs=placed, out_specs=P(None, "row", "col"), check_vma=False
    )
```

```python
import functools

import jax
import jax.numpy as jnp
from jax import lax
from jax.experimental import pallas as pl
from jax.experimental.pallas import tpu as pltpu
from jax.sharding import PartitionSpec as P

norm_eps = 1e-05
bf16 = jnp.bfloat16
f32 = jnp.float32
n_row = 16
n_col = 8
samples = 32
vmem_bytes = 20 * 1024 * 1024
high_masks = (0, 2, 3, 1)
deep_masks = (0, 3, 1, 2)


def dot(left, right):
    return jnp.dot(left, right, preferred_element_type=f32)


def relu16(wide):
    return jnp.maximum(wide.astype(bf16), 0)


def low_half(shape):
    return lax.broadcasted_iota(jnp.int32, shape, len(shape) - 1) < 64


def whole_call(body, out_shapes, scratch, args, smem=(), outside=()):
    args = [
        pltpu.with_memory_space_constraint(x, pltpu.HBM) if i in outside else x
        for i, x in enumerate(args)
    ]
    specs = [
        pl.BlockSpec(
            memory_space=pltpu.SMEM if i in smem else pltpu.HBM if i in outside else pltpu.VMEM
        )
        for i in range(len(args))
    ]
    return pl.pallas_call(
        body,
        out_shape=out_shapes,
        in_specs=specs,
        out_specs=jax.tree.map(lambda _: pl.BlockSpec(memory_space=pltpu.VMEM), out_shapes),
        scratch_shapes=scratch,
        compiler_params=pltpu.CompilerParams(vmem_limit_bytes=vmem_bytes),
    )(*args)


def arr(shape, dtype=bf16):
    return jax.ShapeDtypeStruct(shape, dtype)


def fill_quad_weights(src, out, layer, from_odd):
    zero = jnp.zeros((64, 64), bf16)

    def tap_of(step, parity_in, parity_out):
        place_in = 1 - parity_in if from_odd else parity_in
        place_out = parity_out if from_odd else 1 - parity_out
        tap = 2 * step + place_in - place_out
        return tap if 0 <= tap <= 2 else None

    for di in range(2):
        for dj in range(2):
            for a in range(2):
                for b in range(2):
                    base = ((di * 2 + dj) * 4 + a * 2 + b) * 64
                    for oa in range(2):
                        tap_row = tap_of(di, a, oa)
                        blocks = []
                        for ob in range(2):
                            tap_col = tap_of(dj, b, ob)
                            if tap_row is None or tap_col is None:
                                blocks.append(zero)
                            else:
                                blocks.append(src[layer, 3 * tap_row + tap_col])
                        out[layer, base : base + 64, oa * 128 : oa * 128 + 128] = jnp.concatenate(
                            blocks, axis=1
                        )


def dot_rows(left, right):
    return lax.dot_general(left, right, (((0,), (0,)), ((), ())), preferred_element_type=f32)


def lane_copies(first, second):
    row = lax.broadcasted_iota(jnp.int32, (64, 128), 0)
    lane = lax.broadcasted_iota(jnp.int32, (64, 128), 1)
    kept = jnp.where(lane < 64, first, second) > 0
    return jnp.where(kept & (row == lane % 64), 1.0, 0.0).astype(bf16)


def copies_in(sems, *pairs):
    copies = [pltpu.make_async_copy(src, dst, sems.at[i]) for i, (src, dst) in enumerate(pairs)]
    for copy in copies:
        copy.start()
    return copies


def prep_body(
    own,
    w_up,
    w_embed,
    merge_in,
    merge_out_t,
    w_down,
    down_in,
    down_out_t,
    w_head_t,
    own_out,
    wq,
    we,
    mi,
    mo,
    wq_down,
    di,
    dc,
    dp,
    do0,
    do,
    wh,
    w2,
    w7,
    w_up_s,
    w_embed_s,
    mo_s,
    w_down_s,
    do_s,
    head_s,
    sems,
):
    copies = copies_in(
        sems,
        (w_up, w_up_s),
        (w_embed, w_embed_s),
        (merge_out_t, mo_s),
        (own, own_out),
        (merge_in, mi),
        (w_down, w_down_s),
        (down_in, di),
        (down_out_t, do_s),
        (w_head_t, head_s),
    )
    copies[0].wait()
    for layer in range(3):
        fill_quad_weights(w_up_s, wq, layer, layer % 2 == 0)
    copies[1].wait()
    tiled = jnp.concatenate([w_embed_s[...].astype(f32)] * 16, axis=0)
    none = jnp.zeros((128, 64), f32)
    for a in range(2):
        for b in range(2):
            q = 2 * a + b
            pair = [tiled, none] if b == 0 else [none, tiled]
            we[q * 128 : q * 128 + 128, a * 128 : a * 128 + 128] = jnp.concatenate(
                pair, axis=1
            ).astype(bf16)
            we[q * 128 : q * 128 + 128, (1 - a) * 128 : (1 - a) * 128 + 128] = jnp.zeros(
                (128, 128), bf16
            )
    copies[2].wait()
    mo[...] = dot_rows(mo_s[...], lane_copies(1, 1)).astype(bf16)
    copies[3].wait()
    copies[4].wait()
    copies[5].wait()
    for layer in range(3):
        fill_quad_weights(w_down_s, wq_down, layer, layer % 2 == 0)
    copies[6].wait()
    zero = jnp.zeros((64, 256), bf16)
    child = di[64:128, :]
    dc[0:64, 0:256] = child
    dc[0:64, 256:512] = zero
    dc[64:128, 0:256] = zero
    dc[64:128, 256:512] = child
    dp[0:64, :] = di[0:64, :]
    dp[64:128, :] = zero
    copies[7].wait()
    back = do_s[...]
    do0[0:256, :] = dot_rows(back, lane_copies(1, 0)).astype(bf16)
    do0[256:512, :] = dot_rows(back, lane_copies(0, 1)).astype(bf16)
    do[...] = dot_rows(back, lane_copies(1, 1)).astype(bf16)
    w2[0:128, :] = dp[...]
    w2[128:384, :] = dot(do[...], dp[...]).astype(bf16)
    w7[...] = dot(mo[...], dp[...]).astype(bf16)
    copies[8].wait()
    output = lax.broadcasted_iota(jnp.int32, (4, 128), 0)
    lane = lax.broadcasted_iota(jnp.int32, (4, 128), 1)
    head = dot_rows(head_s[...], jnp.where(lane % 4 == output, 1.0, 0.0).astype(bf16))
    lane = lax.broadcasted_iota(jnp.int32, (64, 128), 1)
    for quad in range(8):
        for a in range(2):
            for b in range(2):
                base = quad * 256 + (a * 2 + b) * 64
                first = a * 64 + 4 * (2 * quad + b)
                kept = jnp.where((lane >= first) & (lane < first + 4), head, 0.0)
                wh[base : base + 64, :] = kept.astype(bf16)


def row_chunks(first, last, cols):
    step = max(1, 14 // cols)
    return [(i, min(i + step, last)) for i in range(first, last, step)]


def conv_block(src, dst, weights, row_range, col_range, to_odd, src_at=(0, 0), dst_at=(0, 0)):
    c0, c1 = col_range
    cols = c1 - c0
    for r0, r1 in row_chunks(*row_range, cols):
        rows = r1 - r0
        i, j = r0 - src_at[0], c0 - src_at[1]
        here = src[i : i + rows, j : j + cols]
        right = src[i : i + rows, j + 1 : j + 1 + cols]
        below = src[i + 1 : i + 1 + rows, j : j + cols]
        corner = src[i + 1 : i + 1 + rows, j + 1 : j + 1 + cols]
        stacked = jnp.concatenate([here, right, below, corner], axis=-1)
        update = dot(stacked.reshape(rows * cols * samples, 1024), weights[...])
        update = jnp.maximum(update, 0.0).reshape(rows, cols, samples, 256)
        low = low_half((rows, cols, samples, 128))
        if to_odd:
            old0 = jnp.where(low, corner[..., 0:128], below[..., 0:128])
            old1 = jnp.where(low, right[..., 128:256], here[..., 128:256])
        else:
            old0 = jnp.where(low, here[..., 0:128], right[..., 0:128])
            old1 = jnp.where(low, below[..., 128:256], corner[..., 128:256])
        new0 = (old0.astype(f32) + update[..., 0:128]).astype(bf16)
        new1 = (old1.astype(f32) + update[..., 128:256]).astype(bf16)
        i, j = r0 - dst_at[0], c0 - dst_at[1]
        dst[i : i + rows, j : j + cols, :, 0:128] = new0
        dst[i : i + rows, j : j + cols, :, 128:256] = new1


def spread_tiles(place, tiles, ext):
    row_even = place[0] % 2 == 0
    after_row = jnp.where(row_even, 16, 0)
    before_row = jnp.where(row_even, 0, 16)
    for tile, start in ((0, 8), (1, before_row), (2, after_row)):
        cells = tiles[tile].astype(f32)
        ext[pl.ds(start, 8), 1] = cells[:, 0:8]
        ext[pl.ds(start, 8), 2] = cells[:, 8:16]


def spread_sides(place, col_a, col_b, ext):
    row_even = place[0] % 2 == 0
    col_even = place[1] % 2 == 0
    after_row = jnp.where(row_even, 16, 0)
    before_row = jnp.where(row_even, 0, 16)
    after_col = jnp.where(col_even, 3, 0)
    before_col = jnp.where(col_even, 0, 3)
    for tile, start in ((0, 8), (1, before_row), (2, after_row)):
        ext[pl.ds(start, 8), after_col] = col_a[tile].astype(f32)
        ext[pl.ds(start, 8), before_col] = col_b[tile].astype(f32)


def embed_block(ext, we, dst, row_range, col_range, dst_at=(0, 0)):
    c0, c1 = col_range
    cols = c1 - c0
    sub = lax.broadcasted_iota(jnp.int32, (16, 128), 0)
    lane = lax.broadcasted_iota(jnp.int32, (16, 128), 1)
    own_lanes = (lane // 8 == sub).astype(f32)
    for r0, r1 in row_chunks(*row_range, cols):
        quads = []
        for i in range(r0, r1):
            for quad in range(c0, c1):
                parts = []
                for a in range(2):
                    row = 1 + 2 * i + (1 - a)
                    for b in range(2):
                        col = 1 + 2 * quad + (1 - b)
                        cell = ext[row, col // 8, col % 8 : col % 8 + 1, :]
                        halves = [
                            jnp.broadcast_to(cell[:, k : k + 128], (16, 128)) * own_lanes
                            for k in (0, 128)
                        ]
                        parts.append(jnp.concatenate(halves, axis=0).astype(bf16))
                quads.append(jnp.concatenate(parts, axis=-1))
        embedded = dot(jnp.concatenate(quads, axis=0), we[...]).astype(bf16)
        i, j = r0 - dst_at[0], c0 - dst_at[1]
        dst[i : i + r1 - r0, j : j + cols] = embedded.reshape(r1 - r0, cols, samples, 256)


def merge_block(src, dst, merge_in, mo, row_range, col_range):
    c0, c1 = col_range
    cols = c1 - c0
    for r0, r1 in row_chunks(*row_range, cols):
        stacked = src[r0:r1, c0:c1].reshape((r1 - r0) * cols * samples, 256)
        hidden = relu16(dot(stacked, merge_in[...]))
        merged = dot(hidden, mo[...]).astype(bf16)
        dst[r0:r1, c0:c1] = merged.reshape(r1 - r0, cols, samples, 128)


def blocks_ring(rows, cols):
    return [
        ((0, 2), (0, cols)),
        ((2, rows - 2), (0, 2)),
        ((2, rows - 2), (cols - 2, cols)),
        ((rows - 2, rows), (0, cols)),
    ]


def copy_rim(dst, inner, sides, rows, cols):
    for place, row in ((2, 0), (rows - 3, rows - 5)):
        dst[place, 2:4] = sides[0, row, 0:2]
        dst[place, 4 : cols - 4] = inner[row]
        dst[place, cols - 4 : cols - 2] = sides[1, row, 1:3]
    dst[3 : rows - 3, 2] = sides[0, 1 : rows - 5, 0]
    dst[3 : rows - 3, cols - 3] = sides[1, 1 : rows - 5, 2]


def merge_pair(top, bottom, merge_in, mo):
    count = top.shape[0]
    stacked = jnp.concatenate([top, bottom], axis=-1).reshape(count * samples, 256)
    hidden = relu16(dot(stacked, merge_in))
    return dot(hidden, mo).astype(bf16).reshape(count, samples, 128)


def paired_columns(cells):
    count = cells.shape[0] // 2
    split = cells.reshape(count, 2, samples, 128)
    low = low_half((count, samples, 128))
    return jnp.where(low, split[:, 0], split[:, 1])


def up_inner_body(place, tiles, wq, we, merge_in, mo, f0, f1, f2, f3, l1, ext):
    at = (2, 4)
    spread_tiles(place, tiles, ext)
    embed_block(ext, we, f0, (2, 9), (4, 11), at)
    conv_block(f0, f1, wq.at[0], (2, 8), (4, 10), False, at, at)
    conv_block(f1, f2, wq.at[1], (2, 7), (4, 9), True, at, at)
    conv_block(f2, f3, wq.at[2], (2, 6), (4, 8), False, at, at)
    merge_block(f3, l1, merge_in, mo, (0, 4), (0, 4))


def up_own_body(
    place,
    tiles,
    col_b,
    col_a,
    wq,
    we,
    merge_in,
    mo,
    i0,
    i1,
    i2,
    il1,
    s0,
    s1,
    s2,
    s3,
    l1,
    out,
    ext,
):
    spread_tiles(place, tiles, ext)
    spread_sides(place, col_a, col_b, ext)
    for ref, inner, rows, cols in ((s0, i0, 7, 7), (s1, i1, 6, 6), (s2, i2, 5, 5)):
        ref[0, :, 2] = inner[:, 0]
        ref[1, :, 0] = inner[:, cols - 1]
    left = (2, 4)
    for k, cols in ((0, left), (1, (11, 13))):
        embed_block(ext, we, s0.at[k], (2, 9), cols, (2, 2 if k == 0 else 10))
    for k, cols in ((0, left), (1, (10, 12))):
        src_at = (2, 2 if k == 0 else 10)
        dst_at = (2, 2 if k == 0 else 9)
        conv_block(s0.at[k], s1.at[k], wq.at[0], (2, 8), cols, False, src_at, dst_at)
    for k, cols in ((0, left), (1, (9, 11))):
        src_at = (2, 2 if k == 0 else 9)
        dst_at = (2, 2 if k == 0 else 8)
        conv_block(s1.at[k], s2.at[k], wq.at[1], (2, 7), cols, True, src_at, dst_at)
    for k, cols in ((0, left), (1, (8, 10))):
        src_at = (2, 2 if k == 0 else 8)
        conv_block(s2.at[k], s3.at[k], wq.at[2], (2, 6), cols, False, src_at, (2, cols[0]))
    merged = merge_pair(
        s3[..., 0:128].reshape(16, samples, 128),
        s3[..., 128:256].reshape(16, samples, 128),
        merge_in[...],
        mo[...],
    ).reshape(2, 4, 2, samples, 128)
    cells = jnp.concatenate([merged[0], il1[...], merged[1]], axis=1)
    l1[...] = cells
    top = jnp.concatenate([paired_columns(cells[0]), paired_columns(cells[2])], axis=0)
    bottom = jnp.concatenate([paired_columns(cells[1]), paired_columns(cells[3])], axis=0)
    l2 = merge_pair(top, bottom, merge_in[...], mo[...])
    l3 = merge_pair(paired_columns(l2[0:4]), paired_columns(l2[4:8]), merge_in[...], mo[...])
    out[...] = paired_columns(l3)[0]


def up_ring_embed_body(ext, we, i0, s0, f0):
    copy_rim(f0, i0, s0, 11, 15)
    for block in blocks_ring(11, 15):
        embed_block(ext, we, f0, *block)


def up_ring_first_body(f0, wq, i1, s1, f1):
    for block in blocks_ring(10, 14):
        conv_block(f0, f1, wq.at[0], *block, False)
    copy_rim(f1, i1, s1, 10, 14)


def up_ring_second_body(f1, wq, i2, s2, i3, s3, f3, f2):
    copy_rim(f2, i2, s2, 9, 13)
    for block in blocks_ring(9, 13):
        conv_block(f1, f2, wq.at[1], *block, True)
    for block in blocks_ring(8, 12):
        conv_block(f2, f3, wq.at[2], *block, False)
    f3[2:6, 4:8] = i3[...]
    f3[2:6, 2:4] = s3[0]
    f3[2:6, 8:10] = s3[1]


def up_ring_merge_body(f3, merge_in, mo, own1, dc, l1, l2, child0, child1):
    for block in blocks_ring(8, 12):
        merge_block(f3, l1, merge_in, mo, *block)
    l1[2:6, 2:10] = own1[...]
    for i in (0, 2):
        top = jnp.concatenate([paired_columns(l1[2 * i]), paired_columns(l1[2 * i + 2])], axis=0)
        bottom = jnp.concatenate(
            [paired_columns(l1[2 * i + 1]), paired_columns(l1[2 * i + 3])], axis=0
        )
        l2[i : i + 2] = merge_pair(top, bottom, merge_in[...], mo[...]).reshape(2, 6, samples, 128)
    for i in range(8):
        for a in range(2):
            if 0 <= i - (1 - a) < 7:
                cells = f3[i, :, :, a * 128 : a * 128 + 128].reshape(12 * samples, 128)
                child0[i - (1 - a), a] = dot(cells, dc[...]).astype(bf16)
        child1[i] = dot(l1[i].reshape(12 * samples, 128), dc[:, 0:256]).astype(bf16)


def mid_body(place, z0, z1, z2, z3, merge_in, mo, a3, a4, p5, send1, send3, strip, l4s):
    row = place[0]
    col = place[1]
    deep = row // 4
    high = row % 4
    wide = col // 2
    core = col % 2
    for m, ref in zip(deep_masks, (z0, z1, z2, z3)):
        for n, mask in enumerate(high_masks):
            for k in range(2):
                strip[deep ^ m, high ^ mask, core ^ k] = ref[n, k]
    cells = strip[...].reshape(8, 2, 2, samples, 128)
    l4 = merge_pair(
        cells[:, 0].reshape(16, samples, 128),
        cells[:, 1].reshape(16, samples, 128),
        merge_in[...],
        mo[...],
    )
    l4s[...] = l4.reshape(8, 2, samples, 128)
    pairs = paired_columns(l4).reshape(4, 2, samples, 128)
    l5 = merge_pair(pairs[:, 0], pairs[:, 1], merge_in[...], mo[...])
    packed = paired_columns(l5)
    p5[...] = packed
    low = low_half((samples, 128))
    wide_even = wide % 2 == 0
    for d in range(3):
        line = (row + d + (n_row - 1)) % n_row
        left = strip[line // 4, line % 4, 0]
        right = strip[line // 4, line % 4, 1]
        a3[d, 0] = left
        a3[d, 1] = right
        left4 = l4s[line // 2, 0]
        right4 = l4s[line // 2, 1]
        a4[d, 0] = left4
        a4[d, 1] = right4
        to_right = jnp.where(low, right4, right)
        to_left = jnp.where(low, left, left4)
        send1[d] = jnp.where(wide_even, to_right, to_left)
        send3[d] = jnp.where(wide_even, to_left, to_right)
    send1[3:5] = packed
    send3[3:5] = packed


def both_lanes(cells):
    wide = cells.astype(f32)
    turned = pltpu.roll(wide, 64, wide.ndim - 1)
    low = low_half(wide.shape)
    return jnp.where(low, wide, turned).astype(bf16), jnp.where(low, turned, wide).astype(bf16)


def descent_body(
    place,
    slots,
    a3,
    a4,
    p5,
    q1,
    q2,
    q3,
    f3,
    l1,
    l2,
    merge_in,
    mo,
    do,
    dc,
    dp,
    w2,
    w7,
    do0,
    child0,
    child1,
    wq,
    wh,
    out,
    l5s,
    c6s,
    g6s,
    c2s,
    p2s,
    c1s,
    p1s,
    n0,
    r1,
    r2,
    r3,
):
    row = place[0]
    col = place[1]
    wide = col // 2
    core = col % 2
    wide_even = wide % 2 == 0
    merge_weights = merge_in[...]
    back_weights = mo[...]
    child_weights = dc[:, 0:256]
    parent_weights = dp[...]
    step_weights = w2[...]
    out_weights = do[...]

    for m, ref, start in ((0, p5, 0), (1, q1, 3), (2, q2, 0), (3, q3, 3)):
        for pair in range(2):
            first, second = both_lanes(ref[start + pair])
            l5s[wide ^ m, 2 * pair] = first
            l5s[wide ^ m, 2 * pair + 1] = second
    grid = l5s[...].reshape(2, 2, 2, 2, samples, 128)
    low4 = low_half((4, samples, 128))
    top = jnp.where(
        low4,
        grid[:, 0, :, 0].reshape(4, samples, 128),
        grid[:, 1, :, 0].reshape(4, samples, 128),
    )
    bottom = jnp.where(
        low4,
        grid[:, 0, :, 1].reshape(4, samples, 128),
        grid[:, 1, :, 1].reshape(4, samples, 128),
    )
    l6 = merge_pair(top, bottom, merge_weights, back_weights)
    low1 = low_half((1, samples, 128))
    stacked7 = jnp.concatenate(
        [jnp.where(low1, l6[0:1], l6[2:3]), jnp.where(low1, l6[1:2], l6[3:4])], axis=-1
    )
    hidden7 = relu16(dot(stacked7.reshape(samples, 256), merge_weights))
    part7 = dot(hidden7, w7[...]).reshape(1, samples, 256)
    c7 = dot(hidden7, back_weights).reshape(1, samples, 128)

    def descend(parent, part, child):
        count = child.shape[0]
        flat = child.reshape(count * samples, 128)
        ahead = dot(flat, child_weights).reshape(count, samples, 256)
        inner = relu16(ahead + part).reshape(count * samples, 256)
        step = dot(jnp.concatenate([flat, inner], axis=-1), step_weights)
        part = part + step.reshape(count, samples, 256)
        outcome = dot(inner, out_weights).reshape(count, samples, 128)
        return outcome + child.astype(f32) + parent, part

    c6, part6 = descend(c7, part7, l6)
    c6s[...] = c6.reshape(2, 2, samples, 128)
    g6s[...] = part6.reshape(2, 2, samples, 256)

    side = jnp.where(core == 0, (wide + 3) % 4, (wide + 1) % 4)
    lines = [(row + d + (n_row - 1)) % n_row for d in range(3)]
    parents5 = []
    parts5 = []
    children5 = []
    for place_x in (wide, side):
        for line in lines:
            deep = line // 4
            parents5.append(c6s[place_x // 2, deep // 2])
            parts5.append(g6s[place_x // 2, deep // 2])
            children5.append(l5s[place_x, deep])
    c5, part5 = descend(jnp.stack(parents5), jnp.stack(parts5), jnp.stack(children5))

    from_first = jnp.logical_xor(wide_even, core == 0)
    side_cells = jnp.where(from_first, q1[0:3], q3[0:3])
    side_low, side_high = both_lanes(side_cells)
    side4 = jnp.where(core == 0, side_low, side_high)
    side3 = jnp.where(core == 0, side_high, side_low)
    own4 = a4[...]
    children4 = jnp.concatenate([own4[:, 0], own4[:, 1], side4, side4], axis=0)
    parents4 = jnp.concatenate([c5[0:3], c5, c5[3:6]], axis=0)
    parts4 = jnp.concatenate([part5[0:3], part5, part5[3:6]], axis=0)
    c4, part4 = descend(parents4, parts4, children4)
    own3_0, own3_1 = both_lanes(a3[:, 0])
    own3_2, own3_3 = both_lanes(a3[:, 1])
    first_core = core == 0

    def window(blocks):
        left = jnp.concatenate(blocks[0:4], axis=0)
        right = jnp.concatenate(blocks[2:6], axis=0)
        return jnp.where(first_core, left, right)

    starts = (6, 0, 0, 3, 3, 6)
    c3, part3 = descend(
        window([c4[k : k + 3] for k in starts]),
        window([part4[k : k + 3] for k in starts]),
        window([side3, own3_0, own3_1, own3_2, own3_3, side3]),
    )
    above = [3 * j + i for i in (0, 1, 1, 2) for j in (0, 1, 1, 2, 2, 3)]
    c2, part2 = descend(
        jnp.stack([c3[k] for k in above]),
        jnp.stack([part3[k] for k in above]),
        l2[...].reshape(24, samples, 128),
    )
    c2s[...] = c2.reshape(4, 6, samples, 128)
    p2s[...] = part2.astype(bf16).reshape(4, 6, samples, 256)

    rows = 12 * samples
    low11 = low_half((11, samples, 128))
    sub = lax.broadcasted_iota(jnp.int32, (256, 256), 0)
    lane = lax.broadcasted_iota(jnp.int32, (256, 256), 1)
    averager = jnp.where(sub // 64 == lane // 64, 1.0 / 64, 0.0).astype(bf16)
    def context_row(i):
        parent = c2s[i // 2][:, None]
        parent = jnp.broadcast_to(parent, (6, 2, samples, 128)).reshape(rows, 128)
        part = jnp.broadcast_to(p2s[i // 2][:, None], (6, 2, samples, 256)).reshape(rows, 256)
        inner = relu16(child1[i] + part)
        c1 = dot(inner, out_weights) + l1[i].astype(f32).reshape(rows, 128) + parent
        c1s[i] = c1.astype(bf16)

    def part_row(i):
        p1s[i] = dot(c1s[i], parent_weights)

    def fine_row(i):
        part = p1s[i]
        part = jnp.concatenate([part, part], axis=-1).astype(bf16)
        context = c1s[i].astype(f32)
        halves = [a for a in range(2) if 0 <= i - (1 - a) < 7]
        fine = []
        for a in halves:
            inner = relu16(child0[i - (1 - a), a] + part)
            child = f3[i, :, :, a * 128 : a * 128 + 128].astype(f32).reshape(rows, 128)
            fine.append(dot(inner, do0[...]) + child + context)
        fine = jnp.concatenate(fine, axis=-1)
        width = fine.shape[-1]
        mean = dot((fine * fine).astype(bf16), averager[:width, :width])
        normed = (fine * lax.rsqrt(mean + norm_eps)).astype(bf16).reshape(12, samples, width)
        for k, a in enumerate(halves):
            part16 = normed[..., k * 128 : k * 128 + 128]
            n0[i - (1 - a), :, :, a * 128 : a * 128 + 128] = jnp.where(
                low11, part16[1:12], part16[0:11]
            )

    for t in range(15):
        if t < 8:
            context_row(t)
        if 0 <= t - 1 < 8:
            part_row(t - 1)
        if 0 <= t - 2 < 8:
            fine_row(t - 2)
        if 0 <= t - 5 < 6:
            conv_block(n0, r1, wq.at[0], (t - 5, t - 4), (0, 10), False)
        if 0 <= t - 7 < 5:
            conv_block(r1, r2, wq.at[1], (t - 7, t - 6), (0, 9), True)
        if 0 <= t - 9 < 4:
            conv_block(r2, r3, wq.at[2], (t - 9, t - 8), (0, 8), False)
    stacked = jnp.concatenate(
        [r3[:, quad].reshape(4 * samples, 256) for quad in range(8)], axis=-1
    )
    cell_logits = dot(stacked, wh[...]).reshape(4, samples, 128)
    coarse = cell_logits.astype(bf16)
    rest = (cell_logits - coarse.astype(f32)).astype(bf16)
    places = lax.broadcasted_iota(jnp.int32, (128, 64), 0)
    for i in range(8):
        chosen = (places == slots[i : i + 1, :] + 64 * (i % 2)).astype(bf16)
        out[:, i, :] = dot(coarse[i // 2], chosen) + dot(rest[i // 2], chosen)


def swap(value, partner):
    pairs = []
    for r in range(n_row):
        for c in range(n_col):
            pr, pc = partner(r, c)
            pairs.append((r * n_col + c, pr * n_col + pc))
    return lax.ppermute(value, ("row", "col"), pairs)


def pair_after(i, count):
    return i ^ 1


def pair_before(i, count):
    return (((i - 1) % count ^ 1) + 1) % count


def on_device(
    readouts, w_embed, w_up, merge_in, merge_out, down_in, down_out, w_down, w_head, qubit_slot
):
    row = lax.axis_index("row")
    col = lax.axis_index("col")
    place = jnp.stack([row, col]).astype(jnp.int32)
    col_even = col % 2 == 0

    row_a = swap(readouts, lambda r, c: (pair_after(r, n_row), c))
    row_b = swap(readouts, lambda r, c: (pair_before(r, n_row), c))
    own, wq_up, we, mi, mo, wq_down, di, dc, dp, do0, do, wh, w2, w7 = whole_call(
        prep_body,
        (
            arr((8, 16, 256)),
            arr((3, 1024, 256)),
            arr((512, 256)),
            arr((256, 256)),
            arr((256, 128)),
            arr((3, 1024, 256)),
            arr((128, 256)),
            arr((128, 512)),
            arr((128, 256)),
            arr((512, 128)),
            arr((256, 128)),
            arr((2048, 128)),
            arr((384, 256)),
            arr((256, 256)),
        ),
        [
            pltpu.VMEM((3, 9, 64, 64), bf16),
            pltpu.VMEM((8, 64), bf16),
            pltpu.VMEM((64, 256), bf16),
            pltpu.VMEM((3, 9, 64, 64), bf16),
            pltpu.VMEM((64, 256), bf16),
            pltpu.VMEM((4, 64), bf16),
            pltpu.SemaphoreType.DMA((9,)),
        ],
        (
            readouts,
            w_up,
            w_embed,
            merge_in,
            merge_out.T,
            w_down,
            down_in,
            down_out.T,
            w_head.T,
        ),
        outside=tuple(range(9)),
    )
    tiles = jnp.stack([own, row_b, row_a])
    left = tiles[:, :, 0:8]
    right = tiles[:, :, 8:16]
    col_a = swap(jnp.where(col_even, right, left), lambda r, c: (r, pair_after(c, n_col)))
    col_b = swap(jnp.where(col_even, left, right), lambda r, c: (r, pair_before(c, n_col)))
    quads = lambda rows, cols: pltpu.VMEM((rows, cols, samples, 256), bf16)
    ext = pltpu.VMEM((24, 4, 8, 256), f32)
    i0, i1, i2, i3, il1 = whole_call(
        up_inner_body,
        (
            arr((7, 7, samples, 256)),
            arr((6, 6, samples, 256)),
            arr((5, 5, samples, 256)),
            arr((4, 4, samples, 256)),
            arr((4, 4, samples, 128)),
        ),
        [ext],
        (place, tiles, wq_up, we, mi, mo),
        smem=(0,),
    )
    i0, col_b, col_a = lax.optimization_barrier((i0, col_b, col_a))
    s0, s1, s2, s3, own1, l3, cells = whole_call(
        up_own_body,
        (
            arr((2, 7, 3, samples, 256)),
            arr((2, 6, 3, samples, 256)),
            arr((2, 5, 3, samples, 256)),
            arr((2, 4, 2, samples, 256)),
            arr((4, 8, samples, 128)),
            arr((samples, 128)),
            arr((24, 4, 8, 256), f32),
        ),
        [],
        (place, tiles, col_b, col_a, wq_up, we, mi, mo, i0, i1, i2, il1),
        smem=(0,),
    )

    pair = jnp.stack([l3, swap(l3, lambda r, c: (r, c ^ 1))])
    f0 = whole_call(
        up_ring_embed_body,
        arr((11, 15, samples, 256)),
        [],
        (cells, we, i0, s0),
    )
    pair, f0 = lax.optimization_barrier((pair, f0))
    four = jnp.stack([pair] + [swap(pair, lambda r, c, m=m: (r ^ m, c)) for m in high_masks[1:]])
    f1 = whole_call(
        up_ring_first_body, arr((10, 14, samples, 256)), [], (f0, wq_up, i1, s1)
    )
    four, f1 = lax.optimization_barrier((four, f1))
    strips = [four] + [swap(four, lambda r, c, m=m: (r ^ (4 * m), c)) for m in deep_masks[1:]]
    f3 = whole_call(
        up_ring_second_body,
        arr((8, 12, samples, 256)),
        [quads(9, 13)],
        (f1, wq_up, i2, s2, i3, s3),
    )
    strips[3], f3 = lax.optimization_barrier((strips[3], f3))
    a3, a4, p5, send1, send3 = whole_call(
        mid_body,
        (
            arr((3, 2, samples, 128)),
            arr((3, 2, samples, 128)),
            arr((2, samples, 128)),
            arr((5, samples, 128)),
            arr((5, samples, 128)),
        ),
        [pltpu.VMEM((4, 4, 2, samples, 128), bf16), pltpu.VMEM((8, 2, samples, 128), bf16)],
        (place, *strips, mi, mo),
        smem=(0,),
    )
    q1 = swap(send1, lambda r, c: (r, c ^ 2))
    q2 = swap(p5, lambda r, c: (r, c ^ 4))
    q3 = swap(send3, lambda r, c: (r, c ^ 6))
    l1, l2, child0, child1 = whole_call(
        up_ring_merge_body,
        (
            arr((8, 12, samples, 128)),
            arr((4, 6, samples, 128)),
            arr((7, 2, 12 * samples, 512)),
            arr((8, 12 * samples, 256)),
        ),
        [],
        (f3, mi, mo, own1, dc),
    )
    slots = qubit_slot.reshape(qubit_slot.shape[0], qubit_slot.shape[2])
    return whole_call(
        descent_body,
        arr((samples, 8, 64), f32),
        [
            pltpu.VMEM((4, 4, samples, 128), bf16),
            pltpu.VMEM((2, 2, samples, 128), f32),
            pltpu.VMEM((2, 2, samples, 256), f32),
            pltpu.VMEM((4, 6, samples, 128), f32),
            pltpu.VMEM((4, 6, samples, 256), bf16),
            pltpu.VMEM((8, 12 * samples, 128), bf16),
            pltpu.VMEM((8, 12 * samples, 256), f32),
            quads(7, 11),
            quads(6, 10),
            quads(5, 9),
            quads(4, 8),
        ],
        (
            place,
            slots,
            a3,
            a4,
            p5,
            q1,
            q2,
            q3,
            f3,
            l1,
            l2,
            mi,
            mo,
            do,
            dc,
            dp,
            w2,
            w7,
            do0,
            child0,
            child1,
            wq_down,
            wh,
        ),
        smem=(0,),
    )


def solution(mesh):
    placed = (P("row", "col", None), P(), P(), P(), P(), P(), P(), P(), P(), P("row", "col", None))
    return jax.shard_map(
        on_device, mesh=mesh, in_specs=placed, out_specs=P(None, "row", "col"), check_vma=False
    )
```

```python
import functools

import jax
import jax.numpy as jnp
from jax import lax
from jax.experimental import pallas as pl
from jax.experimental.pallas import tpu as pltpu
from jax.sharding import PartitionSpec as P

norm_eps = 1e-05
bf16 = jnp.bfloat16
f32 = jnp.float32
n_row = 16
n_col = 8
samples = 32
vmem_bytes = 20 * 1024 * 1024
high_masks = (0, 2, 3, 1)
deep_masks = (0, 3, 1, 2)


def dot(left, right):
    return jnp.dot(left, right, preferred_element_type=f32)


def relu16(wide):
    return jnp.maximum(wide.astype(bf16), 0)


def low_half(shape):
    return lax.broadcasted_iota(jnp.int32, shape, len(shape) - 1) < 64


def whole_call(body, out_shapes, scratch, args, smem=(), outside=()):
    args = [
        pltpu.with_memory_space_constraint(x, pltpu.HBM) if i in outside else x
        for i, x in enumerate(args)
    ]
    specs = [
        pl.BlockSpec(
            memory_space=pltpu.SMEM if i in smem else pltpu.HBM if i in outside else pltpu.VMEM
        )
        for i in range(len(args))
    ]
    return pl.pallas_call(
        body,
        out_shape=out_shapes,
        in_specs=specs,
        out_specs=jax.tree.map(lambda _: pl.BlockSpec(memory_space=pltpu.VMEM), out_shapes),
        scratch_shapes=scratch,
        compiler_params=pltpu.CompilerParams(vmem_limit_bytes=vmem_bytes),
    )(*args)


def arr(shape, dtype=bf16):
    return jax.ShapeDtypeStruct(shape, dtype)


def fill_quad_weights(src, out, layer, from_odd):
    zero = jnp.zeros((64, 64), bf16)

    def tap_of(step, parity_in, parity_out):
        place_in = 1 - parity_in if from_odd else parity_in
        place_out = parity_out if from_odd else 1 - parity_out
        tap = 2 * step + place_in - place_out
        return tap if 0 <= tap <= 2 else None

    for di in range(2):
        for dj in range(2):
            for a in range(2):
                for b in range(2):
                    base = ((di * 2 + dj) * 4 + a * 2 + b) * 64
                    for oa in range(2):
                        tap_row = tap_of(di, a, oa)
                        blocks = []
                        for ob in range(2):
                            tap_col = tap_of(dj, b, ob)
                            if tap_row is None or tap_col is None:
                                blocks.append(zero)
                            else:
                                blocks.append(src[layer, 3 * tap_row + tap_col])
                        out[layer, base : base + 64, oa * 128 : oa * 128 + 128] = jnp.concatenate(
                            blocks, axis=1
                        )


def dot_rows(left, right):
    return lax.dot_general(left, right, (((0,), (0,)), ((), ())), preferred_element_type=f32)


def lane_copies(first, second):
    row = lax.broadcasted_iota(jnp.int32, (64, 128), 0)
    lane = lax.broadcasted_iota(jnp.int32, (64, 128), 1)
    kept = jnp.where(lane < 64, first, second) > 0
    return jnp.where(kept & (row == lane % 64), 1.0, 0.0).astype(bf16)


def copies_in(sems, *pairs):
    copies = [pltpu.make_async_copy(src, dst, sems.at[i]) for i, (src, dst) in enumerate(pairs)]
    for copy in copies:
        copy.start()
    return copies


def prep_body(
    own,
    w_up,
    w_embed,
    merge_in,
    merge_out_t,
    w_down,
    down_in,
    down_out_t,
    w_head_t,
    own_out,
    wq,
    we,
    mi,
    mo,
    wq_down,
    di,
    dc,
    dp,
    do0,
    do,
    wh,
    w2,
    w7,
    w_up_s,
    w_embed_s,
    mo_s,
    w_down_s,
    do_s,
    head_s,
    sems,
):
    copies = copies_in(
        sems,
        (w_up, w_up_s),
        (w_embed, w_embed_s),
        (merge_out_t, mo_s),
        (own, own_out),
        (merge_in, mi),
        (w_down, w_down_s),
        (down_in, di),
        (down_out_t, do_s),
        (w_head_t, head_s),
    )
    copies[0].wait()
    for layer in range(3):
        fill_quad_weights(w_up_s, wq, layer, layer % 2 == 0)
    copies[1].wait()
    tiled = jnp.concatenate([w_embed_s[...].astype(f32)] * 16, axis=0)
    none = jnp.zeros((128, 64), f32)
    for a in range(2):
        for b in range(2):
            q = 2 * a + b
            pair = [tiled, none] if b == 0 else [none, tiled]
            we[q * 128 : q * 128 + 128, a * 128 : a * 128 + 128] = jnp.concatenate(
                pair, axis=1
            ).astype(bf16)
            we[q * 128 : q * 128 + 128, (1 - a) * 128 : (1 - a) * 128 + 128] = jnp.zeros(
                (128, 128), bf16
            )
    copies[2].wait()
    mo[...] = dot_rows(mo_s[...], lane_copies(1, 1)).astype(bf16)
    copies[3].wait()
    copies[4].wait()
    copies[5].wait()
    for layer in range(3):
        fill_quad_weights(w_down_s, wq_down, layer, layer % 2 == 0)
    copies[6].wait()
    zero = jnp.zeros((64, 256), bf16)
    child = di[64:128, :]
    dc[0:64, 0:256] = child
    dc[0:64, 256:512] = zero
    dc[64:128, 0:256] = zero
    dc[64:128, 256:512] = child
    dp[0:64, :] = di[0:64, :]
    dp[64:128, :] = zero
    copies[7].wait()
    back = do_s[...]
    do0[0:256, :] = dot_rows(back, lane_copies(1, 0)).astype(bf16)
    do0[256:512, :] = dot_rows(back, lane_copies(0, 1)).astype(bf16)
    do[...] = dot_rows(back, lane_copies(1, 1)).astype(bf16)
    w2[0:128, :] = dp[...]
    w2[128:384, :] = dot(do[...], dp[...]).astype(bf16)
    w7[...] = dot(mo[...], dp[...]).astype(bf16)
    copies[8].wait()
    output = lax.broadcasted_iota(jnp.int32, (4, 128), 0)
    lane = lax.broadcasted_iota(jnp.int32, (4, 128), 1)
    head = dot_rows(head_s[...], jnp.where(lane % 4 == output, 1.0, 0.0).astype(bf16))
    lane = lax.broadcasted_iota(jnp.int32, (64, 128), 1)
    for quad in range(8):
        for a in range(2):
            for b in range(2):
                base = quad * 256 + (a * 2 + b) * 64
                first = a * 64 + 4 * (2 * quad + b)
                kept = jnp.where((lane >= first) & (lane < first + 4), head, 0.0)
                wh[base : base + 64, :] = kept.astype(bf16)


def row_chunks(first, last, cols):
    step = max(1, 14 // cols)
    return [(i, min(i + step, last)) for i in range(first, last, step)]


def conv_block(src, dst, weights, row_range, col_range, to_odd, src_at=(0, 0), dst_at=(0, 0)):
    c0, c1 = col_range
    cols = c1 - c0
    for r0, r1 in row_chunks(*row_range, cols):
        rows = r1 - r0
        i, j = r0 - src_at[0], c0 - src_at[1]
        here = src[i : i + rows, j : j + cols]
        right = src[i : i + rows, j + 1 : j + 1 + cols]
        below = src[i + 1 : i + 1 + rows, j : j + cols]
        corner = src[i + 1 : i + 1 + rows, j + 1 : j + 1 + cols]
        stacked = jnp.concatenate([here, right, below, corner], axis=-1)
        update = dot(stacked.reshape(rows * cols * samples, 1024), weights[...])
        update = jnp.maximum(update, 0.0).reshape(rows, cols, samples, 256)
        low = low_half((rows, cols, samples, 128))
        if to_odd:
            old0 = jnp.where(low, corner[..., 0:128], below[..., 0:128])
            old1 = jnp.where(low, right[..., 128:256], here[..., 128:256])
        else:
            old0 = jnp.where(low, here[..., 0:128], right[..., 0:128])
            old1 = jnp.where(low, below[..., 128:256], corner[..., 128:256])
        new0 = (old0.astype(f32) + update[..., 0:128]).astype(bf16)
        new1 = (old1.astype(f32) + update[..., 128:256]).astype(bf16)
        i, j = r0 - dst_at[0], c0 - dst_at[1]
        dst[i : i + rows, j : j + cols, :, 0:128] = new0
        dst[i : i + rows, j : j + cols, :, 128:256] = new1


def spread_tiles(place, tiles, ext):
    row_even = place[0] % 2 == 0
    after_row = jnp.where(row_even, 16, 0)
    before_row = jnp.where(row_even, 0, 16)
    for tile, start in ((0, 8), (1, before_row), (2, after_row)):
        cells = tiles[tile].astype(f32)
        ext[pl.ds(start, 8), 1] = cells[:, 0:8]
        ext[pl.ds(start, 8), 2] = cells[:, 8:16]


def spread_sides(place, col_a, col_b, ext):
    row_even = place[0] % 2 == 0
    col_even = place[1] % 2 == 0
    after_row = jnp.where(row_even, 16, 0)
    before_row = jnp.where(row_even, 0, 16)
    after_col = jnp.where(col_even, 3, 0)
    before_col = jnp.where(col_even, 0, 3)
    for tile, start in ((0, 8), (1, before_row), (2, after_row)):
        ext[pl.ds(start, 8), after_col] = col_a[tile].astype(f32)
        ext[pl.ds(start, 8), before_col] = col_b[tile].astype(f32)


def embed_block(ext, we, dst, row_range, col_range, dst_at=(0, 0)):
    c0, c1 = col_range
    cols = c1 - c0
    sub = lax.broadcasted_iota(jnp.int32, (16, 128), 0)
    lane = lax.broadcasted_iota(jnp.int32, (16, 128), 1)
    own_lanes = (lane // 8 == sub).astype(f32)
    for r0, r1 in row_chunks(*row_range, cols):
        quads = []
        for i in range(r0, r1):
            for quad in range(c0, c1):
                parts = []
                for a in range(2):
                    row = 1 + 2 * i + (1 - a)
                    for b in range(2):
                        col = 1 + 2 * quad + (1 - b)
                        cell = ext[row, col // 8, col % 8 : col % 8 + 1, :]
                        halves = [
                            jnp.broadcast_to(cell[:, k : k + 128], (16, 128)) * own_lanes
                            for k in (0, 128)
                        ]
                        parts.append(jnp.concatenate(halves, axis=0).astype(bf16))
                quads.append(jnp.concatenate(parts, axis=-1))
        embedded = dot(jnp.concatenate(quads, axis=0), we[...]).astype(bf16)
        i, j = r0 - dst_at[0], c0 - dst_at[1]
        dst[i : i + r1 - r0, j : j + cols] = embedded.reshape(r1 - r0, cols, samples, 256)


def merge_block(src, dst, merge_in, mo, row_range, col_range):
    c0, c1 = col_range
    cols = c1 - c0
    for r0, r1 in row_chunks(*row_range, cols):
        stacked = src[r0:r1, c0:c1].reshape((r1 - r0) * cols * samples, 256)
        hidden = relu16(dot(stacked, merge_in[...]))
        merged = dot(hidden, mo[...]).astype(bf16)
        dst[r0:r1, c0:c1] = merged.reshape(r1 - r0, cols, samples, 128)


def blocks_ring(rows, cols):
    return [
        ((0, 2), (0, cols)),
        ((2, rows - 2), (0, 2)),
        ((2, rows - 2), (cols - 2, cols)),
        ((rows - 2, rows), (0, cols)),
    ]


def copy_rim(dst, inner, sides, rows, cols):
    for place, row in ((2, 0), (rows - 3, rows - 5)):
        dst[place, 2:4] = sides[0, row, 0:2]
        dst[place, 4 : cols - 4] = inner[row]
        dst[place, cols - 4 : cols - 2] = sides[1, row, 1:3]
    dst[3 : rows - 3, 2] = sides[0, 1 : rows - 5, 0]
    dst[3 : rows - 3, cols - 3] = sides[1, 1 : rows - 5, 2]


def merge_pair(top, bottom, merge_in, mo):
    count = top.shape[0]
    stacked = jnp.concatenate([top, bottom], axis=-1).reshape(count * samples, 256)
    hidden = relu16(dot(stacked, merge_in))
    return dot(hidden, mo).astype(bf16).reshape(count, samples, 128)


def paired_columns(cells):
    count = cells.shape[0] // 2
    split = cells.reshape(count, 2, samples, 128)
    low = low_half((count, samples, 128))
    return jnp.where(low, split[:, 0], split[:, 1])


def up_inner_body(place, tiles, wq, we, merge_in, mo, f0, f1, f2, f3, l1, ext):
    at = (2, 4)
    spread_tiles(place, tiles, ext)
    embed_block(ext, we, f0, (2, 9), (4, 11), at)
    conv_block(f0, f1, wq.at[0], (2, 8), (4, 10), False, at, at)
    conv_block(f1, f2, wq.at[1], (2, 7), (4, 9), True, at, at)
    conv_block(f2, f3, wq.at[2], (2, 6), (4, 8), False, at, at)
    merge_block(f3, l1, merge_in, mo, (0, 4), (0, 4))


def up_own_body(
    place,
    tiles,
    col_b,
    col_a,
    wq,
    we,
    merge_in,
    mo,
    i0,
    i1,
    i2,
    il1,
    s0,
    s1,
    s2,
    s3,
    l1,
    out,
    ext,
):
    spread_tiles(place, tiles, ext)
    spread_sides(place, col_a, col_b, ext)
    for ref, inner, rows, cols in ((s0, i0, 7, 7), (s1, i1, 6, 6), (s2, i2, 5, 5)):
        ref[0, :, 2] = inner[:, 0]
        ref[1, :, 0] = inner[:, cols - 1]
    left = (2, 4)
    for k, cols in ((0, left), (1, (11, 13))):
        embed_block(ext, we, s0.at[k], (2, 9), cols, (2, 2 if k == 0 else 10))
    for k, cols in ((0, left), (1, (10, 12))):
        src_at = (2, 2 if k == 0 else 10)
        dst_at = (2, 2 if k == 0 else 9)
        conv_block(s0.at[k], s1.at[k], wq.at[0], (2, 8), cols, False, src_at, dst_at)
    for k, cols in ((0, left), (1, (9, 11))):
        src_at = (2, 2 if k == 0 else 9)
        dst_at = (2, 2 if k == 0 else 8)
        conv_block(s1.at[k], s2.at[k], wq.at[1], (2, 7), cols, True, src_at, dst_at)
    for k, cols in ((0, left), (1, (8, 10))):
        src_at = (2, 2 if k == 0 else 8)
        conv_block(s2.at[k], s3.at[k], wq.at[2], (2, 6), cols, False, src_at, (2, cols[0]))
    merged = merge_pair(
        s3[..., 0:128].reshape(16, samples, 128),
        s3[..., 128:256].reshape(16, samples, 128),
        merge_in[...],
        mo[...],
    ).reshape(2, 4, 2, samples, 128)
    cells = jnp.concatenate([merged[0], il1[...], merged[1]], axis=1)
    l1[...] = cells
    top = jnp.concatenate([paired_columns(cells[0]), paired_columns(cells[2])], axis=0)
    bottom = jnp.concatenate([paired_columns(cells[1]), paired_columns(cells[3])], axis=0)
    l2 = merge_pair(top, bottom, merge_in[...], mo[...])
    l3 = merge_pair(paired_columns(l2[0:4]), paired_columns(l2[4:8]), merge_in[...], mo[...])
    out[...] = paired_columns(l3)[0]


def up_ring_embed_body(ext, we, i0, s0, f0):
    copy_rim(f0, i0, s0, 11, 15)
    for block in blocks_ring(11, 15):
        embed_block(ext, we, f0, *block)


def up_ring_first_body(f0, wq, i1, s1, f1):
    for block in blocks_ring(10, 14):
        conv_block(f0, f1, wq.at[0], *block, False)
    copy_rim(f1, i1, s1, 10, 14)


def up_ring_second_body(f1, wq, i2, s2, i3, s3, f3, f2):
    copy_rim(f2, i2, s2, 9, 13)
    for block in blocks_ring(9, 13):
        conv_block(f1, f2, wq.at[1], *block, True)
    for block in blocks_ring(8, 12):
        conv_block(f2, f3, wq.at[2], *block, False)
    f3[2:6, 4:8] = i3[...]
    f3[2:6, 2:4] = s3[0]
    f3[2:6, 8:10] = s3[1]


def up_ring_merge_body(f3, merge_in, mo, own1, dc, l1, l2, child0, child1):
    for block in blocks_ring(8, 12):
        merge_block(f3, l1, merge_in, mo, *block)
    l1[2:6, 2:10] = own1[...]
    for i in (0, 2):
        top = jnp.concatenate([paired_columns(l1[2 * i]), paired_columns(l1[2 * i + 2])], axis=0)
        bottom = jnp.concatenate(
            [paired_columns(l1[2 * i + 1]), paired_columns(l1[2 * i + 3])], axis=0
        )
        l2[i : i + 2] = merge_pair(top, bottom, merge_in[...], mo[...]).reshape(2, 6, samples, 128)
    for i in range(8):
        for a in range(2):
            if 0 <= i - (1 - a) < 7:
                cells = f3[i, :, :, a * 128 : a * 128 + 128].reshape(12 * samples, 128)
                child0[i - (1 - a), a] = dot(cells, dc[...]).astype(bf16)
        child1[i] = dot(l1[i].reshape(12 * samples, 128), dc[:, 0:256]).astype(bf16)


def mid_body(place, z0, z1, z2, z3, merge_in, mo, a3, a4, p5, send1, send3, strip, l4s):
    row = place[0]
    col = place[1]
    deep = row // 4
    high = row % 4
    wide = col // 2
    core = col % 2
    for m, ref in zip(deep_masks, (z0, z1, z2, z3)):
        for n, mask in enumerate(high_masks):
            for k in range(2):
                strip[deep ^ m, high ^ mask, core ^ k] = ref[n, k]
    cells = strip[...].reshape(8, 2, 2, samples, 128)
    l4 = merge_pair(
        cells[:, 0].reshape(16, samples, 128),
        cells[:, 1].reshape(16, samples, 128),
        merge_in[...],
        mo[...],
    )
    l4s[...] = l4.reshape(8, 2, samples, 128)
    pairs = paired_columns(l4).reshape(4, 2, samples, 128)
    l5 = merge_pair(pairs[:, 0], pairs[:, 1], merge_in[...], mo[...])
    packed = paired_columns(l5)
    p5[...] = packed
    low = low_half((samples, 128))
    wide_even = wide % 2 == 0
    for d in range(3):
        line = (row + d + (n_row - 1)) % n_row
        left = strip[line // 4, line % 4, 0]
        right = strip[line // 4, line % 4, 1]
        a3[d, 0] = left
        a3[d, 1] = right
        left4 = l4s[line // 2, 0]
        right4 = l4s[line // 2, 1]
        a4[d, 0] = left4
        a4[d, 1] = right4
        to_right = jnp.where(low, right4, right)
        to_left = jnp.where(low, left, left4)
        send1[d] = jnp.where(wide_even, to_right, to_left)
        send3[d] = jnp.where(wide_even, to_left, to_right)
    send1[3:5] = packed
    send3[3:5] = packed


def both_lanes(cells):
    wide = cells.astype(f32)
    turned = pltpu.roll(wide, 64, wide.ndim - 1)
    low = low_half(wide.shape)
    return jnp.where(low, wide, turned).astype(bf16), jnp.where(low, turned, wide).astype(bf16)


def descent_body(
    place,
    slots,
    a3,
    a4,
    p5,
    q1,
    q2,
    q3,
    f3,
    l1,
    l2,
    merge_in,
    mo,
    do,
    dc,
    dp,
    w2,
    w7,
    do0,
    child0,
    child1,
    wq,
    wh,
    out,
    l5s,
    c6s,
    g6s,
    c2s,
    p2s,
    c1s,
    p1s,
    n0,
    r1,
    r2,
    r3,
):
    row = place[0]
    col = place[1]
    wide = col // 2
    core = col % 2
    wide_even = wide % 2 == 0
    merge_weights = merge_in[...]
    back_weights = mo[...]
    child_weights = dc[:, 0:256]
    parent_weights = dp[...]
    step_weights = w2[...]
    out_weights = do[...]

    for m, ref, start in ((0, p5, 0), (1, q1, 3), (2, q2, 0), (3, q3, 3)):
        for pair in range(2):
            first, second = both_lanes(ref[start + pair])
            l5s[wide ^ m, 2 * pair] = first
            l5s[wide ^ m, 2 * pair + 1] = second
    grid = l5s[...].reshape(2, 2, 2, 2, samples, 128)
    low4 = low_half((4, samples, 128))
    top = jnp.where(
        low4,
        grid[:, 0, :, 0].reshape(4, samples, 128),
        grid[:, 1, :, 0].reshape(4, samples, 128),
    )
    bottom = jnp.where(
        low4,
        grid[:, 0, :, 1].reshape(4, samples, 128),
        grid[:, 1, :, 1].reshape(4, samples, 128),
    )
    l6 = merge_pair(top, bottom, merge_weights, back_weights)
    low1 = low_half((1, samples, 128))
    stacked7 = jnp.concatenate(
        [jnp.where(low1, l6[0:1], l6[2:3]), jnp.where(low1, l6[1:2], l6[3:4])], axis=-1
    )
    hidden7 = relu16(dot(stacked7.reshape(samples, 256), merge_weights))
    part7 = dot(hidden7, w7[...]).reshape(1, samples, 256)
    c7 = dot(hidden7, back_weights).reshape(1, samples, 128)

    def descend(parent, part, child):
        count = child.shape[0]
        flat = child.reshape(count * samples, 128)
        ahead = dot(flat, child_weights).reshape(count, samples, 256)
        inner = relu16(ahead + part).reshape(count * samples, 256)
        step = dot(jnp.concatenate([flat, inner], axis=-1), step_weights)
        part = part + step.reshape(count, samples, 256)
        outcome = dot(inner, out_weights).reshape(count, samples, 128)
        return outcome + child.astype(f32) + parent, part

    c6, part6 = descend(c7, part7, l6)
    c6s[...] = c6.reshape(2, 2, samples, 128)
    g6s[...] = part6.reshape(2, 2, samples, 256)

    side = jnp.where(core == 0, (wide + 3) % 4, (wide + 1) % 4)
    lines = [(row + d + (n_row - 1)) % n_row for d in range(3)]
    parents5 = []
    parts5 = []
    children5 = []
    for place_x in (wide, side):
        for line in lines:
            deep = line // 4
            parents5.append(c6s[place_x // 2, deep // 2])
            parts5.append(g6s[place_x // 2, deep // 2])
            children5.append(l5s[place_x, deep])
    c5, part5 = descend(jnp.stack(parents5), jnp.stack(parts5), jnp.stack(children5))

    from_first = jnp.logical_xor(wide_even, core == 0)
    side_cells = jnp.where(from_first, q1[0:3], q3[0:3])
    side_low, side_high = both_lanes(side_cells)
    side4 = jnp.where(core == 0, side_low, side_high)
    side3 = jnp.where(core == 0, side_high, side_low)
    own4 = a4[...]
    children4 = jnp.concatenate([own4[:, 0], own4[:, 1], side4, side4], axis=0)
    parents4 = jnp.concatenate([c5[0:3], c5, c5[3:6]], axis=0)
    parts4 = jnp.concatenate([part5[0:3], part5, part5[3:6]], axis=0)
    c4, part4 = descend(parents4, parts4, children4)
    own3_0, own3_1 = both_lanes(a3[:, 0])
    own3_2, own3_3 = both_lanes(a3[:, 1])
    first_core = core == 0

    def window(blocks):
        left = jnp.concatenate(blocks[0:4], axis=0)
        right = jnp.concatenate(blocks[2:6], axis=0)
        return jnp.where(first_core, left, right)

    starts = (6, 0, 0, 3, 3, 6)
    c3, part3 = descend(
        window([c4[k : k + 3] for k in starts]),
        window([part4[k : k + 3] for k in starts]),
        window([side3, own3_0, own3_1, own3_2, own3_3, side3]),
    )
    above = [3 * j + i for i in (0, 1, 1, 2) for j in (0, 1, 1, 2, 2, 3)]
    c2, part2 = descend(
        jnp.stack([c3[k] for k in above]),
        jnp.stack([part3[k] for k in above]),
        l2[...].reshape(24, samples, 128),
    )
    c2s[...] = c2.reshape(4, 6, samples, 128)
    p2s[...] = part2.astype(bf16).reshape(4, 6, samples, 256)

    rows = 12 * samples
    low11 = low_half((11, samples, 128))
    sub = lax.broadcasted_iota(jnp.int32, (256, 256), 0)
    lane = lax.broadcasted_iota(jnp.int32, (256, 256), 1)
    averager = jnp.where(sub // 64 == lane // 64, 1.0 / 64, 0.0).astype(bf16)
    def context_row(i):
        parent = c2s[i // 2][:, None]
        parent = jnp.broadcast_to(parent, (6, 2, samples, 128)).reshape(rows, 128)
        part = jnp.broadcast_to(p2s[i // 2][:, None], (6, 2, samples, 256)).reshape(rows, 256)
        inner = relu16(child1[i] + part)
        c1 = dot(inner, out_weights) + l1[i].astype(f32).reshape(rows, 128) + parent
        c1s[i] = c1.astype(bf16)

    def part_row(i):
        p1s[i] = dot(c1s[i], parent_weights)

    def fine_row(i):
        part = p1s[i]
        part = jnp.concatenate([part, part], axis=-1).astype(bf16)
        context = c1s[i].astype(f32)
        halves = [a for a in range(2) if 0 <= i - (1 - a) < 7]
        fine = []
        for a in halves:
            inner = relu16(child0[i - (1 - a), a] + part)
            child = f3[i, :, :, a * 128 : a * 128 + 128].astype(f32).reshape(rows, 128)
            fine.append(dot(inner, do0[...]) + child + context)
        fine = jnp.concatenate(fine, axis=-1)
        width = fine.shape[-1]
        mean = dot((fine * fine).astype(bf16), averager[:width, :width])
        normed = (fine * lax.rsqrt(mean + norm_eps)).astype(bf16).reshape(12, samples, width)
        for k, a in enumerate(halves):
            part16 = normed[..., k * 128 : k * 128 + 128]
            n0[i - (1 - a), :, :, a * 128 : a * 128 + 128] = jnp.where(
                low11, part16[1:12], part16[0:11]
            )

    for t in range(15):
        if t < 8:
            context_row(t)
        if 0 <= t - 1 < 8:
            part_row(t - 1)
        if 0 <= t - 2 < 8:
            fine_row(t - 2)
        if 0 <= t - 5 < 6:
            conv_block(n0, r1, wq.at[0], (t - 5, t - 4), (0, 10), False)
        if 0 <= t - 7 < 5:
            conv_block(r1, r2, wq.at[1], (t - 7, t - 6), (0, 9), True)
        if 0 <= t - 9 < 4:
            conv_block(r2, r3, wq.at[2], (t - 9, t - 8), (0, 8), False)
    stacked = jnp.concatenate(
        [r3[:, quad].reshape(4 * samples, 256) for quad in range(8)], axis=-1
    )
    cell_logits = dot(stacked, wh[...]).reshape(4, samples, 128)
    coarse = cell_logits.astype(bf16)
    rest = (cell_logits - coarse.astype(f32)).astype(bf16)
    both = jnp.concatenate([coarse, rest], axis=-1)
    places = lax.broadcasted_iota(jnp.int32, (256, 128), 0) % 128
    for i in range(4):
        wanted = jnp.concatenate([slots[2 * i : 2 * i + 1], slots[2 * i + 1 : 2 * i + 2] + 64], axis=1)
        chosen = jnp.where(places == wanted, 1.0, 0.0).astype(bf16)
        picked = dot(both[i], chosen)
        out[:, 2 * i, :] = picked[:, 0:64]
        out[:, 2 * i + 1, :] = picked[:, 64:128]


def swap(value, partner):
    pairs = []
    for r in range(n_row):
        for c in range(n_col):
            pr, pc = partner(r, c)
            pairs.append((r * n_col + c, pr * n_col + pc))
    return lax.ppermute(value, ("row", "col"), pairs)


def pair_after(i, count):
    return i ^ 1


def pair_before(i, count):
    return (((i - 1) % count ^ 1) + 1) % count


def on_device(
    readouts, w_embed, w_up, merge_in, merge_out, down_in, down_out, w_down, w_head, qubit_slot
):
    row = lax.axis_index("row")
    col = lax.axis_index("col")
    place = jnp.stack([row, col]).astype(jnp.int32)
    col_even = col % 2 == 0

    row_a = swap(readouts, lambda r, c: (pair_after(r, n_row), c))
    row_b = swap(readouts, lambda r, c: (pair_before(r, n_row), c))
    own, wq_up, we, mi, mo, wq_down, di, dc, dp, do0, do, wh, w2, w7 = whole_call(
        prep_body,
        (
            arr((8, 16, 256)),
            arr((3, 1024, 256)),
            arr((512, 256)),
            arr((256, 256)),
            arr((256, 128)),
            arr((3, 1024, 256)),
            arr((128, 256)),
            arr((128, 512)),
            arr((128, 256)),
            arr((512, 128)),
            arr((256, 128)),
            arr((2048, 128)),
            arr((384, 256)),
            arr((256, 256)),
        ),
        [
            pltpu.VMEM((3, 9, 64, 64), bf16),
            pltpu.VMEM((8, 64), bf16),
            pltpu.VMEM((64, 256), bf16),
            pltpu.VMEM((3, 9, 64, 64), bf16),
            pltpu.VMEM((64, 256), bf16),
            pltpu.VMEM((4, 64), bf16),
            pltpu.SemaphoreType.DMA((9,)),
        ],
        (
            readouts,
            w_up,
            w_embed,
            merge_in,
            merge_out.T,
            w_down,
            down_in,
            down_out.T,
            w_head.T,
        ),
        outside=tuple(range(9)),
    )
    tiles = jnp.stack([own, row_b, row_a])
    left = tiles[:, :, 0:8]
    right = tiles[:, :, 8:16]
    col_a = swap(jnp.where(col_even, right, left), lambda r, c: (r, pair_after(c, n_col)))
    col_b = swap(jnp.where(col_even, left, right), lambda r, c: (r, pair_before(c, n_col)))
    quads = lambda rows, cols: pltpu.VMEM((rows, cols, samples, 256), bf16)
    ext = pltpu.VMEM((24, 4, 8, 256), f32)
    i0, i1, i2, i3, il1 = whole_call(
        up_inner_body,
        (
            arr((7, 7, samples, 256)),
            arr((6, 6, samples, 256)),
            arr((5, 5, samples, 256)),
            arr((4, 4, samples, 256)),
            arr((4, 4, samples, 128)),
        ),
        [ext],
        (place, tiles, wq_up, we, mi, mo),
        smem=(0,),
    )
    i0, col_b, col_a = lax.optimization_barrier((i0, col_b, col_a))
    s0, s1, s2, s3, own1, l3, cells = whole_call(
        up_own_body,
        (
            arr((2, 7, 3, samples, 256)),
            arr((2, 6, 3, samples, 256)),
            arr((2, 5, 3, samples, 256)),
            arr((2, 4, 2, samples, 256)),
            arr((4, 8, samples, 128)),
            arr((samples, 128)),
            arr((24, 4, 8, 256), f32),
        ),
        [],
        (place, tiles, col_b, col_a, wq_up, we, mi, mo, i0, i1, i2, il1),
        smem=(0,),
    )

    pair = jnp.stack([l3, swap(l3, lambda r, c: (r, c ^ 1))])
    f0 = whole_call(
        up_ring_embed_body,
        arr((11, 15, samples, 256)),
        [],
        (cells, we, i0, s0),
    )
    pair, f0 = lax.optimization_barrier((pair, f0))
    four = jnp.stack([pair] + [swap(pair, lambda r, c, m=m: (r ^ m, c)) for m in high_masks[1:]])
    f1 = whole_call(
        up_ring_first_body, arr((10, 14, samples, 256)), [], (f0, wq_up, i1, s1)
    )
    four, f1 = lax.optimization_barrier((four, f1))
    strips = [four] + [swap(four, lambda r, c, m=m: (r ^ (4 * m), c)) for m in deep_masks[1:]]
    f3 = whole_call(
        up_ring_second_body,
        arr((8, 12, samples, 256)),
        [quads(9, 13)],
        (f1, wq_up, i2, s2, i3, s3),
    )
    strips[3], f3 = lax.optimization_barrier((strips[3], f3))
    a3, a4, p5, send1, send3 = whole_call(
        mid_body,
        (
            arr((3, 2, samples, 128)),
            arr((3, 2, samples, 128)),
            arr((2, samples, 128)),
            arr((5, samples, 128)),
            arr((5, samples, 128)),
        ),
        [pltpu.VMEM((4, 4, 2, samples, 128), bf16), pltpu.VMEM((8, 2, samples, 128), bf16)],
        (place, *strips, mi, mo),
        smem=(0,),
    )
    q1 = swap(send1, lambda r, c: (r, c ^ 2))
    q2 = swap(p5, lambda r, c: (r, c ^ 4))
    q3 = swap(send3, lambda r, c: (r, c ^ 6))
    l1, l2, child0, child1 = whole_call(
        up_ring_merge_body,
        (
            arr((8, 12, samples, 128)),
            arr((4, 6, samples, 128)),
            arr((7, 2, 12 * samples, 512)),
            arr((8, 12 * samples, 256)),
        ),
        [],
        (f3, mi, mo, own1, dc),
    )
    slots = qubit_slot.reshape(qubit_slot.shape[0], qubit_slot.shape[2])
    return whole_call(
        descent_body,
        arr((samples, 8, 64), f32),
        [
            pltpu.VMEM((4, 4, samples, 128), bf16),
            pltpu.VMEM((2, 2, samples, 128), f32),
            pltpu.VMEM((2, 2, samples, 256), f32),
            pltpu.VMEM((4, 6, samples, 128), f32),
            pltpu.VMEM((4, 6, samples, 256), bf16),
            pltpu.VMEM((8, 12 * samples, 128), bf16),
            pltpu.VMEM((8, 12 * samples, 256), f32),
            quads(7, 11),
            quads(6, 10),
            quads(5, 9),
            quads(4, 8),
        ],
        (
            place,
            slots,
            a3,
            a4,
            p5,
            q1,
            q2,
            q3,
            f3,
            l1,
            l2,
            mi,
            mo,
            do,
            dc,
            dp,
            w2,
            w7,
            do0,
            child0,
            child1,
            wq_down,
            wh,
        ),
        smem=(0,),
    )


def solution(mesh):
    placed = (P("row", "col", None), P(), P(), P(), P(), P(), P(), P(), P(), P("row", "col", None))
    return jax.shard_map(
        on_device, mesh=mesh, in_specs=placed, out_specs=P(None, "row", "col"), check_vma=False
    )
```
